256 devices in a mesh: ctx: 32 (over z_hi, y, x), exp: 8 (over z_lo, core).
Axes of the slice: x: 4, y: 4, z: 8 (z_hi: 2, z_lo: 4; z = z_hi * 4 + z_lo), core: 2. Of those that a mesh axis runs over, the one named last changes fastest.
Arguments:
- queries: bfloat16 [4096, 5120], P('ctx', 'exp'), may hold values from -4.6 to 4.6
- keys: bfloat16 [4096, 1024], P('ctx', 'exp'), may hold values from -4.6 to 4.6
- values: bfloat16 [4096, 1024], P('ctx', 'exp'), may hold values from -6 to 6
- block_order: int32 [64], replicated, may hold values from 0 to 63, each once
- routes: int32 [4096, 1], P('ctx'), may hold values from 0 to 7; in each aligned block of 128 rows (0 to 127, 128 to 255, ...) at most 32 rows name the same one
- norm_gain: float32 [5120], replicated, may hold values from 0.1 to 1.9
- router: float32 [5120, 8], replicated, may hold values from -0.078125 to 0.078125
- w_gate: bfloat16 [8, 5120, 8192], P('exp', None, 'ctx'), may hold values from -0.078125 to 0.078125
- w_up: bfloat16 [8, 5120, 8192], P('exp', None, 'ctx'), may hold values from -0.078125 to 0.078125
- w_down: bfloat16 [8, 8192, 5120], P('exp', 'ctx'), may hold values from -0.0625 to 0.0625
Outputs:
- attended: bfloat16 [4096, 5120], P('ctx', 'exp')
- routed: bfloat16 [4096, 5120], P('ctx', 'exp')
The draws below stay inside these ranges and needn't reach their ends.
Inputs may be any that keep to these rules, and one draw needn't show every extreme that they name: `routes`: in the rows of one index of ctx (aligned blocks of 128 rows) no expert is named more than 32 times. `block_order`: A permutation of 0 to 63.
All inputs are finite; a program needn't handle non-finite values.
Results may differ from the reference program's by a relative error of at most 0.03.
Values may be sent and summed in bfloat16 or wider, within the bound.
A program may use at most 128 MiB of HBM per device.

```python
import math
import jax
import jax.numpy as jnp
import numpy as np
from jax import lax

HEADS = 40
KV_HEADS = 8
HEAD_DIM = 128
EXPERTS = 8
FF = 8192
S_DEV = 128
D = 5120
CAP = 32
SEQ = 4096
N_CTX = 32


def draw_queries(key, part):
    key = jax.random.fold_in(key, 11)
    base = jnp.clip(jax.random.normal(key, (SEQ, HEADS * HEAD_DIM), jnp.float32), -4.5, 4.5)
    return base.astype(jnp.bfloat16)


def draw_keys(key, part):
    key = jax.random.fold_in(key, 12)
    base = jnp.clip(jax.random.normal(key, (SEQ, KV_HEADS * HEAD_DIM), jnp.float32), -4.5, 4.5)
    return base.astype(jnp.bfloat16)


def steps_of(rng, shape, cuts, smallest, high):
    def one(dim, parts):
        heights = jax.random.uniform(jax.random.fold_in(jax.random.fold_in(rng, 6), dim), (parts,), jnp.float32, smallest / len(cuts), high / len(cuts))
        return jnp.repeat(jnp.exp(heights), shape[dim] // parts).reshape((-1,) + (1,) * (len(shape) - dim - 1))

    loudness = one(*cuts[0])
    for cut in cuts[1:]:
        loudness = loudness * one(*cut)
    return loudness


def assign_block(own_key, own, number, rows, amount, top, limit, slope):
    ranking = jax.random.permutation(own_key, amount)
    heavy_load, ordinary = load_shares(amount, rows * top, limit, slope, True), load_shares(amount, rows * top, limit, slope, False)
    places = jnp.arange(amount)

    def named(lengths, turn):
        used = int((lengths > 0).sum())
        fixed = max(1, used // 4)
        passed = fixed + (places - fixed + turn * (used - fixed)) % max(1, amount - fixed)
        return jnp.zeros((amount,), jnp.int32).at[ranking[jnp.where(places < fixed, places, passed)]].set(jnp.asarray(lengths, jnp.int32))

    lengths = jnp.where(number % 4 == 0, named(heavy_load, number // 4), named(ordinary, number - number // 4 - 1))
    mixed = jax.random.permutation(jax.random.fold_in(own, 3), amount)
    source_of, receiver = mixed[0:amount // 2 * 2:2], mixed[1:amount // 2 * 2:2]
    room = jnp.minimum(lengths[source_of] - 1, limit - lengths[receiver]) // 2
    room = jnp.where((source_of == ranking[0]) | (receiver == ranking[0]) | (lengths[receiver] == 0), 0, jnp.maximum(room, 0))
    passed = jax.random.randint(jax.random.fold_in(own, 4), (amount // 2,), 0, 1 << 20) % (room + 1)
    lengths = lengths.at[source_of].add(-passed).at[receiver].add(passed)
    items = jnp.searchsorted(jnp.cumsum(lengths), jnp.arange(rows * top), side="right").astype(jnp.int32)
    grid = items.reshape(top, rows).T
    grid = grid[jax.random.permutation(jax.random.fold_in(own, 1), rows)]
    turn = jax.random.randint(jax.random.fold_in(own, 2), (rows, 1), 0, top)
    return jnp.take_along_axis(grid, (jnp.arange(top)[None, :] + turn) % top, axis=1)


def load_shares(amount, total, reach, lean, full):
    loads = [(1 << 20) // math.isqrt(standing ** lean) + 1 for standing in range(1, amount + 1)]
    largest = reach if full else min(reach, max(-(-total // amount), total * loads[0] // sum(loads)))
    least = 1 if total - largest >= amount - 1 else 0
    given, spare = [largest] + [least] * (amount - 1), total - largest - least * (amount - 1)
    while spare > 0:
        candidates = [i for i in range(1, amount) if given[i] < largest] or [i for i in range(1, amount) if given[i] < reach]
        pool, left = sum([loads[i] for i in candidates]), spare
        for i in candidates:
            more = min(reach - given[i], max(1, left * loads[i] // pool), spare)
            given[i] = given[i] + more
            spare = spare - more
    return np.array(given)


def bell_draw(rng, shape, width, reach, pieces=(), kind=jnp.bfloat16):
    drawn = jax.random.normal(rng, shape, jnp.float32) * width
    if len(pieces) > 0:
        drawn = steps_of(rng, shape, pieces, -0.22, 0.18) * drawn
    return jnp.clip(drawn, min=-reach, max=reach).astype(kind)


def setup_inputs(seed: int = 0) -> dict:
    streams_of = jax.random.split(jax.random.key(seed), 11)
    queries = draw_queries(jax.random.fold_in(streams_of[10], 71), 0)
    keys = draw_keys(jax.random.fold_in(streams_of[10], 71), 0)
    values = bell_draw(streams_of[2], (SEQ, KV_HEADS * HEAD_DIM), 1.0, 6.0, ((0, 32), (1, 8)))
    block_order = jax.random.permutation(streams_of[3], 2 * N_CTX).astype(jnp.int32)
    routes_keys = jax.random.split(jax.random.fold_in(streams_of[4], 1), SEQ // S_DEV)
    routes_turns = jax.random.permutation(jax.random.fold_in(streams_of[4], 3), SEQ // S_DEV)
    routes = jax.vmap(lambda own, number: assign_block(jax.random.fold_in(streams_of[4], 2), own, number, S_DEV, EXPERTS, 1, CAP, 2))(routes_keys, routes_turns).reshape((SEQ, 1))
    norm_gain = jnp.clip(1.0 + 0.18 * jax.random.normal(streams_of[5], (D,), jnp.float32), 0.1, 1.9)
    router = bell_draw(streams_of[6], (D, EXPERTS), D ** -0.5, 0.078125, (), jnp.float32)
    w_gate = bell_draw(streams_of[7], (EXPERTS, D, FF), D ** -0.5, 0.078125, ((0, 8), (2, 32)))
    w_up = bell_draw(streams_of[8], (EXPERTS, D, FF), D ** -0.5, 0.078125, ((0, 8), (2, 32)))
    w_down = bell_draw(streams_of[9], (EXPERTS, FF, D), FF ** -0.5, 0.0625, ((0, 8), (1, 32)))
    return dict(queries=queries, keys=keys, values=values, block_order=block_order, routes=routes, norm_gain=norm_gain, router=router, w_gate=w_gate, w_up=w_up, w_down=w_down)


def reference(queries, keys, values, block_order, routes, norm_gain, router, w_gate, w_up, w_down):
    half_rows = S_DEV // 2
    row_index = jnp.arange(SEQ, dtype=jnp.int32)
    position = block_order[row_index // half_rows] * half_rows + row_index % half_rows
    per_group = HEADS // KV_HEADS
    score_scale = 1.0 / math.sqrt(HEAD_DIM)
    query_heads = queries.reshape(SEQ, HEADS, HEAD_DIM)
    key_heads = keys.reshape(SEQ, KV_HEADS, HEAD_DIM)
    value_heads = values.reshape(SEQ, KV_HEADS, HEAD_DIM)
    visible = position[None, :] <= position[:, None]

    def attend_head(head_index):
        group_index = head_index // per_group
        query_now = lax.dynamic_index_in_dim(query_heads, head_index, 1, keepdims=False)
        key_now = lax.dynamic_index_in_dim(key_heads, group_index, 1, keepdims=False)
        value_now = lax.dynamic_index_in_dim(value_heads, group_index, 1, keepdims=False)
        scores = jnp.dot(query_now, key_now.T, preferred_element_type=jnp.float32) * score_scale
        scores = jnp.where(visible, scores, -1e+30)
        highest = lax.optimization_barrier(jnp.max(scores, axis=1, keepdims=True))
        probs = jnp.where(visible, jnp.exp(scores - highest), 0.0)
        totals = lax.optimization_barrier(jnp.sum(probs, axis=1))
        mixed = jnp.dot(probs.astype(jnp.bfloat16), value_now, preferred_element_type=jnp.float32)
        return (mixed / totals[:, None]).astype(jnp.bfloat16)
    heads_out = lax.map(attend_head, jnp.arange(HEADS, dtype=jnp.int32))
    attended = heads_out.transpose(1, 0, 2).reshape(SEQ, D)
    values_f32 = attended.astype(jnp.float32)
    inverse = lax.rsqrt(lax.optimization_barrier(jnp.mean(values_f32 * values_f32, axis=1)) + 1e-05)
    normed = values_f32 * inverse[:, None] * norm_gain[None, :]
    logits = jnp.dot(normed, router, precision=lax.Precision.HIGHEST)
    expert_id = routes[:, 0]
    onehot = expert_id[:, None] == jnp.arange(EXPERTS, dtype=jnp.int32)[None, :]
    gate_value = jax.nn.sigmoid(lax.optimization_barrier(jnp.sum(jnp.where(onehot, logits, 0.0), axis=1)))
    expert_in = (normed * gate_value[:, None]).astype(jnp.bfloat16)
    owner = row_index // S_DEV
    counts = onehot.astype(jnp.int32).reshape(N_CTX, S_DEV, EXPERTS)
    earlier = jnp.cumsum(counts, axis=1) - counts
    slot_index = lax.optimization_barrier(jnp.sum(earlier * counts, axis=2)).reshape(SEQ).astype(jnp.int32)
    slot_rows = N_CTX * CAP
    target = (owner * CAP + slot_index).astype(jnp.int32)
    buffer = jnp.zeros((EXPERTS, slot_rows, D), jnp.bfloat16).at[expert_id, target].set(expert_in)
    group_width = FF // N_CTX

    def expert_output(expert_index):
        slot_inputs = lax.dynamic_index_in_dim(buffer, expert_index, 0, keepdims=False)
        gate_matrix = lax.dynamic_index_in_dim(w_gate, expert_index, 0, keepdims=False)
        up_matrix = lax.dynamic_index_in_dim(w_up, expert_index, 0, keepdims=False)
        down_matrix = lax.dynamic_index_in_dim(w_down, expert_index, 0, keepdims=False)
        gate_part = jnp.dot(slot_inputs, gate_matrix, preferred_element_type=jnp.float32)
        up_part = jnp.dot(slot_inputs, up_matrix, preferred_element_type=jnp.float32)
        hidden = (jax.nn.silu(gate_part) * up_part).astype(jnp.bfloat16)
        hidden_groups = hidden.reshape(slot_rows, N_CTX, group_width).transpose(1, 0, 2)
        down_groups = down_matrix.reshape(N_CTX, group_width, D)

        def add_group(running, operands):
            product = jnp.dot(operands[0], operands[1], preferred_element_type=jnp.float32).astype(jnp.bfloat16)
            product = lax.optimization_barrier(product)
            return (running + product.astype(jnp.float32), None)
        running, _ = lax.scan(add_group, jnp.zeros((slot_rows, D), jnp.float32), (hidden_groups, down_groups))
        return running.astype(jnp.bfloat16)
    outputs = lax.map(expert_output, jnp.arange(EXPERTS, dtype=jnp.int32))
    routed = outputs[expert_id, target]
    return (attended, routed)
```

```python
import functools
import math

import jax
import jax.numpy as jnp
from jax import lax
from jax.experimental import pallas as pl
from jax.experimental.pallas import tpu as pltpu
from jax.sharding import PartitionSpec as P

HEAD_DIM = 128
CAP = 32
MESH = pl.DeviceIdType.MESH

PLANES = 2
SIDE = 4
EXPERTS = 8
WIDTH = 5120
CHUNK = WIDTH // EXPERTS
HALF = CAP // 2
PIECE_COLS = WIDTH // 2
GROUP = SIDE * SIDE * HALF
HID = 256


def mod4(v):
    return lax.rem(v + 2 * SIDE, SIDE)


class Torus:
    def __init__(self, h, plane, y, x, e):
        self.h, self.plane, self.y, self.x, self.e = h, plane, y, x, e

    def at(self, dp, dq):
        if self.h == 0:
            return mod4(self.y + dq), mod4(self.x + dp)
        return mod4(self.y + dp), mod4(self.x + dq)

    def rows(self, dp, dq):
        y, x = self.at(dp, dq)
        return pl.ds(pl.multiple_of((y * SIDE + x) * HALF, HALF), HALF)

    def dev(self, dp, dq):
        y, x = self.at(dp, dq)
        return (self.plane * SIDE * SIDE + y * SIDE + x, self.e)


def moe_kernel(
    att_ref,
    routes_ref,
    gain_ref,
    router_ref,
    wg_hbm,
    wu_hbm,
    wd_hbm,
    out_ref,
    wg,
    wu,
    wd,
    pack,
    xin,
    g,
    part,
    ru1,
    ru2,
    rv1,
    rv2,
    fin,
    ret,
    acc,
    hid,
    w_sem,
    a2a_s,
    a2a_r,
    ag_s,
    ag_r,
    rs_s,
    rs_r,
    back_s,
    back_r,
):
    ctx = lax.axis_index("ctx")
    e = lax.axis_index("exp")
    plane = ctx // (SIDE * SIDE)
    other = 1 - plane
    spot = lax.rem(ctx, SIDE * SIDE)
    y, x = spot // SIDE, lax.rem(spot, SIDE)
    tori = [Torus(h, plane, y, x, e) for h in range(2)]
    planes = (plane, other)
    sent = []

    def send(src, dst, ssem, rsem, dev):
        copy = pltpu.make_async_remote_copy(
            src_ref=src, dst_ref=dst, send_sem=ssem, recv_sem=rsem, device_id=dev, device_id_type=MESH
        )
        copy.start()
        sent.append(copy)

    def arrived(dst, ssem, rsem):
        pltpu.make_async_remote_copy(
            src_ref=dst, dst_ref=dst, send_sem=ssem, recv_sem=rsem, device_id=tori[0].dev(1, 0), device_id_type=MESH
        ).wait_recv()

    def column(pl_index, d):
        return (pl_index * SIDE * SIDE + spot, lax.rem(e + d, EXPERTS))

    barrier = pltpu.get_barrier_semaphore()
    partners = [column(plane, d) for d in range(1, EXPERTS)]
    partners += [column(other, d) for d in range(EXPERTS)]
    partners += [tori[0].dev(1, 0), tori[0].dev(-1, 0), tori[0].dev(0, 1), tori[0].dev(0, -1)]
    for dev in partners:
        pl.semaphore_signal(barrier, inc=1, device_id=dev, device_id_type=MESH)

    loads = [
        pltpu.make_async_copy(wg_hbm, wg, w_sem.at[0]),
        pltpu.make_async_copy(wu_hbm, wu, w_sem.at[1]),
        pltpu.make_async_copy(wd_hbm, wd, w_sem.at[2]),
    ]
    for load in loads:
        load.start()

    n_rows = att_ref.shape[0]
    onehot = (lax.broadcasted_iota(jnp.int32, (EXPERTS, n_rows), 0) == routes_ref[...]).astype(jnp.float32)
    before = (
        lax.broadcasted_iota(jnp.int32, (n_rows, n_rows), 0)
        < lax.broadcasted_iota(jnp.int32, (n_rows, n_rows), 1)
    ).astype(jnp.bfloat16)
    earlier = jnp.dot(onehot.astype(jnp.bfloat16), before, preferred_element_type=jnp.float32)
    code = jnp.sum(onehot * earlier, axis=0, keepdims=True).astype(jnp.int32) + routes_ref[...] * CAP
    placing = (lax.broadcasted_iota(jnp.int32, (EXPERTS * CAP, n_rows), 0) == code).astype(jnp.bfloat16)
    packed = jnp.dot(placing, att_ref[...], preferred_element_type=jnp.float32).astype(jnp.bfloat16)
    pack[...] = packed.reshape(EXPERTS, CAP, CHUNK)

    pl.semaphore_wait(barrier, len(partners))

    for w in range(PLANES):
        for d in range(1 - w, EXPERTS):
            to = lax.rem(e + d, EXPERTS)
            send(
                pack.at[to],
                xin.at[w, e],
                a2a_s.at[w, d],
                a2a_r.at[w, d],
                column(planes[w], d),
            )
    own = pltpu.make_async_copy(pack.at[e], xin.at[0, e], a2a_s.at[0, 0])
    own.start()

    def norm(w):
        for d in range(1 - w, EXPERTS):
            src = lax.rem(e - d + EXPERTS, EXPERTS)
            arrived(xin.at[w, src], a2a_s.at[w, d], a2a_r.at[w, d])
        if w == 0:
            own.wait()
        squares = jnp.zeros((CAP, 1), jnp.float32)
        for j in range(EXPERTS):
            v = xin[w, j].astype(jnp.float32)
            squares += jnp.sum(v * v, axis=1, keepdims=True)
        inverse = lax.rsqrt(squares / WIDTH + 1e-05)
        logits = jnp.zeros((CAP, EXPERTS), jnp.float32)
        for j in range(EXPERTS):
            cols = pl.ds(j * CHUNK, CHUNK)
            v = xin[w, j].astype(jnp.float32) * inverse * gain_ref[:, cols]
            logits += jnp.dot(
                v, router_ref[cols, :], precision=lax.Precision.HIGHEST, preferred_element_type=jnp.float32
            )
        mine = lax.broadcasted_iota(jnp.int32, logits.shape, 1) == e
        logit = jnp.sum(jnp.where(mine, logits, 0.0), axis=1, keepdims=True)
        gate = 1.0 / (1.0 + jnp.exp(-logit))
        for j in range(EXPERTS):
            cols = pl.ds(j * CHUNK, CHUNK)
            v = xin[w, j].astype(jnp.float32) * inverse * gain_ref[:, cols]
            v = (v * gate).astype(jnp.bfloat16)
            for t in tori:
                g[w, t.h, t.rows(0, 0), cols] = v[t.h * HALF : (t.h + 1) * HALF]

    left_half, right_half = pl.ds(0, PIECE_COLS), pl.ds(PIECE_COLS, PIECE_COLS)
    OFFS = (0, -1, 1, 2)

    def ag_second(w, t, i):
        piece = g.at[w, t.h, t.rows(OFFS[i], 0)]
        for s, dq in ((0, 1), (1, -1)):
            n = 4 + 2 * i + s
            send(piece, piece, ag_s.at[w, t.h, n], ag_r.at[w, t.h, n], t.dev(0, dq))

    def ag_second_arrived(w, t, i, s):
        n = 4 + 2 * i + s
        arrived(g.at[w, t.h, t.rows(OFFS[i], -1 if s == 0 else 1)], ag_s.at[w, t.h, n], ag_r.at[w, t.h, n])

    def ag_start(w):
        for t in tori:
            piece = g.at[w, t.h, t.rows(0, 0)]
            for s, dp in ((0, 1), (1, -1)):
                send(piece, piece, ag_s.at[w, t.h, s], ag_r.at[w, t.h, s], t.dev(dp, 0))
        for t in tori:
            ag_second(w, t, 0)

    def ag_near(w):
        for t in tori:
            for s, dp, cols in ((0, -1, left_half), (1, 1, right_half)):
                arrived(g.at[w, t.h, t.rows(dp, 0)], ag_s.at[w, t.h, s], ag_r.at[w, t.h, s])
                part_of = g.at[w, t.h, t.rows(dp, 0), cols]
                send(part_of, part_of, ag_s.at[w, t.h, 2 + s], ag_r.at[w, t.h, 2 + s], t.dev(-dp, 0))
        for t in tori:
            ag_second(w, t, 1)
            ag_second(w, t, 2)

    def ag_far(w):
        for t in tori:
            for s, cols in ((0, left_half), (1, right_half)):
                arrived(g.at[w, t.h, t.rows(2, 0), cols], ag_s.at[w, t.h, 2 + s], ag_r.at[w, t.h, 2 + s])
            ag_second(w, t, 3)

    OPPOSITE = ((0, 0), (1, 1), (2, 1), (3, 0))

    def ag_forward(w, i):
        s = OPPOSITE[i][1]
        dq = 1 if s == 0 else -1
        for t in tori:
            ag_second_arrived(w, t, i, s)
            piece = g.at[w, t.h, t.rows(OFFS[i], -dq)]
            send(piece, piece, ag_s.at[w, t.h, 12 + i], ag_r.at[w, t.h, 12 + i], t.dev(0, dq))

    def ag_done(w, t):
        for i in range(4):
            ag_second_arrived(w, t, i, 1 - OPPOSITE[i][1])
            arrived(g.at[w, t.h, t.rows(OFFS[i], 2)], ag_s.at[w, t.h, 12 + i], ag_r.at[w, t.h, 12 + i])

    def ffn(w, h):
        step = 1280
        acc[...] = jnp.zeros_like(acc)

        @pl.loop(0, WIDTH // step)
        def _(k):
            cols = pl.ds(pl.multiple_of(k * step, step), step)
            rows = g[w, h, :, cols]
            acc[0] += jnp.dot(rows, wg[cols, :], preferred_element_type=jnp.float32)
            acc[1] += jnp.dot(rows, wu[cols, :], preferred_element_type=jnp.float32)

        v = acc[0]
        hid[...] = (v / (1.0 + jnp.exp(-v)) * acc[1]).astype(jnp.bfloat16)
        wide = 512

        @pl.loop(0, WIDTH // wide)
        def _(k):
            cols = pl.ds(pl.multiple_of(k * wide, wide), wide)
            part[w, h, :, cols] = jnp.dot(hid[...], wd[:, cols], preferred_element_type=jnp.float32).astype(
                jnp.bfloat16
            )

    def add(ref, *more):
        total = ref[...].astype(jnp.float32)
        for m in more:
            total = total + m[...].astype(jnp.float32)
        ref[...] = total.astype(jnp.bfloat16)

    def rs_start(w):
        for t in tori:
            for i, s in OPPOSITE:
                send(
                    part.at[w, t.h, t.rows(OFFS[i], 2)],
                    ru1.at[w, t.h, i],
                    rs_s.at[w, t.h, i],
                    rs_r.at[w, t.h, i],
                    t.dev(0, 1 if s == 0 else -1),
                )

    def rs_second(w, t, i, s):
        n = 4 + 2 * i + s
        dq = 1 if s == 0 else -1
        send(
            part.at[w, t.h, t.rows(OFFS[i], dq)],
            ru2.at[w, t.h, i, s],
            rs_s.at[w, t.h, n],
            rs_r.at[w, t.h, n],
            t.dev(0, dq),
        )

    def rs_plain(w):
        for t in tori:
            for i, s in OPPOSITE:
                rs_second(w, t, i, 1 - s)

    def rs_joined(w, i):
        s = OPPOSITE[i][1]
        dq = 1 if s == 0 else -1
        for t in tori:
            arrived(ru1.at[w, t.h, i], rs_s.at[w, t.h, i], rs_r.at[w, t.h, i])
            add(part.at[w, t.h, t.rows(OFFS[i], dq)], ru1.at[w, t.h, i])
            rs_second(w, t, i, s)

    def rs_sum(w, t, i):
        for s in range(2):
            n = 4 + 2 * i + s
            arrived(ru2.at[w, t.h, i, s], rs_s.at[w, t.h, n], rs_r.at[w, t.h, n])
        add(part.at[w, t.h, t.rows(OFFS[i], 0)], ru2.at[w, t.h, i, 0], ru2.at[w, t.h, i, 1])

    def rs_turn(w):
        for t in tori:
            rs_sum(w, t, 3)
            for s, dp, cols in ((0, 1, left_half), (1, -1, right_half)):
                send(
                    part.at[w, t.h, t.rows(2, 0), cols],
                    rv1.at[w, t.h, s],
                    rs_s.at[w, t.h, 12 + s],
                    rs_r.at[w, t.h, 12 + s],
                    t.dev(dp, 0),
                )
        for t in tori:
            for i in (1, 2):
                rs_sum(w, t, i)

    def rs_last(w):
        for t in tori:
            for s, dp, cols in ((0, 1, left_half), (1, -1, right_half)):
                arrived(rv1.at[w, t.h, s], rs_s.at[w, t.h, 12 + s], rs_r.at[w, t.h, 12 + s])
                add(part.at[w, t.h, t.rows(dp, 0), cols], rv1.at[w, t.h, s])
                send(
                    part.at[w, t.h, t.rows(dp, 0)],
                    rv2.at[w, t.h, s],
                    rs_s.at[w, t.h, 14 + s],
                    rs_r.at[w, t.h, 14 + s],
                    t.dev(dp, 0),
                )
        for t in tori:
            rs_sum(w, t, 0)

    def rs_finish(w):
        for t in tori:
            for s in range(2):
                arrived(rv2.at[w, t.h, s], rs_s.at[w, t.h, 14 + s], rs_r.at[w, t.h, 14 + s])
            for j in range(EXPERTS):
                cols = pl.ds(j * CHUNK, CHUNK)
                total = part[w, t.h, t.rows(0, 0), cols].astype(jnp.float32)
                for s in range(2):
                    total = total + rv2[w, t.h, s, :, cols].astype(jnp.float32)
                fin[w, j, pl.ds(t.h * HALF, HALF)] = total.astype(jnp.bfloat16)

    def back(w):
        for d in range(1 - w, EXPERTS):
            to = lax.rem(e + d, EXPERTS)
            send(fin.at[w, to], ret.at[w, e], back_s.at[w, d], back_r.at[w, d], column(planes[w], d))

    ag = ag_start
    norm(0)
    ag(0)
    norm(1)
    ag_near(0)
    ag_far(0)
    ag(1)
    ag_forward(0, 0)
    ag_forward(0, 1)
    ag_near(1)
    ag_forward(0, 2)
    ag_forward(0, 3)
    ag_far(1)
    for load in loads:
        load.wait()
    ag_done(0, tori[0])
    ag_done(0, tori[1])
    ag_forward(1, 0)
    ag_forward(1, 1)
    ffn(0, 0)
    ag_forward(1, 2)
    ag_forward(1, 3)
    ffn(0, 1)
    rs_start(0)
    rs_plain(0)
    ag_done(1, tori[0])
    ag_done(1, tori[1])
    for i in range(4):
        rs_joined(0, i)
    ffn(1, 0)
    ffn(1, 1)
    rs_start(1)
    rs_plain(1)
    rs_turn(0)
    for i in range(4):
        rs_joined(1, i)
    rs_last(0)
    rs_finish(0)
    back(0)
    rs_turn(1)
    rs_last(1)
    rs_finish(1)
    back(1)
    mine = pltpu.make_async_copy(fin.at[0, e], ret.at[0, e], back_s.at[0, 0])
    mine.start()

    routed = None
    for w in range(PLANES):
        for d in range(1 - w, EXPERTS):
            src = lax.rem(e - d + EXPERTS, EXPERTS)
            arrived(ret.at[w, src], back_s.at[w, d], back_r.at[w, d])
        if w == 0:
            mine.wait()
        rows = ret[w].reshape(EXPERTS * CAP, CHUNK)
        term = lax.dot_general(
            placing, rows, (((0,), (0,)), ((), ())), preferred_element_type=jnp.float32
        )
        routed = term if routed is None else routed + term
    out_ref[...] = routed.astype(jnp.bfloat16)
    for copy in sent:
        copy.wait_send()


def moe(attended, routes, norm_gain, router, w_gate, w_up, w_down):
    vmem = pl.BlockSpec(memory_space=pltpu.VMEM)
    anywhere = pl.BlockSpec(memory_space=pl.ANY)
    bf16, f32 = jnp.bfloat16, jnp.float32
    dma = pltpu.SemaphoreType.DMA
    return pl.pallas_call(
        moe_kernel,
        out_shape=jax.ShapeDtypeStruct(attended.shape, bf16),
        in_specs=[vmem, vmem, vmem, vmem, anywhere, anywhere, anywhere],
        out_specs=vmem,
        scratch_shapes=[
            pltpu.VMEM((WIDTH, HID), bf16),
            pltpu.VMEM((WIDTH, HID), bf16),
            pltpu.VMEM((HID, WIDTH), bf16),
            pltpu.VMEM((EXPERTS, CAP, CHUNK), bf16),
            pltpu.VMEM((PLANES, EXPERTS, CAP, CHUNK), bf16),
            pltpu.VMEM((PLANES, 2, GROUP, WIDTH), bf16),
            pltpu.VMEM((PLANES, 2, GROUP, WIDTH), bf16),
            pltpu.VMEM((PLANES, 2, 4, HALF, WIDTH), bf16),
            pltpu.VMEM((PLANES, 2, 4, 2, HALF, WIDTH), bf16),
            pltpu.VMEM((PLANES, 2, 2, HALF, PIECE_COLS), bf16),
            pltpu.VMEM((PLANES, 2, 2, HALF, WIDTH), bf16),
            pltpu.VMEM((PLANES, EXPERTS, CAP, CHUNK), bf16),
            pltpu.VMEM((PLANES, EXPERTS, CAP, CHUNK), bf16),
            pltpu.VMEM((2, GROUP, HID), f32),
            pltpu.VMEM((GROUP, HID), bf16),
            dma((3,)),
            dma((PLANES, EXPERTS)),
            dma((PLANES, EXPERTS)),
            dma((PLANES, 2, 16)),
            dma((PLANES, 2, 16)),
            dma((PLANES, 2, 16)),
            dma((PLANES, 2, 16)),
            dma((PLANES, EXPERTS)),
            dma((PLANES, EXPERTS)),
        ],
        compiler_params=pltpu.CompilerParams(
            collective_id=1, has_side_effects=True, vmem_limit_bytes=62 << 20
        ),
        name="experts",
    )(
        attended,
        routes.reshape(1, -1),
        norm_gain.reshape(1, -1),
        router,
        w_gate[0],
        w_up[0],
        w_down[0],
    )


def per_device(queries, keys, values, block_order, routes, norm_gain, router, w_gate, w_up, w_down):
    rows_here = queries.shape[0]
    ctx_index = lax.axis_index("ctx")
    kv_local = keys.shape[1] // HEAD_DIM
    q_local = queries.shape[1] // HEAD_DIM
    per_group = q_local // kv_local
    half_rows = rows_here // 2
    position = (block_order[:, None] * half_rows + jnp.arange(half_rows, dtype=jnp.int32)[None, :]).reshape(-1)
    query_pos = lax.dynamic_slice_in_dim(position, ctx_index * rows_here, rows_here)
    grouped = queries.reshape(rows_here, kv_local, per_group, HEAD_DIM)
    score_scale = 1.0 / math.sqrt(HEAD_DIM)
    key_piece = lax.all_gather(keys, "ctx", axis=0, tiled=True)
    value_piece = lax.all_gather(values, "ctx", axis=0, tiled=True)
    piece_rows = key_piece.shape[0]
    scores = (
        jnp.einsum(
            "sgqd,rgd->gqsr",
            grouped,
            key_piece.reshape(piece_rows, kv_local, HEAD_DIM),
            preferred_element_type=jnp.float32,
        )
        * score_scale
    )
    allowed = position[None, :] <= query_pos[:, None]
    scores = jnp.where(allowed, scores, -1e30)
    newest_max = jnp.max(scores, axis=3)
    weights = jnp.where(allowed, jnp.exp(scores - newest_max[..., None]), 0.0)
    running_sum = jnp.sum(weights, axis=3)
    weighted = jnp.einsum(
        "gqsr,rgd->gqsd",
        weights.astype(jnp.bfloat16),
        value_piece.reshape(piece_rows, kv_local, HEAD_DIM),
        preferred_element_type=jnp.float32,
    )
    attended = (
        (weighted / running_sum[..., None])
        .transpose(2, 0, 1, 3)
        .reshape(rows_here, q_local * HEAD_DIM)
    )
    attended = attended.astype(jnp.bfloat16)
    routed = moe(attended, routes, norm_gain, router, w_gate, w_up, w_down)
    return (attended, routed)


def solution(mesh):
    in_specs = (
        P("ctx", "exp"),
        P("ctx", "exp"),
        P("ctx", "exp"),
        P(),
        P("ctx", None),
        P(),
        P(),
        P("exp", None, "ctx"),
        P("exp", None, "ctx"),
        P("exp", "ctx", None),
    )
    out_specs = (P("ctx", "exp"), P("ctx", "exp"))
    return jax.shard_map(
        per_device, mesh=mesh, in_specs=in_specs, out_specs=out_specs, check_vma=False
    )
```

```python
import functools
import math

import jax
import jax.numpy as jnp
from jax import lax
from jax.experimental import pallas as pl
from jax.experimental.pallas import tpu as pltpu
from jax.sharding import PartitionSpec as P

HEAD_DIM = 128
CAP = 32
MESH = pl.DeviceIdType.MESH

PLANES = 2
SIDE = 4
EXPERTS = 8
WIDTH = 5120
CHUNK = WIDTH // EXPERTS
HALF = CAP // 2
PIECE_COLS = WIDTH // 2
GROUP = SIDE * SIDE * HALF
HID = 256


def mod4(v):
    return lax.rem(v + 2 * SIDE, SIDE)


OFFS = (0, -1, 1, 2)
OPPOSITE = ((0, 0), (1, 1), (2, 1), (3, 0))


class Gather:
    def __init__(self, tori, piece, half, ssem, rsem, send, arrived):
        self.tori, self.piece, self.half = tori, piece, half
        self.ssem, self.rsem, self.send, self.arrived = ssem, rsem, send, arrived

    def sems(self, t, n):
        return self.ssem.at[t.h, n], self.rsem.at[t.h, n]

    def second(self, t, i):
        piece = self.piece(t, OFFS[i], 0)
        for s, dq in ((0, 1), (1, -1)):
            self.send(piece, piece, *self.sems(t, 4 + 2 * i + s), t.dev(0, dq))

    def second_arrived(self, t, i, s):
        self.arrived(self.piece(t, OFFS[i], -1 if s == 0 else 1), *self.sems(t, 4 + 2 * i + s))

    def start(self):
        for t in self.tori:
            piece = self.piece(t, 0, 0)
            for s, dp in ((0, 1), (1, -1)):
                self.send(piece, piece, *self.sems(t, s), t.dev(dp, 0))
        for t in self.tori:
            self.second(t, 0)

    def near(self):
        for t in self.tori:
            for s, dp in ((0, -1), (1, 1)):
                self.arrived(self.piece(t, dp, 0), *self.sems(t, s))
                half = self.half(t, dp, 0, s)
                self.send(half, half, *self.sems(t, 2 + s), t.dev(-dp, 0))
        for t in self.tori:
            self.second(t, 1)
            self.second(t, 2)

    def far(self):
        for t in self.tori:
            for s in range(2):
                self.arrived(self.half(t, 2, 0, s), *self.sems(t, 2 + s))
            self.second(t, 3)

    def forward(self, i):
        s = OPPOSITE[i][1]
        dq = 1 if s == 0 else -1
        for t in self.tori:
            self.second_arrived(t, i, s)
            piece = self.piece(t, OFFS[i], -dq)
            self.send(piece, piece, *self.sems(t, 12 + i), t.dev(0, dq))

    def done(self):
        for t in self.tori:
            for i in range(4):
                self.second_arrived(t, i, 1 - OPPOSITE[i][1])
                self.arrived(self.piece(t, OFFS[i], 2), *self.sems(t, 12 + i))


class Torus:
    def __init__(self, h, plane, y, x, e):
        self.h, self.plane, self.y, self.x, self.e = h, plane, y, x, e

    def at(self, dp, dq):
        if self.h == 0:
            return mod4(self.y + dq), mod4(self.x + dp)
        return mod4(self.y + dp), mod4(self.x + dq)

    def rows(self, dp, dq, n=HALF, first=0, count=None):
        y, x = self.at(dp, dq)
        return pl.ds(pl.multiple_of((y * SIDE + x) * n + first, HALF), count or n)

    def dev(self, dp, dq):
        y, x = self.at(dp, dq)
        return (self.plane * SIDE * SIDE + y * SIDE + x, self.e)


def kernel(
    q_ref,
    k_ref,
    v_ref,
    order_ref,
    routes_ref,
    gain_ref,
    router_ref,
    wg_hbm,
    wu_hbm,
    wd_hbm,
    att_ref,
    out_ref,
    kv,
    soft_max,
    soft_sum,
    soft_acc,
    wg,
    wu,
    wd,
    pack,
    xin,
    g,
    part,
    ru1,
    ru2,
    rv1,
    rv2,
    fin,
    ret,
    acc,
    hid,
    w_sem,
    z_s,
    z_r,
    kv_s,
    kv_r,
    a2a_s,
    a2a_r,
    ag_s,
    ag_r,
    rs_s,
    rs_r,
    back_s,
    back_r,
):
    ctx = lax.axis_index("ctx")
    e = lax.axis_index("exp")
    plane = ctx // (SIDE * SIDE)
    other = 1 - plane
    spot = lax.rem(ctx, SIDE * SIDE)
    y, x = spot // SIDE, lax.rem(spot, SIDE)
    tori = [Torus(h, plane, y, x, e) for h in range(2)]
    planes = (plane, other)
    sent = []

    def send(src, dst, ssem, rsem, dev):
        copy = pltpu.make_async_remote_copy(
            src_ref=src, dst_ref=dst, send_sem=ssem, recv_sem=rsem, device_id=dev, device_id_type=MESH
        )
        copy.start()
        sent.append(copy)

    def arrived(dst, ssem, rsem):
        pltpu.make_async_remote_copy(
            src_ref=dst, dst_ref=dst, send_sem=ssem, recv_sem=rsem, device_id=tori[0].dev(1, 0), device_id_type=MESH
        ).wait_recv()

    def column(pl_index, d):
        return (pl_index * SIDE * SIDE + spot, lax.rem(e + d, EXPERTS))

    barrier = pltpu.get_barrier_semaphore()
    partners = [column(plane, d) for d in range(1, EXPERTS)]
    partners += [column(other, d) for d in range(EXPERTS)]
    partners += [tori[0].dev(1, 0), tori[0].dev(-1, 0), tori[0].dev(0, 1), tori[0].dev(0, -1)]
    for dev in partners:
        pl.semaphore_signal(barrier, inc=1, device_id=dev, device_id_type=MESH)

    loads = [
        pltpu.make_async_copy(wg_hbm, wg, w_sem.at[0]),
        pltpu.make_async_copy(wu_hbm, wu, w_sem.at[1]),
        pltpu.make_async_copy(wd_hbm, wd, w_sem.at[2]),
    ]
    for load in loads:
        load.start()

    n_rows = att_ref.shape[0]
    onehot = (lax.broadcasted_iota(jnp.int32, (EXPERTS, n_rows), 0) == routes_ref[...]).astype(jnp.float32)
    before = (
        lax.broadcasted_iota(jnp.int32, (n_rows, n_rows), 0)
        < lax.broadcasted_iota(jnp.int32, (n_rows, n_rows), 1)
    ).astype(jnp.bfloat16)
    earlier = jnp.dot(onehot.astype(jnp.bfloat16), before, preferred_element_type=jnp.float32)
    code = jnp.sum(onehot * earlier, axis=0, keepdims=True).astype(jnp.int32) + routes_ref[...] * CAP
    placing = (lax.broadcasted_iota(jnp.int32, (EXPERTS * CAP, n_rows), 0) == code).astype(jnp.bfloat16)

    n = n_rows
    kv[0, 0, tori[0].rows(0, 0, n)] = k_ref[...]
    kv[0, 1, tori[1].rows(0, 0, n)] = v_ref[...]
    soft_max[...] = jnp.full_like(soft_max, -1e30)
    soft_sum[...] = jnp.zeros_like(soft_sum)
    soft_acc[...] = jnp.zeros_like(soft_acc)
    pl.semaphore_wait(barrier, len(partners))

    kv_gather = [
        Gather(
            tori,
            lambda t, dp, dq, w=w: kv.at[w, t.h, t.rows(dp, dq, n)],
            lambda t, dp, dq, s, w=w: kv.at[w, t.h, t.rows(dp, dq, n, s * (n // 2), n // 2)],
            kv_s.at[w],
            kv_r.at[w],
            send,
            arrived,
        )
        for w in range(PLANES)
    ]
    for t in tori:
        send(
            kv.at[0, t.h, t.rows(0, 0, n)],
            kv.at[1, t.h, t.rows(0, 0, n)],
            z_s.at[t.h],
            z_r.at[t.h],
            column(other, 0),
        )
    kv_gather[0].start()

    half_n = n // 2
    rising = lax.broadcasted_iota(jnp.int32, (n, 1), 0)
    query_pos = rising + jnp.where(
        rising < half_n, order_ref[2 * ctx] * half_n, (order_ref[2 * ctx + 1] - 1) * half_n
    )
    lanes = lax.broadcasted_iota(jnp.int32, (1, n), 1)
    scale = math.log2(math.e) / math.sqrt(HEAD_DIM)

    def attend(w, dy):
        row = mod4(y + dy)
        biases = []
        for i in range(SIDE):
            c = planes[w] * SIDE * SIDE + row * SIDE + i
            key_pos = lanes + jnp.where(
                lanes < half_n, order_ref[2 * c] * half_n, (order_ref[2 * c + 1] - 1) * half_n
            )
            biases.append(jnp.where(key_pos <= query_pos, 0.0, -1e30))
        bias = jnp.concatenate(biases, axis=1)
        there = pl.ds(pl.multiple_of(row * SIDE * n, SIDE * n), SIDE * n)
        keys, values = kv[w, 0, there], kv[w, 1, there]
        for head in range(q_ref.shape[1] // HEAD_DIM):
            q = q_ref[:, pl.ds(head * HEAD_DIM, HEAD_DIM)]
            scores = lax.dot_general(q, keys, (((1,), (1,)), ((), ())), preferred_element_type=jnp.float32)
            scores = scores + bias
            old = soft_max[head]
            new = jnp.maximum(old, jnp.max(scores, axis=1, keepdims=True))
            soft_max[head] = new
            fade = jnp.exp2((old - new) * scale)
            probs = jnp.exp2((scores - jnp.concatenate([new] * SIDE, axis=1)) * scale)
            total = soft_sum[head] * fade
            for i in range(SIDE):
                total = total + probs[:, i * n : (i + 1) * n]
            soft_sum[head] = total
            soft_acc[head] = soft_acc[head] * fade + jnp.dot(
                probs.astype(jnp.bfloat16), values, preferred_element_type=jnp.float32
            )

    kv_gather[0].near()
    for t in tori:
        arrived(kv.at[1, t.h, t.rows(0, 0, n)], z_s.at[t.h], z_r.at[t.h])
    kv_gather[1].start()
    kv_gather[0].forward(0)
    kv_gather[0].far()
    kv_gather[0].forward(1)
    kv_gather[0].forward(2)
    kv_gather[1].near()
    kv_gather[0].forward(3)
    kv_gather[1].forward(0)
    kv_gather[1].far()
    kv_gather[1].forward(1)
    kv_gather[1].forward(2)
    kv_gather[0].done()
    attend(0, 0)
    kv_gather[1].forward(3)
    for dy in (-1, 1, 2):
        attend(0, dy)
    kv_gather[1].done()
    for dy in (0, -1, 1, 2):
        attend(1, dy)
    for head in range(q_ref.shape[1] // HEAD_DIM):
        total = jnp.sum(soft_sum[head], axis=1, keepdims=True)
        att_ref[:, pl.ds(head * HEAD_DIM, HEAD_DIM)] = (soft_acc[head] / total).astype(jnp.bfloat16)

    packed = jnp.dot(placing, att_ref[...], preferred_element_type=jnp.float32).astype(jnp.bfloat16)
    pack[...] = packed.reshape(EXPERTS, CAP, CHUNK)

    for w in range(PLANES):
        for d in range(1 - w, EXPERTS):
            to = lax.rem(e + d, EXPERTS)
            send(
                pack.at[to],
                xin.at[w, e],
                a2a_s.at[w, d],
                a2a_r.at[w, d],
                column(planes[w], d),
            )
    own = pltpu.make_async_copy(pack.at[e], xin.at[0, e], a2a_s.at[0, 0])
    own.start()

    def norm(w):
        for d in range(1 - w, EXPERTS):
            src = lax.rem(e - d + EXPERTS, EXPERTS)
            arrived(xin.at[w, src], a2a_s.at[w, d], a2a_r.at[w, d])
        if w == 0:
            own.wait()
        squares = jnp.zeros((CAP, 1), jnp.float32)
        for j in range(EXPERTS):
            v = xin[w, j].astype(jnp.float32)
            squares += jnp.sum(v * v, axis=1, keepdims=True)
        inverse = lax.rsqrt(squares / WIDTH + 1e-05)
        mine = lax.broadcasted_iota(jnp.int32, (EXPERTS, CHUNK), 0) == e
        logit = jnp.zeros((CAP, 1), jnp.float32)
        for j in range(EXPERTS):
            cols = pl.ds(j * CHUNK, CHUNK)
            v = xin[w, j].astype(jnp.float32) * inverse * gain_ref[:, cols]
            weight = jnp.sum(jnp.where(mine, router_ref[:, cols], 0.0), axis=0, keepdims=True)
            logit += jnp.sum(v * weight, axis=1, keepdims=True)
        gate = 1.0 / (1.0 + jnp.exp(-logit))
        for j in range(EXPERTS):
            cols = pl.ds(j * CHUNK, CHUNK)
            v = xin[w, j].astype(jnp.float32) * inverse * gain_ref[:, cols]
            v = (v * gate).astype(jnp.bfloat16)
            for t in tori:
                g[w, t.h, t.rows(0, 0), cols] = v[t.h * HALF : (t.h + 1) * HALF]

    left_half, right_half = pl.ds(0, PIECE_COLS), pl.ds(PIECE_COLS, PIECE_COLS)
    gather = [
        Gather(
            tori,
            lambda t, dp, dq, w=w: g.at[w, t.h, t.rows(dp, dq)],
            lambda t, dp, dq, s, w=w: g.at[w, t.h, t.rows(dp, dq), pl.ds(s * PIECE_COLS, PIECE_COLS)],
            ag_s.at[w],
            ag_r.at[w],
            send,
            arrived,
        )
        for w in range(PLANES)
    ]

    def ffn(w, h):
        step = 1280
        acc[...] = jnp.zeros_like(acc)

        @pl.loop(0, WIDTH // step)
        def _(k):
            cols = pl.ds(pl.multiple_of(k * step, step), step)
            rows = g[w, h, :, cols]
            acc[0] += jnp.dot(rows, wg[cols, :], preferred_element_type=jnp.float32)
            acc[1] += jnp.dot(rows, wu[cols, :], preferred_element_type=jnp.float32)

        v = acc[0]
        hid[...] = (v / (1.0 + jnp.exp(-v)) * acc[1]).astype(jnp.bfloat16)
        wide = 512

        @pl.loop(0, WIDTH // wide)
        def _(k):
            cols = pl.ds(pl.multiple_of(k * wide, wide), wide)
            part[w, h, :, cols] = jnp.dot(hid[...], wd[:, cols], preferred_element_type=jnp.float32).astype(
                jnp.bfloat16
            )

    def add(ref, *more):
        total = ref[...].astype(jnp.float32)
        for m in more:
            total = total + m[...].astype(jnp.float32)
        ref[...] = total.astype(jnp.bfloat16)

    def rs_start(w):
        for t in tori:
            for i, s in OPPOSITE:
                send(
                    part.at[w, t.h, t.rows(OFFS[i], 2)],
                    ru1.at[w, t.h, i],
                    rs_s.at[w, t.h, i],
                    rs_r.at[w, t.h, i],
                    t.dev(0, 1 if s == 0 else -1),
                )

    def rs_second(w, t, i, s):
        n = 4 + 2 * i + s
        dq = 1 if s == 0 else -1
        send(
            part.at[w, t.h, t.rows(OFFS[i], dq)],
            ru2.at[w, t.h, i, s],
            rs_s.at[w, t.h, n],
            rs_r.at[w, t.h, n],
            t.dev(0, dq),
        )

    def rs_plain(w):
        for t in tori:
            for i, s in OPPOSITE:
                rs_second(w, t, i, 1 - s)

    def rs_joined(w, i):
        s = OPPOSITE[i][1]
        dq = 1 if s == 0 else -1
        for t in tori:
            arrived(ru1.at[w, t.h, i], rs_s.at[w, t.h, i], rs_r.at[w, t.h, i])
            add(part.at[w, t.h, t.rows(OFFS[i], dq)], ru1.at[w, t.h, i])
            rs_second(w, t, i, s)

    def rs_sum(w, t, i):
        for s in range(2):
            n = 4 + 2 * i + s
            arrived(ru2.at[w, t.h, i, s], rs_s.at[w, t.h, n], rs_r.at[w, t.h, n])
        add(part.at[w, t.h, t.rows(OFFS[i], 0)], ru2.at[w, t.h, i, 0], ru2.at[w, t.h, i, 1])

    def rs_turn(w):
        for t in tori:
            rs_sum(w, t, 3)
            for s, dp, cols in ((0, 1, left_half), (1, -1, right_half)):
                send(
                    part.at[w, t.h, t.rows(2, 0), cols],
                    rv1.at[w, t.h, s],
                    rs_s.at[w, t.h, 12 + s],
                    rs_r.at[w, t.h, 12 + s],
                    t.dev(dp, 0),
                )
        for t in tori:
            for i in (1, 2):
                rs_sum(w, t, i)

    def rs_last(w):
        for t in tori:
            for s, dp, cols in ((0, 1, left_half), (1, -1, right_half)):
                arrived(rv1.at[w, t.h, s], rs_s.at[w, t.h, 12 + s], rs_r.at[w, t.h, 12 + s])
                add(part.at[w, t.h, t.rows(dp, 0), cols], rv1.at[w, t.h, s])
                send(
                    part.at[w, t.h, t.rows(dp, 0)],
                    rv2.at[w, t.h, s],
                    rs_s.at[w, t.h, 14 + s],
                    rs_r.at[w, t.h, 14 + s],
                    t.dev(dp, 0),
                )
        for t in tori:
            rs_sum(w, t, 0)

    def rs_finish(w):
        for t in tori:
            for s in range(2):
                arrived(rv2.at[w, t.h, s], rs_s.at[w, t.h, 14 + s], rs_r.at[w, t.h, 14 + s])
            for j in range(EXPERTS):
                cols = pl.ds(j * CHUNK, CHUNK)
                total = part[w, t.h, t.rows(0, 0), cols].astype(jnp.float32)
                for s in range(2):
                    total = total + rv2[w, t.h, s, :, cols].astype(jnp.float32)
                fin[w, j, pl.ds(t.h * HALF, HALF)] = total.astype(jnp.bfloat16)

    def back(w):
        for d in range(1 - w, EXPERTS):
            to = lax.rem(e + d, EXPERTS)
            send(fin.at[w, to], ret.at[w, e], back_s.at[w, d], back_r.at[w, d], column(planes[w], d))

    norm(0)
    gather[0].start()
    norm(1)
    gather[0].near()
    gather[0].far()
    gather[1].start()
    gather[0].forward(0)
    gather[0].forward(1)
    gather[1].near()
    gather[0].forward(2)
    gather[0].forward(3)
    gather[1].far()
    for load in loads:
        load.wait()
    gather[0].done()
    gather[1].forward(0)
    gather[1].forward(1)
    ffn(0, 0)
    gather[1].forward(2)
    gather[1].forward(3)
    ffn(0, 1)
    rs_start(0)
    rs_plain(0)
    gather[1].done()
    for i in range(4):
        rs_joined(0, i)
    ffn(1, 0)
    ffn(1, 1)
    rs_start(1)
    rs_plain(1)
    rs_turn(0)
    for i in range(4):
        rs_joined(1, i)
    rs_last(0)
    rs_finish(0)
    back(0)
    rs_turn(1)
    rs_last(1)
    rs_finish(1)
    back(1)
    mine = pltpu.make_async_copy(fin.at[0, e], ret.at[0, e], back_s.at[0, 0])
    mine.start()

    routed = None
    for w in range(PLANES):
        for d in range(1 - w, EXPERTS):
            src = lax.rem(e - d + EXPERTS, EXPERTS)
            arrived(ret.at[w, src], back_s.at[w, d], back_r.at[w, d])
        if w == 0:
            mine.wait()
        rows = ret[w].reshape(EXPERTS * CAP, CHUNK)
        term = lax.dot_general(
            placing, rows, (((0,), (0,)), ((), ())), preferred_element_type=jnp.float32
        )
        routed = term if routed is None else routed + term
    out_ref[...] = routed.astype(jnp.bfloat16)
    for copy in sent:
        copy.wait_send()


def per_device(queries, keys, values, block_order, routes, norm_gain, router, w_gate, w_up, w_down):
    vmem = pl.BlockSpec(memory_space=pltpu.VMEM)
    smem = pl.BlockSpec(memory_space=pltpu.SMEM)
    anywhere = pl.BlockSpec(memory_space=pl.ANY)
    bf16, f32 = jnp.bfloat16, jnp.float32
    dma = pltpu.SemaphoreType.DMA
    here, features = queries.shape
    heads = features // HEAD_DIM
    return pl.pallas_call(
        kernel,
        out_shape=(jax.ShapeDtypeStruct(queries.shape, bf16),) * 2,
        in_specs=[vmem, vmem, vmem, smem, vmem, vmem, vmem, anywhere, anywhere, anywhere],
        out_specs=(vmem, vmem),
        scratch_shapes=[
            pltpu.VMEM((PLANES, 2, SIDE * SIDE * here, HEAD_DIM), bf16),
            pltpu.VMEM((heads, here, HEAD_DIM), f32),
            pltpu.VMEM((heads, here, HEAD_DIM), f32),
            pltpu.VMEM((heads, here, HEAD_DIM), f32),
            pltpu.VMEM((WIDTH, HID), bf16),
            pltpu.VMEM((WIDTH, HID), bf16),
            pltpu.VMEM((HID, WIDTH), bf16),
            pltpu.VMEM((EXPERTS, CAP, CHUNK), bf16),
            pltpu.VMEM((PLANES, EXPERTS, CAP, CHUNK), bf16),
            pltpu.VMEM((PLANES, 2, GROUP, WIDTH), bf16),
            pltpu.VMEM((PLANES, 2, GROUP, WIDTH), bf16),
            pltpu.VMEM((PLANES, 2, 4, HALF, WIDTH), bf16),
            pltpu.VMEM((PLANES, 2, 4, 2, HALF, WIDTH), bf16),
            pltpu.VMEM((PLANES, 2, 2, HALF, PIECE_COLS), bf16),
            pltpu.VMEM((PLANES, 2, 2, HALF, WIDTH), bf16),
            pltpu.VMEM((PLANES, EXPERTS, CAP, CHUNK), bf16),
            pltpu.VMEM((PLANES, EXPERTS, CAP, CHUNK), bf16),
            pltpu.VMEM((2, GROUP, HID), f32),
            pltpu.VMEM((GROUP, HID), bf16),
            dma((3,)),
            dma((2,)),
            dma((2,)),
            dma((PLANES, 2, 16)),
            dma((PLANES, 2, 16)),
            dma((PLANES, EXPERTS)),
            dma((PLANES, EXPERTS)),
            dma((PLANES, 2, 16)),
            dma((PLANES, 2, 16)),
            dma((PLANES, 2, 16)),
            dma((PLANES, 2, 16)),
            dma((PLANES, EXPERTS)),
            dma((PLANES, EXPERTS)),
        ],
        compiler_params=pltpu.CompilerParams(
            collective_id=1, has_side_effects=True, vmem_limit_bytes=62 << 20
        ),
        name="layer",
    )(
        queries,
        keys,
        values,
        block_order,
        routes.reshape(1, -1),
        norm_gain.reshape(1, -1),
        router.T,
        w_gate[0],
        w_up[0],
        w_down[0],
    )


def solution(mesh):
    in_specs = (
        P("ctx", "exp"),
        P("ctx", "exp"),
        P("ctx", "exp"),
        P(),
        P("ctx", None),
        P(),
        P(),
        P("exp", None, "ctx"),
        P("exp", None, "ctx"),
        P("exp", "ctx", None),
    )
    out_specs = (P("ctx", "exp"), P("ctx", "exp"))
    return jax.shard_map(
        per_device, mesh=mesh, in_specs=in_specs, out_specs=out_specs, check_vma=False
    )
```

```python
import functools
import math

import jax
import jax.numpy as jnp
from jax import lax
from jax.experimental import pallas as pl
from jax.experimental.pallas import tpu as pltpu
from jax.sharding import PartitionSpec as P

HEAD_DIM = 128
CAP = 32
MESH = pl.DeviceIdType.MESH

PLANES = 2
SIDE = 4
EXPERTS = 8
WIDTH = 5120
CHUNK = WIDTH // EXPERTS
HALF = CAP // 2
PIECE_COLS = WIDTH // 2
UNIT_COLS = WIDTH // 2
GROUP = SIDE * SIDE * HALF
HID = 256


def mod4(v):
    return lax.rem(v + 2 * SIDE, SIDE)


OFFS = (0, -1, 1, 2)
OPPOSITE = ((0, 0), (1, 1), (2, 1), (3, 0))


class Gather:
    def __init__(self, tori, piece, half, ssem, rsem, send, arrived):
        self.tori, self.piece, self.half = tori, piece, half
        self.ssem, self.rsem, self.send, self.arrived = ssem, rsem, send, arrived

    def sems(self, t, n):
        return self.ssem.at[t.h, n], self.rsem.at[t.h, n]

    def second(self, t, i):
        piece = self.piece(t, OFFS[i], 0)
        for s, dq in ((0, 1), (1, -1)):
            self.send(piece, piece, *self.sems(t, 4 + 2 * i + s), t.dev(0, dq))

    def second_arrived(self, t, i, s):
        self.arrived(self.piece(t, OFFS[i], -1 if s == 0 else 1), *self.sems(t, 4 + 2 * i + s))

    def start(self, t):
        piece = self.piece(t, 0, 0)
        for s, dp in ((0, 1), (1, -1)):
            self.send(piece, piece, *self.sems(t, s), t.dev(dp, 0))
        self.second(t, 0)

    def near(self):
        for t in self.tori:
            for s, dp in ((0, -1), (1, 1)):
                self.arrived(self.piece(t, dp, 0), *self.sems(t, s))
                half = self.half(t, dp, 0, s)
                self.send(half, half, *self.sems(t, 2 + s), t.dev(-dp, 0))
        for t in self.tori:
            self.second(t, 1)
            self.second(t, 2)

    def far(self):
        for t in self.tori:
            for s in range(2):
                self.arrived(self.half(t, 2, 0, s), *self.sems(t, 2 + s))
            self.second(t, 3)

    def forward(self, i):
        s = OPPOSITE[i][1]
        dq = 1 if s == 0 else -1
        for t in self.tori:
            self.second_arrived(t, i, s)
            piece = self.piece(t, OFFS[i], -dq)
            self.send(piece, piece, *self.sems(t, 12 + i), t.dev(0, dq))

    def done(self):
        for t in self.tori:
            for i in range(4):
                self.second_arrived(t, i, 1 - OPPOSITE[i][1])
                self.arrived(self.piece(t, OFFS[i], 2), *self.sems(t, 12 + i))


class Torus:
    def __init__(self, h, plane, y, x, e):
        self.h, self.plane, self.y, self.x, self.e = h, plane, y, x, e

    def at(self, dp, dq):
        if self.h == 0:
            return mod4(self.y + dq), mod4(self.x + dp)
        return mod4(self.y + dp), mod4(self.x + dq)

    def rows(self, dp, dq):
        y, x = self.at(dp, dq)
        return pl.ds(pl.multiple_of((y * SIDE + x) * HALF, HALF), HALF)

    def line(self, dq):
        return mod4((self.y if self.h == 0 else self.x) + dq)

    def along(self, dp):
        return mod4((self.x if self.h == 0 else self.y) + dp)

    def dev(self, dp, dq):
        y, x = self.at(dp, dq)
        return (self.plane * SIDE * SIDE + y * SIDE + x, self.e)


def kernel(
    q_hbm,
    k_hbm,
    v_hbm,
    order_hbm,
    routes_hbm,
    gain_hbm,
    router_hbm,
    wg_hbm,
    wu_hbm,
    wd_hbm,
    att_hbm,
    out_hbm,
    q_ref,
    order_ref,
    routes_ref,
    gain_ref,
    router_ref,
    att_ref,
    out_ref,
    hidden_keys,
    kv,
    soft_max,
    soft_sum,
    soft_acc,
    wg,
    wu,
    wd,
    pack,
    xin,
    g,
    part,
    ru1,
    ru2,
    rv1,
    rv2,
    fin,
    ret,
    acc,
    hid,
    in_sem,
    w_sem,
    z_s,
    z_r,
    kv_s,
    kv_r,
    a2a_s,
    a2a_r,
    ag_s,
    ag_r,
    rs_s,
    rs_r,
    back_s,
    back_r,
):
    ctx = lax.axis_index("ctx")
    e = lax.axis_index("exp")
    plane = ctx // (SIDE * SIDE)
    other = 1 - plane
    spot = lax.rem(ctx, SIDE * SIDE)
    y, x = spot // SIDE, lax.rem(spot, SIDE)
    tori = [Torus(h, plane, y, x, e) for h in range(2)]
    planes = (plane, other)
    sent = []

    def send(src, dst, ssem, rsem, dev):
        copy = pltpu.make_async_remote_copy(
            src_ref=src, dst_ref=dst, send_sem=ssem, recv_sem=rsem, device_id=dev, device_id_type=MESH
        )
        copy.start()
        sent.append(copy)

    def arrived(dst, ssem, rsem):
        pltpu.make_async_remote_copy(
            src_ref=dst, dst_ref=dst, send_sem=ssem, recv_sem=rsem, device_id=tori[0].dev(1, 0), device_id_type=MESH
        ).wait_recv()

    def column(pl_index, d):
        return (pl_index * SIDE * SIDE + spot, lax.rem(e + d, EXPERTS))

    barrier = pltpu.get_barrier_semaphore()
    partners = [column(plane, d) for d in range(1, EXPERTS)]
    partners += [column(other, d) for d in range(EXPERTS)]
    partners += [tori[0].dev(k, 0) for k in (1, -1, 2)] + [tori[0].dev(0, k) for k in (1, -1, 2)]
    for dev in partners:
        pl.semaphore_signal(barrier, inc=1, device_id=dev, device_id_type=MESH)

    inputs = [
        pltpu.make_async_copy(src, dst, in_sem.at[i])
        for i, (src, dst) in enumerate(
            (
                (order_hbm, order_ref),
                (routes_hbm, routes_ref),
                (k_hbm, kv.at[0, 0, tori[0].line(0), tori[0].along(0)]),
                (v_hbm, kv.at[0, 1, tori[1].line(0), tori[1].along(0)]),
                (q_hbm, q_ref),
                (gain_hbm, gain_ref),
                (router_hbm, router_ref),
            )
        )
    ]
    for copy in inputs:
        copy.start()
    loads = [
        pltpu.make_async_copy(wg_hbm, wg, w_sem.at[0]),
        pltpu.make_async_copy(wu_hbm, wu, w_sem.at[1]),
    ]
    for f in range(2):
        for m in range(EXPERTS // 2):
            cols = pl.ds(pl.multiple_of((2 * m + lax.rem(e + f, 2)) * CHUNK, CHUNK), CHUNK)
            loads.append(
                pltpu.make_async_copy(
                    wd_hbm.at[:, cols], wd.at[f, :, pl.ds(m * CHUNK, CHUNK)], w_sem.at[2 + f * 4 + m]
                )
            )
    for load in loads:
        load.start()
    inputs[0].wait()
    inputs[1].wait()

    n = n_rows = att_ref.shape[0]
    onehot = (lax.broadcasted_iota(jnp.int32, (EXPERTS, n_rows), 0) == routes_ref[...]).astype(jnp.float32)
    before = (
        lax.broadcasted_iota(jnp.int32, (n_rows, n_rows), 0)
        < lax.broadcasted_iota(jnp.int32, (n_rows, n_rows), 1)
    ).astype(jnp.bfloat16)
    earlier = jnp.dot(onehot.astype(jnp.bfloat16), before, preferred_element_type=jnp.float32)
    code = jnp.sum(onehot * earlier, axis=0, keepdims=True).astype(jnp.int32) + routes_ref[...] * CAP
    placing = (lax.broadcasted_iota(jnp.int32, (EXPERTS * CAP, n_rows), 0) == code).astype(jnp.bfloat16)


    half_n = n // 2

    def positions(c, shape, dim):
        i = lax.broadcasted_iota(jnp.int32, shape, dim)
        return i + jnp.where(i < half_n, order_ref[2 * c] * half_n, (order_ref[2 * c + 1] - 1) * half_n)

    query_pos = positions(ctx, (1, n), 1)
    for w in range(PLANES):

        @pl.loop(0, SIDE * SIDE)
        def _(i):
            kept = positions(planes[w] * SIDE * SIDE + i, (n, 1), 0) <= query_pos
            rows = pl.ds(pl.multiple_of(i * n, n), n)
            hidden_keys[w, rows, :] = jnp.where(kept, 0.0, -1e30).astype(jnp.bfloat16)

    for copy in inputs[2:]:
        copy.wait()
    pl.semaphore_wait(barrier, len(partners))

    for t in tori:
        piece = (t.h, t.line(0), t.along(0))
        send(kv.at[0, *piece], kv.at[1, *piece], z_s.at[t.h], z_r.at[t.h], column(other, 0))

    def kv_near(w):
        for d in (1, -1, 2):
            for t in tori:
                piece = kv.at[w, t.h, t.line(0), t.along(0)]
                send(piece, piece, kv_s.at[w, t.h, d + 1], kv_r.at[w, t.h, d + 1], t.dev(d, 0))

    def kv_far(w):
        for t in tori:
            for d in (1, -1, 2):
                arrived(kv.at[w, t.h, t.line(0), t.along(-d)], kv_s.at[w, t.h, d + 1], kv_r.at[w, t.h, d + 1])
            line = kv.at[w, t.h, t.line(0)]
            for d in (1, -1, 2):
                send(line, line, kv_s.at[w, t.h, d + 5], kv_r.at[w, t.h, d + 5], t.dev(0, d))

    def kv_done(w):
        for t in tori:
            for d in (1, -1, 2):
                arrived(kv.at[w, t.h, t.line(-d)], kv_s.at[w, t.h, d + 5], kv_r.at[w, t.h, d + 5])

    scale = math.log2(math.e) / math.sqrt(HEAD_DIM)
    heads = q_ref.shape[1] // HEAD_DIM
    each = (
        lax.broadcasted_iota(jnp.int32, (n, n), 0) == lax.broadcasted_iota(jnp.int32, (n, n), 1)
    ).astype(jnp.bfloat16)

    def attend(w):
        everyone = SIDE * SIDE * n
        keys = jnp.concatenate([kv[w, 0].reshape(everyone, HEAD_DIM), hidden_keys[w]], axis=1)
        values = jnp.concatenate(
            [kv[w, 1, i, row] for row in range(SIDE) for i in range(SIDE)], axis=0
        )
        for head in range(heads):
            q = jnp.concatenate([q_ref[:, pl.ds(head * HEAD_DIM, HEAD_DIM)], each], axis=1)
            scores = lax.dot_general(q, keys, (((1,), (1,)), ((), ())), preferred_element_type=jnp.float32)
            new = jnp.max(scores, axis=1, keepdims=True)
            if w > 0:
                old = soft_max[head]
                new = jnp.maximum(old, new)
                fade = jnp.exp2((old - new) * scale)
            probs = jnp.exp2(scores * scale - new * scale)
            total = jnp.sum(probs, axis=1, keepdims=True)
            mixed = jnp.dot(probs.astype(jnp.bfloat16), values, preferred_element_type=jnp.float32)
            if w > 0:
                total = total + soft_sum[head] * fade
                mixed = mixed + soft_acc[head] * fade
                att_ref[:, pl.ds(head * HEAD_DIM, HEAD_DIM)] = (mixed / total).astype(jnp.bfloat16)
            else:
                soft_max[head] = new
                soft_sum[head] = total
                soft_acc[head] = mixed

    kv_near(0)
    kv_far(0)
    for t in tori:
        arrived(kv.at[1, t.h, t.line(0), t.along(0)], z_s.at[t.h], z_r.at[t.h])
    kv_near(1)
    kv_far(1)
    kv_done(0)
    attend(0)
    kv_done(1)
    attend(1)
    attended = pltpu.make_async_copy(att_ref, att_hbm, in_sem.at[7])
    attended.start()

    packed = jnp.dot(placing, att_ref[...], preferred_element_type=jnp.float32).astype(jnp.bfloat16)
    pack[...] = packed.reshape(EXPERTS, CAP, CHUNK)

    def dispatch(w, first, count):
        rows = pl.ds(first, count)
        h = first // HALF
        for d in range(1 - w, EXPERTS):
            to = lax.rem(e + d, EXPERTS)
            send(
                pack.at[to, rows], xin.at[w, e, rows], a2a_s.at[w, h, d], a2a_r.at[w, h, d], column(planes[w], d)
            )

    dispatch(0, 0, HALF)
    dispatch(0, HALF, HALF)
    own = pltpu.make_async_copy(pack.at[e], xin.at[0, e], a2a_s.at[0, 0, 0])
    own.start()

    def norm(w, first, count):
        rows = pl.ds(first, count)
        for d in range(1 - w, EXPERTS):
            src = lax.rem(e - d + EXPERTS, EXPERTS)
            h = first // HALF
            arrived(xin.at[w, src, rows], a2a_s.at[w, h, d], a2a_r.at[w, h, d])
        if w == 0 and first == 0:
            own.wait()
        squares = jnp.zeros((count, 1), jnp.float32)
        for j in range(EXPERTS):
            v = xin[w, j, rows].astype(jnp.float32)
            squares += jnp.sum(v * v, axis=1, keepdims=True)
        inverse = lax.rsqrt(squares / WIDTH + 1e-05)
        mine = lax.broadcasted_iota(jnp.int32, (EXPERTS, CHUNK), 0) == e
        logit = jnp.zeros((count, 1), jnp.float32)
        for j in range(EXPERTS):
            cols = pl.ds(j * CHUNK, CHUNK)
            v = xin[w, j, rows].astype(jnp.float32) * inverse * gain_ref[:, cols]
            weight = jnp.sum(jnp.where(mine, router_ref[:, cols], 0.0), axis=0, keepdims=True)
            logit += jnp.sum(v * weight, axis=1, keepdims=True)
        gate = 1.0 / (1.0 + jnp.exp(-logit))
        for j in range(EXPERTS):
            cols = pl.ds(j * CHUNK, CHUNK)
            v = xin[w, j, rows].astype(jnp.float32) * inverse * gain_ref[:, cols]
            v = (v * gate).astype(jnp.bfloat16)
            for k in range(count // HALF):
                g[w, first // HALF + k, tori[0].rows(0, 0), cols] = v[k * HALF : (k + 1) * HALF]

    left_half, right_half = pl.ds(0, UNIT_COLS // 2), pl.ds(UNIT_COLS // 2, UNIT_COLS // 2)
    gather = [
        Gather(
            tori,
            lambda t, dp, dq, w=w: g.at[w, t.h, t.rows(dp, dq)],
            lambda t, dp, dq, s, w=w: g.at[w, t.h, t.rows(dp, dq), pl.ds(s * PIECE_COLS, PIECE_COLS)],
            ag_s.at[w],
            ag_r.at[w],
            send,
            arrived,
        )
        for w in range(PLANES)
    ]

    def ffn(w, h):
        step = 1280
        acc[...] = jnp.zeros_like(acc)

        @pl.loop(0, WIDTH // step)
        def _(k):
            cols = pl.ds(pl.multiple_of(k * step, step), step)
            rows = g[w, h, :, cols]
            acc[0] += jnp.dot(rows, wg[cols, :], preferred_element_type=jnp.float32)
            acc[1] += jnp.dot(rows, wu[cols, :], preferred_element_type=jnp.float32)

        v = acc[0]
        hid[...] = (v / (1.0 + jnp.exp(-v)) * acc[1]).astype(jnp.bfloat16)
        wide = 512

        @pl.loop(0, UNIT_COLS // wide)
        def _(k):
            cols = pl.ds(pl.multiple_of(k * wide, wide), wide)
            for f in range(2):
                part[w, f, h, :, cols] = jnp.dot(
                    hid[...], wd[f, :, cols], preferred_element_type=jnp.float32
                ).astype(jnp.bfloat16)

    def add(ref, *more):
        total = ref[...].astype(jnp.float32)
        for m in more:
            total = total + m[...].astype(jnp.float32)
        ref[...] = total.astype(jnp.bfloat16)

    mine = pltpu.make_async_copy(fin.at[0, 0, e // 2], ret.at[0, e], back_s.at[0, 0])

    def rs_start(u):
        for t in tori:
            for i, s in OPPOSITE:
                send(
                    part.at[*u, t.h, t.rows(OFFS[i], 2)],
                    ru1.at[*u, t.h, i],
                    rs_s.at[*u, t.h, i],
                    rs_r.at[*u, t.h, i],
                    t.dev(0, 1 if s == 0 else -1),
                )

    def rs_second(u, t, i, s):
        n = 4 + 2 * i + s
        dq = 1 if s == 0 else -1
        send(
            part.at[*u, t.h, t.rows(OFFS[i], dq)],
            ru2.at[*u, t.h, i, s],
            rs_s.at[*u, t.h, n],
            rs_r.at[*u, t.h, n],
            t.dev(0, dq),
        )

    def rs_plain(u):
        for t in tori:
            for i, s in OPPOSITE:
                rs_second(u, t, i, 1 - s)

    def rs_joined(u, i):
        s = OPPOSITE[i][1]
        dq = 1 if s == 0 else -1
        for t in tori:
            arrived(ru1.at[*u, t.h, i], rs_s.at[*u, t.h, i], rs_r.at[*u, t.h, i])
            add(part.at[*u, t.h, t.rows(OFFS[i], dq)], ru1.at[*u, t.h, i])
            rs_second(u, t, i, s)

    def rs_sum(u, t, i):
        for s in range(2):
            n = 4 + 2 * i + s
            arrived(ru2.at[*u, t.h, i, s], rs_s.at[*u, t.h, n], rs_r.at[*u, t.h, n])
        add(part.at[*u, t.h, t.rows(OFFS[i], 0)], ru2.at[*u, t.h, i, 0], ru2.at[*u, t.h, i, 1])

    def rs_turn(u):
        for t in tori:
            rs_sum(u, t, 3)
            for s, dp, cols in ((0, 1, left_half), (1, -1, right_half)):
                send(
                    part.at[*u, t.h, t.rows(2, 0), cols],
                    rv1.at[*u, t.h, s],
                    rs_s.at[*u, t.h, 12 + s],
                    rs_r.at[*u, t.h, 12 + s],
                    t.dev(dp, 0),
                )
        for t in tori:
            for i in (1, 2):
                rs_sum(u, t, i)

    def rs_last(u):
        for t in tori:
            for s, dp, cols in ((0, 1, left_half), (1, -1, right_half)):
                arrived(rv1.at[*u, t.h, s], rs_s.at[*u, t.h, 12 + s], rs_r.at[*u, t.h, 12 + s])
                add(part.at[*u, t.h, t.rows(dp, 0), cols], rv1.at[*u, t.h, s])
                send(
                    part.at[*u, t.h, t.rows(dp, 0)],
                    rv2.at[*u, t.h, s],
                    rs_s.at[*u, t.h, 14 + s],
                    rs_r.at[*u, t.h, 14 + s],
                    t.dev(dp, 0),
                )
        for t in tori:
            rs_sum(u, t, 0)

    def rs_finish(u):
        for t in tori:
            for s in range(2):
                arrived(rv2.at[*u, t.h, s], rs_s.at[*u, t.h, 14 + s], rs_r.at[*u, t.h, 14 + s])
            for m in range(EXPERTS // 2):
                cols = pl.ds(m * CHUNK, CHUNK)
                total = part[*u, t.h, t.rows(0, 0), cols].astype(jnp.float32)
                for s in range(2):
                    total = total + rv2[*u, t.h, s, :, cols].astype(jnp.float32)
                fin[*u, m, pl.ds(t.h * HALF, HALF)] = total.astype(jnp.bfloat16)
        w, f = u
        for d in range(f, EXPERTS, 2):
            to = lax.rem(e + d, EXPERTS)
            if w == 0 and d == 0:
                mine.start()
            else:
                send(fin.at[w, f, to // 2], ret.at[w, e], back_s.at[w, d], back_r.at[w, d], column(planes[w], d))

    for t in tori:
        norm(0, t.h * HALF, HALF)
        gather[0].start(t)
    dispatch(1, 0, CAP)
    gather[0].near()
    gather[0].far()
    gather[0].forward(0)
    gather[0].forward(1)
    norm(1, 0, CAP)
    for t in tori:
        gather[1].start(t)
    gather[0].forward(2)
    gather[0].forward(3)
    gather[1].near()
    gather[1].far()
    for load in loads:
        load.wait()
    gather[0].done()
    gather[1].forward(0)
    gather[1].forward(1)
    ffn(0, 0)
    gather[1].forward(2)
    gather[1].forward(3)
    ffn(0, 1)
    a, b, c, d = (0, 0), (1, 0), (1, 1), (0, 1)

    def rs_begin(u):
        rs_start(u)
        rs_plain(u)

    def rs_join(u):
        for i in range(4):
            rs_joined(u, i)

    rs_begin(a)
    rs_begin(d)
    gather[1].done()
    rs_join(a)
    ffn(1, 0)
    ffn(1, 1)
    rs_begin(b)
    rs_turn(a)
    rs_join(b)
    rs_begin(c)
    rs_last(a)
    rs_turn(b)
    rs_finish(a)
    rs_join(c)
    rs_join(d)
    rs_last(b)
    rs_turn(c)
    rs_finish(b)
    rs_turn(d)
    rs_last(c)
    rs_last(d)
    rs_finish(c)
    rs_finish(d)

    routed = None
    for w in range(PLANES):
        for d in range(1 - w, EXPERTS):
            src = lax.rem(e - d + EXPERTS, EXPERTS)
            arrived(ret.at[w, src], back_s.at[w, d], back_r.at[w, d])
        if w == 0:
            mine.wait()
        rows = ret[w].reshape(EXPERTS * CAP, CHUNK)
        term = lax.dot_general(
            placing, rows, (((0,), (0,)), ((), ())), preferred_element_type=jnp.float32
        )
        routed = term if routed is None else routed + term
    out_ref[...] = routed.astype(jnp.bfloat16)
    result = pltpu.make_async_copy(out_ref, out_hbm, in_sem.at[8])
    result.start()
    attended.wait()
    result.wait()
    for copy in sent:
        copy.wait_send()


def per_device(queries, keys, values, block_order, routes, norm_gain, router, w_gate, w_up, w_down):
    anywhere = pl.BlockSpec(memory_space=pl.ANY)
    bf16, f32 = jnp.bfloat16, jnp.float32
    dma = pltpu.SemaphoreType.DMA
    here, features = queries.shape
    heads = features // HEAD_DIM
    return pl.pallas_call(
        kernel,
        out_shape=(jax.ShapeDtypeStruct(queries.shape, bf16),) * 2,
        in_specs=[anywhere] * 10,
        out_specs=(anywhere, anywhere),
        scratch_shapes=[
            pltpu.VMEM((here, features), bf16),
            pltpu.SMEM(block_order.shape, jnp.int32),
            pltpu.VMEM((1, here), jnp.int32),
            pltpu.VMEM((1, WIDTH), f32),
            pltpu.VMEM((EXPERTS, WIDTH), f32),
            pltpu.VMEM((here, features), bf16),
            pltpu.VMEM((here, features), bf16),
            pltpu.VMEM((PLANES, SIDE * SIDE * here, here), bf16),
            pltpu.VMEM((PLANES, 2, SIDE, SIDE, here, HEAD_DIM), bf16),
            pltpu.VMEM((heads, here, 1), f32),
            pltpu.VMEM((heads, here, 1), f32),
            pltpu.VMEM((heads, here, HEAD_DIM), f32),
            pltpu.VMEM((WIDTH, HID), bf16),
            pltpu.VMEM((WIDTH, HID), bf16),
            pltpu.VMEM((2, HID, UNIT_COLS), bf16),
            pltpu.VMEM((EXPERTS, CAP, CHUNK), bf16),
            pltpu.VMEM((PLANES, EXPERTS, CAP, CHUNK), bf16),
            pltpu.VMEM((PLANES, 2, GROUP, WIDTH), bf16),
            pltpu.VMEM((PLANES, 2, 2, GROUP, UNIT_COLS), bf16),
            pltpu.VMEM((PLANES, 2, 2, 4, HALF, UNIT_COLS), bf16),
            pltpu.VMEM((PLANES, 2, 2, 4, 2, HALF, UNIT_COLS), bf16),
            pltpu.VMEM((PLANES, 2, 2, 2, HALF, UNIT_COLS // 2), bf16),
            pltpu.VMEM((PLANES, 2, 2, 2, HALF, UNIT_COLS), bf16),
            pltpu.VMEM((PLANES, 2, EXPERTS // 2, CAP, CHUNK), bf16),
            pltpu.VMEM((PLANES, EXPERTS, CAP, CHUNK), bf16),
            pltpu.VMEM((2, GROUP, HID), f32),
            pltpu.VMEM((GROUP, HID), bf16),
            dma((9,)),
            dma((10,)),
            dma((2,)),
            dma((2,)),
            dma((PLANES, 2, 8)),
            dma((PLANES, 2, 8)),
            dma((PLANES, 2, EXPERTS)),
            dma((PLANES, 2, EXPERTS)),
            dma((PLANES, 2, 16)),
            dma((PLANES, 2, 16)),
            dma((PLANES, 2, 2, 16)),
            dma((PLANES, 2, 2, 16)),
            dma((PLANES, EXPERTS)),
            dma((PLANES, EXPERTS)),
        ],
        compiler_params=pltpu.CompilerParams(
            collective_id=1, has_side_effects=True, vmem_limit_bytes=62 << 20
        ),
        name="layer",
    )(
        queries,
        keys,
        values,
        block_order,
        routes.reshape(1, -1),
        norm_gain.reshape(1, -1),
        router.T,
        w_gate[0],
        w_up[0],
        w_down[0],
    )


def solution(mesh):
    in_specs = (
        P("ctx", "exp"),
        P("ctx", "exp"),
        P("ctx", "exp"),
        P(),
        P("ctx", None),
        P(),
        P(),
        P("exp", None, "ctx"),
        P("exp", None, "ctx"),
        P("exp", "ctx", None),
    )
    out_specs = (P("ctx", "exp"), P("ctx", "exp"))
    return jax.shard_map(
        per_device, mesh=mesh, in_specs=in_specs, out_specs=out_specs, check_vma=False
    )
```

```python
import functools
import math

import jax
import jax.numpy as jnp
from jax import lax
from jax.experimental import pallas as pl
from jax.experimental.pallas import tpu as pltpu
from jax.sharding import PartitionSpec as P

HEAD_DIM = 128
CAP = 32
MESH = pl.DeviceIdType.MESH

PLANES = 2
SIDE = 4
EXPERTS = 8
WIDTH = 5120
CHUNK = WIDTH // EXPERTS
HALF = CAP // 2
PIECE_COLS = WIDTH // 2
UNIT_COLS = WIDTH // 2
GROUP = SIDE * SIDE * HALF
HID = 256


def mod4(v):
    return lax.rem(v + 2 * SIDE, SIDE)


OFFS = (0, -1, 1, 2)
OPPOSITE = ((0, 0), (1, 1), (2, 1), (3, 0))


class Gather:
    def __init__(self, tori, piece, half, rows, ssem, rsem, send, arrived):
        self.tori, self.piece, self.half, self.rows = tori, piece, half, rows
        self.ssem, self.rsem, self.send, self.arrived = ssem, rsem, send, arrived

    def second(self, t, i):
        piece = self.piece(t, OFFS[i], 0)
        for s, dq in ((0, 1), (1, -1)):
            r = 4 + i if s == OPPOSITE[i][1] else 8
            self.send(piece, piece, self.ssem.at[2], self.rsem.at[r], t.dev(0, dq))

    def start(self, t):
        piece = self.piece(t, 0, 0)
        for dp in (1, -1):
            self.send(piece, piece, self.ssem.at[0], self.rsem.at[t.h], t.dev(dp, 0))
        self.second(t, 0)

    def near(self):
        for t in self.tori:
            self.arrived(self.rows(2), self.rsem.at[t.h])
            for s, dp in ((0, -1), (1, 1)):
                half = self.half(t, dp, 0, s)
                self.send(half, half, self.ssem.at[1], self.rsem.at[2 + t.h], t.dev(-dp, 0))
        for t in self.tori:
            self.second(t, 1)
            self.second(t, 2)

    def far(self):
        for t in self.tori:
            self.arrived(self.rows(1), self.rsem.at[2 + t.h])
            self.second(t, 3)

    def forward(self, i):
        dq = 1 if OPPOSITE[i][1] == 0 else -1
        self.arrived(self.rows(2), self.rsem.at[4 + i])
        for t in self.tori:
            piece = self.piece(t, OFFS[i], -dq)
            self.send(piece, piece, self.ssem.at[3], self.rsem.at[8], t.dev(0, dq))

    def done(self):
        self.arrived(self.rows(16), self.rsem.at[8])


class Torus:
    def __init__(self, h, plane, y, x, e):
        self.h, self.plane, self.y, self.x, self.e = h, plane, y, x, e

    def at(self, dp, dq):
        if self.h == 0:
            return mod4(self.y + dq), mod4(self.x + dp)
        return mod4(self.y + dp), mod4(self.x + dq)

    def rows(self, dp, dq):
        y, x = self.at(dp, dq)
        return pl.ds(pl.multiple_of((y * SIDE + x) * HALF, HALF), HALF)

    def line(self, dq):
        return mod4((self.y if self.h == 0 else self.x) + dq)

    def along(self, dp):
        return mod4((self.x if self.h == 0 else self.y) + dp)

    def dev(self, dp, dq):
        y, x = self.at(dp, dq)
        return (self.plane * SIDE * SIDE + y * SIDE + x, self.e)


def kernel(
    q_hbm,
    k_hbm,
    v_hbm,
    order_hbm,
    routes_hbm,
    gain_hbm,
    router_hbm,
    wg_hbm,
    wu_hbm,
    wd_hbm,
    att_hbm,
    out_hbm,
    q_ref,
    order_ref,
    routes_ref,
    gain_ref,
    router_ref,
    att_ref,
    out_ref,
    hidden_keys,
    kv,
    soft_max,
    soft_sum,
    soft_acc,
    wg,
    wu,
    wd,
    pack,
    xin,
    g,
    part,
    ru1,
    ru2,
    rv1,
    rv2,
    fin,
    ret,
    acc,
    hid,
    in_sem,
    w_sem,
    kv_s,
    kv_r,
    a2a_s,
    a2a_r,
    ag_s,
    ag_r,
    rs_s,
    rs_r,
    back_s,
    back_r,
):
    ctx = lax.axis_index("ctx")
    e = lax.axis_index("exp")
    plane = ctx // (SIDE * SIDE)
    other = 1 - plane
    spot = lax.rem(ctx, SIDE * SIDE)
    y, x = spot // SIDE, lax.rem(spot, SIDE)
    tori = [Torus(h, plane, y, x, e) for h in range(2)]
    planes = (plane, other)

    def send(src, dst, ssem, rsem, dev):
        copy = pltpu.make_async_remote_copy(
            src_ref=src, dst_ref=dst, send_sem=ssem, recv_sem=rsem, device_id=dev, device_id_type=MESH
        )
        copy.start()

    def arrived(ref, rsem):
        pltpu.make_async_remote_copy(
            src_ref=ref, dst_ref=ref, send_sem=rsem, recv_sem=rsem, device_id=tori[0].dev(1, 0), device_id_type=MESH
        ).wait_recv()

    def all_sent(ref, ssem):
        pltpu.make_async_remote_copy(
            src_ref=ref, dst_ref=ref, send_sem=ssem, recv_sem=ssem, device_id=tori[0].dev(1, 0), device_id_type=MESH
        ).wait_send()

    def column(pl_index, d):
        return (pl_index * SIDE * SIDE + spot, lax.rem(e + d, EXPERTS))

    barrier = pltpu.get_barrier_semaphore()
    partners = [column(plane, d) for d in range(1, EXPERTS)]
    partners += [column(other, d) for d in range(EXPERTS)]
    partners += [tori[0].dev(k, 0) for k in (1, -1, 2)] + [tori[0].dev(0, k) for k in (1, -1, 2)]
    for dev in partners:
        pl.semaphore_signal(barrier, inc=1, device_id=dev, device_id_type=MESH)

    inputs = [
        pltpu.make_async_copy(src, dst, in_sem.at[i])
        for i, (src, dst) in enumerate(
            (
                (order_hbm, order_ref),
                (routes_hbm, routes_ref),
                (k_hbm, kv.at[0, 0, tori[0].line(0), tori[0].along(0)]),
                (v_hbm, kv.at[0, 1, tori[1].line(0), tori[1].along(0)]),
                (q_hbm, q_ref),
                (gain_hbm, gain_ref),
                (router_hbm, router_ref),
            )
        )
    ]
    for copy in inputs:
        copy.start()
    loads = [
        pltpu.make_async_copy(wg_hbm, wg, w_sem.at[0]),
        pltpu.make_async_copy(wu_hbm, wu, w_sem.at[1]),
    ]
    for f in range(2):
        for m in range(EXPERTS // 2):
            cols = pl.ds(pl.multiple_of((2 * m + lax.rem(e + f, 2)) * CHUNK, CHUNK), CHUNK)
            loads.append(
                pltpu.make_async_copy(
                    wd_hbm.at[:, cols], wd.at[f, :, pl.ds(m * CHUNK, CHUNK)], w_sem.at[2]
                )
            )
    for load in loads:
        load.start()
    inputs[0].wait()
    inputs[1].wait()

    n = n_rows = att_ref.shape[0]
    onehot = (lax.broadcasted_iota(jnp.int32, (EXPERTS, n_rows), 0) == routes_ref[...]).astype(jnp.float32)
    before = (
        lax.broadcasted_iota(jnp.int32, (n_rows, n_rows), 0)
        < lax.broadcasted_iota(jnp.int32, (n_rows, n_rows), 1)
    ).astype(jnp.bfloat16)
    earlier = jnp.dot(onehot.astype(jnp.bfloat16), before, preferred_element_type=jnp.float32)
    code = jnp.sum(onehot * earlier, axis=0, keepdims=True).astype(jnp.int32) + routes_ref[...] * CAP
    placing = (lax.broadcasted_iota(jnp.int32, (EXPERTS * CAP, n_rows), 0) == code).astype(jnp.bfloat16)


    half_n = n // 2

    def positions(c, shape, dim):
        i = lax.broadcasted_iota(jnp.int32, shape, dim)
        return i + jnp.where(i < half_n, order_ref[2 * c] * half_n, (order_ref[2 * c + 1] - 1) * half_n)

    query_pos = positions(ctx, (1, n), 1)
    for w in range(PLANES):

        @pl.loop(0, SIDE * SIDE)
        def _(i):
            kept = positions(planes[w] * SIDE * SIDE + i, (n, 1), 0) <= query_pos
            rows = pl.ds(pl.multiple_of(i * n, n), n)
            hidden_keys[w, rows, :] = jnp.where(kept, 0.0, -1e30).astype(jnp.bfloat16)

    for copy in inputs[2:]:
        copy.wait()
    pl.semaphore_wait(barrier, len(partners))

    for t in tori:
        piece = (t.h, t.line(0), t.along(0))
        send(kv.at[0, *piece], kv.at[1, *piece], kv_s.at[0], kv_r.at[8], column(other, 0))

    def kv_near(w):
        for d in (1, -1, 2):
            for t in tori:
                piece = kv.at[w, t.h, t.line(0), t.along(0)]
                send(piece, piece, kv_s.at[1], kv_r.at[4 * w + t.h], t.dev(d, 0))

    def kv_far(w):
        for t in tori:
            arrived(kv.at[w, t.h, 0, pl.ds(0, SIDE - 1)], kv_r.at[4 * w + t.h])
            line = kv.at[w, t.h, t.line(0)]
            for d in (1, -1, 2):
                send(line, line, kv_s.at[2], kv_r.at[4 * w + 2 + t.h], t.dev(0, d))

    def kv_done(w):
        for t in tori:
            arrived(kv.at[w, t.h, pl.ds(0, SIDE - 1)], kv_r.at[4 * w + 2 + t.h])

    scale = math.log2(math.e) / math.sqrt(HEAD_DIM)
    heads = q_ref.shape[1] // HEAD_DIM
    each = (
        lax.broadcasted_iota(jnp.int32, (n, n), 0) == lax.broadcasted_iota(jnp.int32, (n, n), 1)
    ).astype(jnp.bfloat16)

    def attend(w):
        everyone = SIDE * SIDE * n
        keys = jnp.concatenate([kv[w, 0].reshape(everyone, HEAD_DIM), hidden_keys[w]], axis=1)
        values = jnp.concatenate(
            [kv[w, 1, i, row] for row in range(SIDE) for i in range(SIDE)], axis=0
        )
        for head in range(heads):
            q = jnp.concatenate([q_ref[:, pl.ds(head * HEAD_DIM, HEAD_DIM)], each], axis=1)
            scores = lax.dot_general(q, keys, (((1,), (1,)), ((), ())), preferred_element_type=jnp.float32)
            new = jnp.max(scores, axis=1, keepdims=True)
            if w > 0:
                old = soft_max[head]
                new = jnp.maximum(old, new)
                fade = jnp.exp2((old - new) * scale)
            probs = jnp.exp2(scores * scale - new * scale)
            total = jnp.sum(probs, axis=1, keepdims=True)
            mixed = jnp.dot(probs.astype(jnp.bfloat16), values, preferred_element_type=jnp.float32)
            if w > 0:
                total = total + soft_sum[head] * fade
                mixed = mixed + soft_acc[head] * fade
                att_ref[:, pl.ds(head * HEAD_DIM, HEAD_DIM)] = (mixed / total).astype(jnp.bfloat16)
            else:
                soft_max[head] = new
                soft_sum[head] = total
                soft_acc[head] = mixed

    kv_near(0)
    kv_far(0)
    arrived(kv.at[1, 0, 0, pl.ds(0, 2)], kv_r.at[8])
    kv_near(1)
    kv_far(1)
    kv_done(0)
    attend(0)
    kv_done(1)
    attend(1)
    attended = pltpu.make_async_copy(att_ref, att_hbm, in_sem.at[7])
    attended.start()

    packed = jnp.dot(placing, att_ref[...], preferred_element_type=jnp.float32).astype(jnp.bfloat16)
    pack[...] = packed.reshape(EXPERTS, CAP, CHUNK)

    def dispatch(w, first, count):
        rows = pl.ds(first, count)
        h = first // HALF
        for d in range(1 - w, EXPERTS):
            to = lax.rem(e + d, EXPERTS)
            send(
                pack.at[to, rows], xin.at[w, e, rows], a2a_s.at[w], a2a_r.at[2 * w + h], column(planes[w], d)
            )

    dispatch(0, 0, HALF)
    dispatch(0, HALF, HALF)
    own = pltpu.make_async_copy(pack.at[e], xin.at[0, e], in_sem.at[9])
    own.start()

    def norm(w, first, count):
        rows = pl.ds(first, count)
        arrived(xin.at[w, pl.ds(0, EXPERTS - 1 + w), rows], a2a_r.at[2 * w + first // HALF])
        if w == 0 and first == 0:
            own.wait()
        squares = jnp.zeros((count, 1), jnp.float32)
        for j in range(EXPERTS):
            v = xin[w, j, rows].astype(jnp.float32)
            squares += jnp.sum(v * v, axis=1, keepdims=True)
        inverse = lax.rsqrt(squares / WIDTH + 1e-05)
        mine = lax.broadcasted_iota(jnp.int32, (EXPERTS, CHUNK), 0) == e
        logit = jnp.zeros((count, 1), jnp.float32)
        for j in range(EXPERTS):
            cols = pl.ds(j * CHUNK, CHUNK)
            v = xin[w, j, rows].astype(jnp.float32) * inverse * gain_ref[:, cols]
            weight = jnp.sum(jnp.where(mine, router_ref[:, cols], 0.0), axis=0, keepdims=True)
            logit += jnp.sum(v * weight, axis=1, keepdims=True)
        gate = 1.0 / (1.0 + jnp.exp(-logit))
        for j in range(EXPERTS):
            cols = pl.ds(j * CHUNK, CHUNK)
            v = xin[w, j, rows].astype(jnp.float32) * inverse * gain_ref[:, cols]
            v = (v * gate).astype(jnp.bfloat16)
            for k in range(count // HALF):
                g[w, first // HALF + k, tori[0].rows(0, 0), cols] = v[k * HALF : (k + 1) * HALF]

    left_half, right_half = pl.ds(0, UNIT_COLS // 2), pl.ds(UNIT_COLS // 2, UNIT_COLS // 2)
    gather = [
        Gather(
            tori,
            lambda t, dp, dq, w=w: g.at[w, t.h, t.rows(dp, dq)],
            lambda t, dp, dq, s, w=w: g.at[w, t.h, t.rows(dp, dq), pl.ds(s * PIECE_COLS, PIECE_COLS)],
            lambda k, w=w: g.at[w, 0, pl.ds(0, k * HALF)],
            ag_s,
            ag_r.at[w],
            send,
            arrived,
        )
        for w in range(PLANES)
    ]

    def ffn(w, h):
        step = 1280
        acc[...] = jnp.zeros_like(acc)

        @pl.loop(0, WIDTH // step)
        def _(k):
            cols = pl.ds(pl.multiple_of(k * step, step), step)
            rows = g[w, h, :, cols]
            acc[0] += jnp.dot(rows, wg[cols, :], preferred_element_type=jnp.float32)
            acc[1] += jnp.dot(rows, wu[cols, :], preferred_element_type=jnp.float32)

        v = acc[0]
        hid[...] = (v / (1.0 + jnp.exp(-v)) * acc[1]).astype(jnp.bfloat16)
        wide = 512

        @pl.loop(0, UNIT_COLS // wide)
        def _(k):
            cols = pl.ds(pl.multiple_of(k * wide, wide), wide)
            for f in range(2):
                part[w, f, h, :, cols] = jnp.dot(
                    hid[...], wd[f, :, cols], preferred_element_type=jnp.float32
                ).astype(jnp.bfloat16)

    def add(ref, *more):
        total = ref[...].astype(jnp.float32)
        for m in more:
            total = total + m[...].astype(jnp.float32)
        ref[...] = total.astype(jnp.bfloat16)

    mine = pltpu.make_async_copy(fin.at[0, 0, e // 2], ret.at[0, e], in_sem.at[10])

    def rs_start(u):
        for t in tori:
            for i, s in OPPOSITE:
                send(
                    part.at[*u, t.h, t.rows(OFFS[i], 2)],
                    ru1.at[*u, i, t.h],
                    rs_s.at[0],
                    rs_r.at[*u, i],
                    t.dev(0, 1 if s == 0 else -1),
                )

    def rs_second(u, t, i, s):
        dq = 1 if s == 0 else -1
        send(
            part.at[*u, t.h, t.rows(OFFS[i], dq)],
            ru2.at[*u, i, s, t.h],
            rs_s.at[1],
            rs_r.at[*u, 4 + i],
            t.dev(0, dq),
        )

    def rs_plain(u):
        for t in tori:
            for i, s in OPPOSITE:
                rs_second(u, t, i, 1 - s)

    def rs_joined(u, i):
        s = OPPOSITE[i][1]
        dq = 1 if s == 0 else -1
        arrived(ru1.at[*u, i], rs_r.at[*u, i])
        for t in tori:
            add(part.at[*u, t.h, t.rows(OFFS[i], dq)], ru1.at[*u, i, t.h])
            rs_second(u, t, i, s)

    def rs_sum(u, i):
        arrived(ru2.at[*u, i], rs_r.at[*u, 4 + i])
        for t in tori:
            add(part.at[*u, t.h, t.rows(OFFS[i], 0)], ru2.at[*u, i, 0, t.h], ru2.at[*u, i, 1, t.h])

    SIDES = ((0, 1, left_half), (1, -1, right_half))

    def rs_turn(u):
        rs_sum(u, 3)
        for t in tori:
            for s, dp, cols in SIDES:
                send(part.at[*u, t.h, t.rows(2, 0), cols], rv1.at[*u, t.h, s], rs_s.at[2], rs_r.at[*u, 8], t.dev(dp, 0))
        rs_sum(u, 1)
        rs_sum(u, 2)

    def rs_last(u):
        arrived(rv1.at[*u], rs_r.at[*u, 8])
        for t in tori:
            for s, dp, cols in SIDES:
                add(part.at[*u, t.h, t.rows(dp, 0), cols], rv1.at[*u, t.h, s])
                send(part.at[*u, t.h, t.rows(dp, 0)], rv2.at[*u, t.h, s], rs_s.at[3], rs_r.at[*u, 9], t.dev(dp, 0))
        rs_sum(u, 0)

    def rs_finish(u):
        arrived(rv2.at[*u], rs_r.at[*u, 9])
        for t in tori:
            for m in range(EXPERTS // 2):
                cols = pl.ds(m * CHUNK, CHUNK)
                total = part[*u, t.h, t.rows(0, 0), cols].astype(jnp.float32)
                for s in range(2):
                    total = total + rv2[*u, t.h, s, :, cols].astype(jnp.float32)
                fin[*u, m, pl.ds(t.h * HALF, HALF)] = total.astype(jnp.bfloat16)
        w, f = u
        for d in range(f, EXPERTS, 2):
            to = lax.rem(e + d, EXPERTS)
            if w == 0 and d == 0:
                mine.start()
            else:
                send(fin.at[w, f, to // 2], ret.at[w, e], back_s.at[w], back_r.at[w], column(planes[w], d))

    for t in tori:
        norm(0, t.h * HALF, HALF)
        gather[0].start(t)
    dispatch(1, 0, CAP)
    gather[0].near()
    gather[0].far()
    gather[0].forward(0)
    gather[0].forward(1)
    norm(1, 0, CAP)
    for t in tori:
        gather[1].start(t)
    gather[0].forward(2)
    gather[0].forward(3)
    gather[1].near()
    gather[1].far()
    loads[0].wait()
    loads[1].wait()
    pltpu.make_async_copy(wd, wd, w_sem.at[2]).wait()
    gather[0].done()
    gather[1].forward(0)
    gather[1].forward(1)
    ffn(0, 0)
    gather[1].forward(2)
    gather[1].forward(3)
    ffn(0, 1)
    a, b, c, d = (0, 0), (1, 0), (1, 1), (0, 1)

    def rs_begin(u):
        rs_start(u)
        rs_plain(u)

    def rs_join(u):
        for i in range(4):
            rs_joined(u, i)

    rs_begin(a)
    rs_begin(d)
    gather[1].done()
    rs_join(a)
    ffn(1, 0)
    ffn(1, 1)
    rs_begin(b)
    rs_turn(a)
    rs_join(b)
    rs_begin(c)
    rs_last(a)
    rs_turn(b)
    rs_finish(a)
    rs_join(c)
    rs_join(d)
    rs_last(b)
    rs_turn(c)
    rs_finish(b)
    rs_turn(d)
    rs_last(c)
    rs_last(d)
    rs_finish(c)
    rs_finish(d)

    routed = None
    for w in range(PLANES):
        arrived(ret.at[w, pl.ds(0, EXPERTS - 1 + w)], back_r.at[w])
        if w == 0:
            mine.wait()
        rows = ret[w].reshape(EXPERTS * CAP, CHUNK)
        term = lax.dot_general(
            placing, rows, (((0,), (0,)), ((), ())), preferred_element_type=jnp.float32
        )
        routed = term if routed is None else routed + term
    out_ref[...] = routed.astype(jnp.bfloat16)
    result = pltpu.make_async_copy(out_ref, out_hbm, in_sem.at[8])
    result.start()
    attended.wait()
    result.wait()
    all_sent(kv.at[0, 0, 0, pl.ds(0, 2)], kv_s.at[0])
    all_sent(kv.at[0, 0, pl.ds(0, SIDE - 1)], kv_s.at[1])
    all_sent(kv.at[:, :, pl.ds(0, SIDE - 1)], kv_s.at[2])
    all_sent(xin.at[0, pl.ds(0, EXPERTS - 1)], a2a_s.at[0])
    all_sent(xin.at[1], a2a_s.at[1])
    all_sent(g.at[0, 0, pl.ds(0, 8 * HALF)], ag_s.at[0])
    all_sent(g.at[0, 0, pl.ds(0, 4 * HALF)], ag_s.at[1])
    all_sent(g.at[0], ag_s.at[2])
    all_sent(g.at[0, 0], ag_s.at[3])
    for i, ref in enumerate((ru1, ru2, rv1, rv2)):
        all_sent(ref, rs_s.at[i])
    all_sent(ret.at[0, pl.ds(0, EXPERTS - 1)], back_s.at[0])
    all_sent(ret.at[1], back_s.at[1])


def per_device(queries, keys, values, block_order, routes, norm_gain, router, w_gate, w_up, w_down):
    anywhere = pl.BlockSpec(memory_space=pl.ANY)
    bf16, f32 = jnp.bfloat16, jnp.float32
    dma = pltpu.SemaphoreType.DMA
    here, features = queries.shape
    heads = features // HEAD_DIM
    return pl.pallas_call(
        kernel,
        out_shape=(jax.ShapeDtypeStruct(queries.shape, bf16),) * 2,
        in_specs=[anywhere] * 10,
        out_specs=(anywhere, anywhere),
        scratch_shapes=[
            pltpu.VMEM((here, features), bf16),
            pltpu.SMEM(block_order.shape, jnp.int32),
            pltpu.VMEM((1, here), jnp.int32),
            pltpu.VMEM((1, WIDTH), f32),
            pltpu.VMEM((EXPERTS, WIDTH), f32),
            pltpu.VMEM((here, features), bf16),
            pltpu.VMEM((here, features), bf16),
            pltpu.VMEM((PLANES, SIDE * SIDE * here, here), bf16),
            pltpu.VMEM((PLANES, 2, SIDE, SIDE, here, HEAD_DIM), bf16),
            pltpu.VMEM((heads, here, 1), f32),
            pltpu.VMEM((heads, here, 1), f32),
            pltpu.VMEM((heads, here, HEAD_DIM), f32),
            pltpu.VMEM((WIDTH, HID), bf16),
            pltpu.VMEM((WIDTH, HID), bf16),
            pltpu.VMEM((2, HID, UNIT_COLS), bf16),
            pltpu.VMEM((EXPERTS, CAP, CHUNK), bf16),
            pltpu.VMEM((PLANES, EXPERTS, CAP, CHUNK), bf16),
            pltpu.VMEM((PLANES, 2, GROUP, WIDTH), bf16),
            pltpu.VMEM((PLANES, 2, 2, GROUP, UNIT_COLS), bf16),
            pltpu.VMEM((PLANES, 2, 4, 2, HALF, UNIT_COLS), bf16),
            pltpu.VMEM((PLANES, 2, 4, 2, 2, HALF, UNIT_COLS), bf16),
            pltpu.VMEM((PLANES, 2, 2, 2, HALF, UNIT_COLS // 2), bf16),
            pltpu.VMEM((PLANES, 2, 2, 2, HALF, UNIT_COLS), bf16),
            pltpu.VMEM((PLANES, 2, EXPERTS // 2, CAP, CHUNK), bf16),
            pltpu.VMEM((PLANES, EXPERTS, CAP, CHUNK), bf16),
            pltpu.VMEM((2, GROUP, HID), f32),
            pltpu.VMEM((GROUP, HID), bf16),
            dma((11,)),
            dma((3,)),
            dma((3,)),
            dma((9,)),
            dma((2,)),
            dma((3,)),
            dma((4,)),
            dma((PLANES, 9)),
            dma((4,)),
            dma((PLANES, 2, 10)),
            dma((2,)),
            dma((2,)),
        ],
        compiler_params=pltpu.CompilerParams(
            collective_id=1, has_side_effects=True, vmem_limit_bytes=62 << 20
        ),
        name="layer",
    )(
        queries,
        keys,
        values,
        block_order,
        routes.reshape(1, -1),
        norm_gain.reshape(1, -1),
        router.T,
        w_gate[0],
        w_up[0],
        w_down[0],
    )


def solution(mesh):
    in_specs = (
        P("ctx", "exp"),
        P("ctx", "exp"),
        P("ctx", "exp"),
        P(),
        P("ctx", None),
        P(),
        P(),
        P("exp", None, "ctx"),
        P("exp", None, "ctx"),
        P("exp", "ctx", None),
    )
    out_specs = (P("ctx", "exp"), P("ctx", "exp"))
    return jax.shard_map(
        per_device, mesh=mesh, in_specs=in_specs, out_specs=out_specs, check_vma=False
    )
```

```python
import functools
import math

import jax
import jax.numpy as jnp
from jax import lax
from jax.experimental import pallas as pl
from jax.experimental.pallas import tpu as pltpu
from jax.sharding import PartitionSpec as P

HEAD_DIM = 128
CAP = 32
MESH = pl.DeviceIdType.MESH

PLANES = 2
SIDE = 4
EXPERTS = 8
WIDTH = 5120
CHUNK = WIDTH // EXPERTS
HALF = CAP // 2
PIECE_COLS = WIDTH // 2
UNIT_COLS = WIDTH // 2
GROUP = SIDE * SIDE * HALF
HID = 256


def mod4(v):
    return lax.rem(v + 2 * SIDE, SIDE)


OFFS = (0, -1, 1, 2)
OPPOSITE = ((0, 0), (1, 1), (2, 1), (3, 0))


class Gather:
    def __init__(self, tori, piece, half, rows, ssem, rsem, send, arrived):
        self.tori, self.piece, self.half, self.rows = tori, piece, half, rows
        self.ssem, self.rsem, self.send, self.arrived = ssem, rsem, send, arrived

    def second(self, t, i):
        piece = self.piece(t, OFFS[i], 0)
        for s, dq in ((0, 1), (1, -1)):
            r = 4 + i if s == OPPOSITE[i][1] else 8
            self.send(piece, piece, self.ssem.at[2], self.rsem.at[r], t.dev(0, dq))

    def start(self, t):
        piece = self.piece(t, 0, 0)
        for dp in (1, -1):
            self.send(piece, piece, self.ssem.at[0], self.rsem.at[t.h], t.dev(dp, 0))
        self.second(t, 0)

    def near(self):
        for t in self.tori:
            self.arrived(self.rows(2), self.rsem.at[t.h])
            for s, dp in ((0, -1), (1, 1)):
                half = self.half(t, dp, 0, s)
                self.send(half, half, self.ssem.at[1], self.rsem.at[2 + t.h], t.dev(-dp, 0))
        for t in self.tori:
            self.second(t, 1)
            self.second(t, 2)

    def far(self):
        for t in self.tori:
            self.arrived(self.rows(1), self.rsem.at[2 + t.h])
            self.second(t, 3)

    def forward(self, i):
        dq = 1 if OPPOSITE[i][1] == 0 else -1
        self.arrived(self.rows(2), self.rsem.at[4 + i])
        for t in self.tori:
            piece = self.piece(t, OFFS[i], -dq)
            self.send(piece, piece, self.ssem.at[3], self.rsem.at[8], t.dev(0, dq))

    def done(self):
        self.arrived(self.rows(16), self.rsem.at[8])


class Torus:
    def __init__(self, h, plane, y, x, e):
        self.h, self.plane, self.y, self.x, self.e = h, plane, y, x, e

    def at(self, dp, dq):
        if self.h == 0:
            return mod4(self.y + dq), mod4(self.x + dp)
        return mod4(self.y + dp), mod4(self.x + dq)

    def rows(self, dp, dq):
        y, x = self.at(dp, dq)
        return pl.ds(pl.multiple_of((y * SIDE + x) * HALF, HALF), HALF)

    def line(self, dq):
        return mod4((self.y if self.h == 0 else self.x) + dq)

    def along(self, dp):
        return mod4((self.x if self.h == 0 else self.y) + dp)

    def dev(self, dp, dq):
        y, x = self.at(dp, dq)
        return (self.plane * SIDE * SIDE + y * SIDE + x, self.e)


def kernel(
    q_hbm,
    k_hbm,
    v_hbm,
    order_hbm,
    routes_hbm,
    gain_hbm,
    router_hbm,
    wg_hbm,
    wu_hbm,
    wd_hbm,
    both_hbm,
    q_ref,
    order_ref,
    routes_ref,
    gain_ref,
    router_ref,
    att_ref,
    out_ref,
    hidden_keys,
    kv,
    soft_max,
    soft_sum,
    soft_acc,
    wg,
    wu,
    wd,
    pack,
    xin,
    g,
    part,
    ru1,
    ru2,
    rv1,
    rv2,
    fin,
    ret,
    acc,
    hid,
    in_sem,
    w_sem,
    kv_s,
    kv_r,
    a2a_s,
    a2a_r,
    ag_s,
    ag_r,
    rs_s,
    rs_r,
    back_s,
    back_r,
):
    ctx = lax.axis_index("ctx")
    e = lax.axis_index("exp")
    plane = ctx // (SIDE * SIDE)
    other = 1 - plane
    spot = lax.rem(ctx, SIDE * SIDE)
    y, x = spot // SIDE, lax.rem(spot, SIDE)
    tori = [Torus(h, plane, y, x, e) for h in range(2)]
    planes = (plane, other)

    def send(src, dst, ssem, rsem, dev):
        copy = pltpu.make_async_remote_copy(
            src_ref=src, dst_ref=dst, send_sem=ssem, recv_sem=rsem, device_id=dev, device_id_type=MESH
        )
        copy.start()

    def arrived(ref, rsem):
        pltpu.make_async_remote_copy(
            src_ref=ref, dst_ref=ref, send_sem=rsem, recv_sem=rsem, device_id=tori[0].dev(1, 0), device_id_type=MESH
        ).wait_recv()

    def all_sent(ref, ssem):
        pltpu.make_async_remote_copy(
            src_ref=ref, dst_ref=ref, send_sem=ssem, recv_sem=ssem, device_id=tori[0].dev(1, 0), device_id_type=MESH
        ).wait_send()

    def column(pl_index, d):
        return (pl_index * SIDE * SIDE + spot, lax.rem(e + d, EXPERTS))

    barrier = pltpu.get_barrier_semaphore()
    partners = [column(plane, d) for d in range(1, EXPERTS)]
    partners += [column(other, d) for d in range(EXPERTS)]
    partners += [tori[0].dev(k, 0) for k in (1, -1, 2)] + [tori[0].dev(0, k) for k in (1, -1, 2)]
    for dev in partners:
        pl.semaphore_signal(barrier, inc=1, device_id=dev, device_id_type=MESH)

    inputs = [
        pltpu.make_async_copy(src, dst, in_sem.at[i])
        for i, (src, dst) in enumerate(
            (
                (order_hbm, order_ref),
                (routes_hbm, routes_ref),
                (k_hbm, kv.at[0, 0, tori[0].line(0), tori[0].along(0)]),
                (v_hbm, kv.at[0, 1, tori[1].line(0), tori[1].along(0)]),
                (q_hbm, q_ref),
                (gain_hbm, gain_ref),
                (router_hbm, router_ref),
            )
        )
    ]
    for copy in inputs:
        copy.start()
    loads = [
        pltpu.make_async_copy(wg_hbm, wg, w_sem.at[0]),
        pltpu.make_async_copy(wu_hbm, wu, w_sem.at[1]),
    ]
    for f in range(2):
        for m in range(EXPERTS // 2):
            cols = pl.ds(pl.multiple_of((2 * m + lax.rem(e + f, 2)) * CHUNK, CHUNK), CHUNK)
            loads.append(
                pltpu.make_async_copy(
                    wd_hbm.at[:, cols], wd.at[f, :, pl.ds(m * CHUNK, CHUNK)], w_sem.at[2]
                )
            )
    for load in loads:
        load.start()
    inputs[0].wait()
    inputs[1].wait()

    n = n_rows = att_ref.shape[0]
    onehot = (lax.broadcasted_iota(jnp.int32, (EXPERTS, n_rows), 0) == routes_ref[...]).astype(jnp.float32)
    before = (
        lax.broadcasted_iota(jnp.int32, (n_rows, n_rows), 0)
        < lax.broadcasted_iota(jnp.int32, (n_rows, n_rows), 1)
    ).astype(jnp.bfloat16)
    earlier = jnp.dot(onehot.astype(jnp.bfloat16), before, preferred_element_type=jnp.float32)
    code = jnp.sum(onehot * earlier, axis=0, keepdims=True).astype(jnp.int32) + routes_ref[...] * CAP
    placing = (lax.broadcasted_iota(jnp.int32, (EXPERTS * CAP, n_rows), 0) == code).astype(jnp.bfloat16)


    half_n = n // 2

    def positions(c, shape, dim):
        i = lax.broadcasted_iota(jnp.int32, shape, dim)
        return i + jnp.where(i < half_n, order_ref[2 * c] * half_n, (order_ref[2 * c + 1] - 1) * half_n)

    query_pos = positions(ctx, (1, n), 1)
    for w in range(PLANES):

        @pl.loop(0, SIDE * SIDE)
        def _(i):
            kept = positions(planes[w] * SIDE * SIDE + i, (n, 1), 0) <= query_pos
            rows = pl.ds(pl.multiple_of(i * n, n), n)
            hidden_keys[w, rows, :] = jnp.where(kept, 0.0, -1e30).astype(jnp.bfloat16)

    for copy in inputs[2:]:
        copy.wait()
    pl.semaphore_wait(barrier, len(partners))

    for t in tori:
        piece = (t.h, t.line(0), t.along(0))
        send(kv.at[0, *piece], kv.at[1, *piece], kv_s.at[0], kv_r.at[8], column(other, 0))

    def kv_near(w):
        for d in (1, -1, 2):
            for t in tori:
                piece = kv.at[w, t.h, t.line(0), t.along(0)]
                send(piece, piece, kv_s.at[1], kv_r.at[4 * w + t.h], t.dev(d, 0))

    def kv_far(w):
        for t in tori:
            arrived(kv.at[w, t.h, 0, pl.ds(0, SIDE - 1)], kv_r.at[4 * w + t.h])
            line = kv.at[w, t.h, t.line(0)]
            for d in (1, -1, 2):
                send(line, line, kv_s.at[2], kv_r.at[4 * w + 2 + t.h], t.dev(0, d))

    def kv_done(w):
        for t in tori:
            arrived(kv.at[w, t.h, pl.ds(0, SIDE - 1)], kv_r.at[4 * w + 2 + t.h])

    scale = math.log2(math.e) / math.sqrt(HEAD_DIM)
    heads = q_ref.shape[1] // HEAD_DIM
    each = (
        lax.broadcasted_iota(jnp.int32, (n, n), 0) == lax.broadcasted_iota(jnp.int32, (n, n), 1)
    ).astype(jnp.bfloat16)

    def attend(w):
        everyone = SIDE * SIDE * n
        keys = jnp.concatenate([kv[w, 0].reshape(everyone, HEAD_DIM), hidden_keys[w]], axis=1)
        values = jnp.concatenate(
            [kv[w, 1, i, row] for row in range(SIDE) for i in range(SIDE)], axis=0
        )
        for head in range(heads):
            q = jnp.concatenate([q_ref[:, pl.ds(head * HEAD_DIM, HEAD_DIM)], each], axis=1)
            scores = lax.dot_general(q, keys, (((1,), (1,)), ((), ())), preferred_element_type=jnp.float32)
            new = jnp.max(scores, axis=1, keepdims=True)
            if w > 0:
                old = soft_max[head]
                new = jnp.maximum(old, new)
                fade = jnp.exp2((old - new) * scale)
            probs = jnp.exp2(scores * scale - new * scale)
            total = jnp.sum(probs, axis=1, keepdims=True)
            mixed = jnp.dot(probs.astype(jnp.bfloat16), values, preferred_element_type=jnp.float32)
            if w > 0:
                total = total + soft_sum[head] * fade
                mixed = mixed + soft_acc[head] * fade
                att_ref[:, pl.ds(head * HEAD_DIM, HEAD_DIM)] = (mixed / total).astype(jnp.bfloat16)
            else:
                soft_max[head] = new
                soft_sum[head] = total
                soft_acc[head] = mixed

    kv_near(0)
    kv_far(0)
    arrived(kv.at[1, 0, 0, pl.ds(0, 2)], kv_r.at[8])
    kv_near(1)
    kv_far(1)
    kv_done(0)
    attend(0)
    kv_done(1)
    attend(1)
    attended = pltpu.make_async_copy(att_ref, both_hbm.at[0], in_sem.at[7])
    attended.start()

    packed = jnp.dot(placing, att_ref[...], preferred_element_type=jnp.float32).astype(jnp.bfloat16)
    pack[...] = packed.reshape(EXPERTS, CAP, CHUNK)

    def dispatch(w, first, count):
        rows = pl.ds(first, count)
        h = first // HALF
        for d in range(1 - w, EXPERTS):
            to = lax.rem(e + d, EXPERTS)
            send(
                pack.at[to, rows], xin.at[w, e, rows], a2a_s.at[w], a2a_r.at[2 * w + h], column(planes[w], d)
            )

    dispatch(0, 0, HALF)
    dispatch(0, HALF, HALF)
    own = pltpu.make_async_copy(pack.at[e], xin.at[0, e], in_sem.at[9])
    own.start()

    def norm(w, first, count):
        rows = pl.ds(first, count)
        arrived(xin.at[w, pl.ds(0, EXPERTS - 1 + w), rows], a2a_r.at[2 * w + first // HALF])
        if w == 0 and first == 0:
            own.wait()
        squares = jnp.zeros((count, 1), jnp.float32)
        for j in range(EXPERTS):
            v = xin[w, j, rows].astype(jnp.float32)
            squares += jnp.sum(v * v, axis=1, keepdims=True)
        inverse = lax.rsqrt(squares / WIDTH + 1e-05)
        mine = lax.broadcasted_iota(jnp.int32, (EXPERTS, CHUNK), 0) == e
        logit = jnp.zeros((count, 1), jnp.float32)
        for j in range(EXPERTS):
            cols = pl.ds(j * CHUNK, CHUNK)
            v = xin[w, j, rows].astype(jnp.float32) * inverse * gain_ref[:, cols]
            weight = jnp.sum(jnp.where(mine, router_ref[:, cols], 0.0), axis=0, keepdims=True)
            logit += jnp.sum(v * weight, axis=1, keepdims=True)
        gate = 1.0 / (1.0 + jnp.exp(-logit))
        for j in range(EXPERTS):
            cols = pl.ds(j * CHUNK, CHUNK)
            v = xin[w, j, rows].astype(jnp.float32) * inverse * gain_ref[:, cols]
            v = (v * gate).astype(jnp.bfloat16)
            for k in range(count // HALF):
                g[w, first // HALF + k, tori[0].rows(0, 0), cols] = v[k * HALF : (k + 1) * HALF]

    left_half, right_half = pl.ds(0, UNIT_COLS // 2), pl.ds(UNIT_COLS // 2, UNIT_COLS // 2)
    gather = [
        Gather(
            tori,
            lambda t, dp, dq, w=w: g.at[w, t.h, t.rows(dp, dq)],
            lambda t, dp, dq, s, w=w: g.at[w, t.h, t.rows(dp, dq), pl.ds(s * PIECE_COLS, PIECE_COLS)],
            lambda k, w=w: g.at[w, 0, pl.ds(0, k * HALF)],
            ag_s,
            ag_r.at[w],
            send,
            arrived,
        )
        for w in range(PLANES)
    ]

    def ffn(w, h):
        step = 1280
        acc[...] = jnp.zeros_like(acc)

        @pl.loop(0, WIDTH // step)
        def _(k):
            cols = pl.ds(pl.multiple_of(k * step, step), step)
            rows = g[w, h, :, cols]
            acc[0] += jnp.dot(rows, wg[cols, :], preferred_element_type=jnp.float32)
            acc[1] += jnp.dot(rows, wu[cols, :], preferred_element_type=jnp.float32)

        v = acc[0]
        hid[...] = (v / (1.0 + jnp.exp(-v)) * acc[1]).astype(jnp.bfloat16)
        wide = 512

        @pl.loop(0, UNIT_COLS // wide)
        def _(k):
            cols = pl.ds(pl.multiple_of(k * wide, wide), wide)
            for f in range(2):
                part[w, f, h, :, cols] = jnp.dot(
                    hid[...], wd[f, :, cols], preferred_element_type=jnp.float32
                ).astype(jnp.bfloat16)

    def add(ref, *more):
        total = ref[...].astype(jnp.float32)
        for m in more:
            total = total + m[...].astype(jnp.float32)
        ref[...] = total.astype(jnp.bfloat16)

    mine = pltpu.make_async_copy(fin.at[0, 0, e // 2], ret.at[0, e], in_sem.at[10])

    def rs_start(u):
        for t in tori:
            for i, s in OPPOSITE:
                send(
                    part.at[*u, t.h, t.rows(OFFS[i], 2)],
                    ru1.at[*u, i, t.h],
                    rs_s.at[0],
                    rs_r.at[*u, i],
                    t.dev(0, 1 if s == 0 else -1),
                )

    def rs_second(u, t, i, s):
        dq = 1 if s == 0 else -1
        send(
            part.at[*u, t.h, t.rows(OFFS[i], dq)],
            ru2.at[*u, i, s, t.h],
            rs_s.at[1],
            rs_r.at[*u, 4 + i],
            t.dev(0, dq),
        )

    def rs_plain(u):
        for t in tori:
            for i, s in OPPOSITE:
                rs_second(u, t, i, 1 - s)

    def rs_joined(u, i):
        s = OPPOSITE[i][1]
        dq = 1 if s == 0 else -1
        arrived(ru1.at[*u, i], rs_r.at[*u, i])
        for t in tori:
            add(part.at[*u, t.h, t.rows(OFFS[i], dq)], ru1.at[*u, i, t.h])
            rs_second(u, t, i, s)

    def rs_sum(u, i):
        arrived(ru2.at[*u, i], rs_r.at[*u, 4 + i])
        for t in tori:
            add(part.at[*u, t.h, t.rows(OFFS[i], 0)], ru2.at[*u, i, 0, t.h], ru2.at[*u, i, 1, t.h])

    SIDES = ((0, 1, left_half), (1, -1, right_half))

    def rs_turn(u):
        rs_sum(u, 3)
        for t in tori:
            for s, dp, cols in SIDES:
                send(part.at[*u, t.h, t.rows(2, 0), cols], rv1.at[*u, t.h, s], rs_s.at[2], rs_r.at[*u, 8], t.dev(dp, 0))
        rs_sum(u, 1)
        rs_sum(u, 2)

    def rs_last(u):
        arrived(rv1.at[*u], rs_r.at[*u, 8])
        for t in tori:
            for s, dp, cols in SIDES:
                add(part.at[*u, t.h, t.rows(dp, 0), cols], rv1.at[*u, t.h, s])
                send(part.at[*u, t.h, t.rows(dp, 0)], rv2.at[*u, t.h, s], rs_s.at[3], rs_r.at[*u, 9], t.dev(dp, 0))
        rs_sum(u, 0)

    def rs_finish(u):
        arrived(rv2.at[*u], rs_r.at[*u, 9])
        for t in tori:
            for m in range(EXPERTS // 2):
                cols = pl.ds(m * CHUNK, CHUNK)
                total = part[*u, t.h, t.rows(0, 0), cols].astype(jnp.float32)
                for s in range(2):
                    total = total + rv2[*u, t.h, s, :, cols].astype(jnp.float32)
                fin[*u, m, pl.ds(t.h * HALF, HALF)] = total.astype(jnp.bfloat16)
        w, f = u
        for d in range(f, EXPERTS, 2):
            to = lax.rem(e + d, EXPERTS)
            if w == 0 and d == 0:
                mine.start()
            else:
                send(fin.at[w, f, to // 2], ret.at[w, e], back_s.at[w], back_r.at[w], column(planes[w], d))

    for t in tori:
        norm(0, t.h * HALF, HALF)
        gather[0].start(t)
    dispatch(1, 0, CAP)
    gather[0].near()
    gather[0].far()
    gather[0].forward(0)
    gather[0].forward(1)
    norm(1, 0, CAP)
    for t in tori:
        gather[1].start(t)
    gather[0].forward(2)
    gather[0].forward(3)
    gather[1].near()
    gather[1].far()
    loads[0].wait()
    loads[1].wait()
    pltpu.make_async_copy(wd, wd, w_sem.at[2]).wait()
    gather[0].done()
    gather[1].forward(0)
    gather[1].forward(1)
    ffn(0, 0)
    gather[1].forward(2)
    gather[1].forward(3)
    ffn(0, 1)
    a, b, c, d = (0, 0), (1, 0), (1, 1), (0, 1)

    def rs_begin(u):
        rs_start(u)
        rs_plain(u)

    def rs_join(u):
        for i in range(4):
            rs_joined(u, i)

    rs_begin(a)
    rs_begin(d)
    gather[1].done()
    rs_join(a)
    ffn(1, 0)
    ffn(1, 1)
    rs_begin(b)
    rs_turn(a)
    rs_join(b)
    rs_begin(c)
    rs_last(a)
    rs_turn(b)
    rs_finish(a)
    rs_join(c)
    rs_last(b)
    rs_turn(c)
    rs_join(d)
    rs_finish(b)
    rs_last(c)
    rs_turn(d)
    rs_finish(c)
    rs_last(d)
    rs_finish(d)

    routed = None
    for w in range(PLANES):
        arrived(ret.at[w, pl.ds(0, EXPERTS - 1 + w)], back_r.at[w])
        if w == 0:
            mine.wait()
        rows = ret[w].reshape(EXPERTS * CAP, CHUNK)
        term = lax.dot_general(
            placing, rows, (((0,), (0,)), ((), ())), preferred_element_type=jnp.float32
        )
        routed = term if routed is None else routed + term
    out_ref[...] = routed.astype(jnp.bfloat16)
    result = pltpu.make_async_copy(out_ref, both_hbm.at[1], in_sem.at[8])
    result.start()
    attended.wait()
    result.wait()
    all_sent(kv.at[0, 0, 0, pl.ds(0, 2)], kv_s.at[0])
    all_sent(kv.at[0, 0, pl.ds(0, SIDE - 1)], kv_s.at[1])
    all_sent(kv.at[:, :, pl.ds(0, SIDE - 1)], kv_s.at[2])
    all_sent(xin.at[0, pl.ds(0, EXPERTS - 1)], a2a_s.at[0])
    all_sent(xin.at[1], a2a_s.at[1])
    all_sent(g.at[0, 0, pl.ds(0, 8 * HALF)], ag_s.at[0])
    all_sent(g.at[0, 0, pl.ds(0, 4 * HALF)], ag_s.at[1])
    all_sent(g.at[0], ag_s.at[2])
    all_sent(g.at[0, 0], ag_s.at[3])
    for i, ref in enumerate((ru1, ru2, rv1, rv2)):
        all_sent(ref, rs_s.at[i])
    all_sent(ret.at[0, pl.ds(0, EXPERTS - 1)], back_s.at[0])
    all_sent(ret.at[1], back_s.at[1])


def per_device(queries, keys, values, block_order, routes, norm_gain, router, w_gate, w_up, w_down):
    anywhere = pl.BlockSpec(memory_space=pl.ANY)
    bf16, f32 = jnp.bfloat16, jnp.float32
    dma = pltpu.SemaphoreType.DMA
    here, features = queries.shape
    heads = features // HEAD_DIM
    both = pl.pallas_call(
        kernel,
        out_shape=jax.ShapeDtypeStruct((2, *queries.shape), bf16),
        in_specs=[anywhere] * 10,
        out_specs=anywhere,
        scratch_shapes=[
            pltpu.VMEM((here, features), bf16),
            pltpu.SMEM(block_order.shape, jnp.int32),
            pltpu.VMEM((1, here), jnp.int32),
            pltpu.VMEM((1, WIDTH), f32),
            pltpu.VMEM((EXPERTS, WIDTH), f32),
            pltpu.VMEM((here, features), bf16),
            pltpu.VMEM((here, features), bf16),
            pltpu.VMEM((PLANES, SIDE * SIDE * here, here), bf16),
            pltpu.VMEM((PLANES, 2, SIDE, SIDE, here, HEAD_DIM), bf16),
            pltpu.VMEM((heads, here, 1), f32),
            pltpu.VMEM((heads, here, 1), f32),
            pltpu.VMEM((heads, here, HEAD_DIM), f32),
            pltpu.VMEM((WIDTH, HID), bf16),
            pltpu.VMEM((WIDTH, HID), bf16),
            pltpu.VMEM((2, HID, UNIT_COLS), bf16),
            pltpu.VMEM((EXPERTS, CAP, CHUNK), bf16),
            pltpu.VMEM((PLANES, EXPERTS, CAP, CHUNK), bf16),
            pltpu.VMEM((PLANES, 2, GROUP, WIDTH), bf16),
            pltpu.VMEM((PLANES, 2, 2, GROUP, UNIT_COLS), bf16),
            pltpu.VMEM((PLANES, 2, 4, 2, HALF, UNIT_COLS), bf16),
            pltpu.VMEM((PLANES, 2, 4, 2, 2, HALF, UNIT_COLS), bf16),
            pltpu.VMEM((PLANES, 2, 2, 2, HALF, UNIT_COLS // 2), bf16),
            pltpu.VMEM((PLANES, 2, 2, 2, HALF, UNIT_COLS), bf16),
            pltpu.VMEM((PLANES, 2, EXPERTS // 2, CAP, CHUNK), bf16),
            pltpu.VMEM((PLANES, EXPERTS, CAP, CHUNK), bf16),
            pltpu.VMEM((2, GROUP, HID), f32),
            pltpu.VMEM((GROUP, HID), bf16),
            dma((11,)),
            dma((3,)),
            dma((3,)),
            dma((9,)),
            dma((2,)),
            dma((3,)),
            dma((4,)),
            dma((PLANES, 9)),
            dma((4,)),
            dma((PLANES, 2, 10)),
            dma((2,)),
            dma((2,)),
        ],
        compiler_params=pltpu.CompilerParams(
            collective_id=1, has_side_effects=True, vmem_limit_bytes=62 << 20
        ),
        name="layer",
    )(
        queries,
        keys,
        values,
        block_order,
        routes.reshape(1, -1),
        norm_gain.reshape(1, -1),
        router.T,
        w_gate[0],
        w_up[0],
        w_down[0],
    )
    return both[0], both[1]


def solution(mesh):
    in_specs = (
        P("ctx", "exp"),
        P("ctx", "exp"),
        P("ctx", "exp"),
        P(),
        P("ctx", None),
        P(),
        P(),
        P("exp", None, "ctx"),
        P("exp", None, "ctx"),
        P("exp", "ctx", None),
    )
    out_specs = (P("ctx", "exp"), P("ctx", "exp"))
    return jax.shard_map(
        per_device, mesh=mesh, in_specs=in_specs, out_specs=out_specs, check_vma=False
    )
```

```python
import functools
import math

import jax
import jax.numpy as jnp
from jax import lax
from jax.experimental import pallas as pl
from jax.experimental.pallas import tpu as pltpu
from jax.sharding import PartitionSpec as P

HEAD_DIM = 128
CAP = 32
MESH = pl.DeviceIdType.MESH

PLANES = 2
SIDE = 4
EXPERTS = 8
WIDTH = 5120
CHUNK = WIDTH // EXPERTS
HALF = CAP // 2
PIECE_COLS = WIDTH // 2
UNIT_COLS = WIDTH // 2
GROUP = SIDE * SIDE * HALF
HID = 256


def mod4(v):
    return lax.rem(v + 2 * SIDE, SIDE)


OFFS = (0, -1, 1, 2)
OPPOSITE = ((0, 0), (1, 1), (2, 1), (3, 0))


class Gather:
    def __init__(self, tori, piece, half, rows, ssem, rsem, send, arrived):
        self.tori, self.piece, self.half, self.rows = tori, piece, half, rows
        self.ssem, self.rsem, self.send, self.arrived = ssem, rsem, send, arrived

    def second(self, t, i):
        piece = self.piece(t, OFFS[i], 0)
        for s, dq in ((0, 1), (1, -1)):
            r = 4 + i if s == OPPOSITE[i][1] else 8
            self.send(piece, piece, self.ssem.at[2], self.rsem.at[r], t.dev(0, dq))

    def start(self, t):
        piece = self.piece(t, 0, 0)
        for dp in (1, -1):
            self.send(piece, piece, self.ssem.at[0], self.rsem.at[t.h], t.dev(dp, 0))
        self.second(t, 0)

    def near(self):
        for t in self.tori:
            self.arrived(self.rows(2), self.rsem.at[t.h])
            for s, dp in ((0, -1), (1, 1)):
                half = self.half(t, dp, 0, s)
                self.send(half, half, self.ssem.at[1], self.rsem.at[2 + t.h], t.dev(-dp, 0))
        for t in self.tori:
            self.second(t, 1)
            self.second(t, 2)

    def far(self):
        for t in self.tori:
            self.arrived(self.rows(1), self.rsem.at[2 + t.h])
            self.second(t, 3)

    def forward(self, i):
        dq = 1 if OPPOSITE[i][1] == 0 else -1
        self.arrived(self.rows(2), self.rsem.at[4 + i])
        for t in self.tori:
            piece = self.piece(t, OFFS[i], -dq)
            self.send(piece, piece, self.ssem.at[3], self.rsem.at[8], t.dev(0, dq))

    def done(self):
        self.arrived(self.rows(16), self.rsem.at[8])


class Torus:
    def __init__(self, h, plane, y, x, e):
        self.h, self.plane, self.y, self.x, self.e = h, plane, y, x, e

    def at(self, dp, dq):
        if self.h == 0:
            return mod4(self.y + dq), mod4(self.x + dp)
        return mod4(self.y + dp), mod4(self.x + dq)

    def rows(self, dp, dq):
        y, x = self.at(dp, dq)
        return pl.ds(pl.multiple_of((y * SIDE + x) * HALF, HALF), HALF)

    def line(self, dq):
        return mod4((self.y if self.h == 0 else self.x) + dq)

    def along(self, dp):
        return mod4((self.x if self.h == 0 else self.y) + dp)

    def dev(self, dp, dq):
        y, x = self.at(dp, dq)
        return (self.plane * SIDE * SIDE + y * SIDE + x, self.e)


def kernel(
    q_hbm,
    k_hbm,
    v_hbm,
    order_hbm,
    routes_hbm,
    gain_hbm,
    router_hbm,
    wg_hbm,
    wu_hbm,
    wd_hbm,
    both_hbm,
    q_ref,
    order_ref,
    routes_ref,
    gain_ref,
    router_ref,
    att_ref,
    out_ref,
    hidden_keys,
    kv,
    soft_max,
    soft_sum,
    soft_acc,
    wg,
    wu,
    wd,
    pack,
    xin,
    g,
    part,
    ru1,
    ru2,
    rv1,
    rv2,
    fin,
    ret,
    acc,
    hid,
    in_sem,
    w_sem,
    kv_s,
    kv_r,
    a2a_s,
    a2a_r,
    ag_s,
    ag_r,
    rs_s,
    rs_r,
    back_s,
    back_r,
):
    ctx = lax.axis_index("ctx")
    e = lax.axis_index("exp")
    plane = ctx // (SIDE * SIDE)
    other = 1 - plane
    spot = lax.rem(ctx, SIDE * SIDE)
    y, x = spot // SIDE, lax.rem(spot, SIDE)
    tori = [Torus(h, plane, y, x, e) for h in range(2)]
    planes = (plane, other)

    def send(src, dst, ssem, rsem, dev):
        copy = pltpu.make_async_remote_copy(
            src_ref=src, dst_ref=dst, send_sem=ssem, recv_sem=rsem, device_id=dev, device_id_type=MESH
        )
        copy.start()

    def arrived(ref, rsem):
        pltpu.make_async_remote_copy(
            src_ref=ref, dst_ref=ref, send_sem=rsem, recv_sem=rsem, device_id=tori[0].dev(1, 0), device_id_type=MESH
        ).wait_recv()

    def all_sent(ref, ssem):
        pltpu.make_async_remote_copy(
            src_ref=ref, dst_ref=ref, send_sem=ssem, recv_sem=ssem, device_id=tori[0].dev(1, 0), device_id_type=MESH
        ).wait_send()

    def column(pl_index, d):
        return (pl_index * SIDE * SIDE + spot, lax.rem(e + d, EXPERTS))

    barrier = pltpu.get_barrier_semaphore()
    partners = [column(plane, d) for d in range(1, EXPERTS)]
    partners += [column(other, d) for d in range(EXPERTS)]
    partners += [tori[0].dev(k, 0) for k in (1, -1, 2)] + [tori[0].dev(0, k) for k in (1, -1, 2)]
    for dev in partners:
        pl.semaphore_signal(barrier, inc=1, device_id=dev, device_id_type=MESH)

    inputs = [
        pltpu.make_async_copy(src, dst, in_sem.at[i])
        for i, (src, dst) in enumerate(
            (
                (order_hbm, order_ref),
                (routes_hbm, routes_ref),
                (k_hbm, kv.at[0, 0, tori[0].line(0), tori[0].along(0)]),
                (v_hbm, kv.at[0, 1, tori[1].line(0), tori[1].along(0)]),
                (q_hbm, q_ref),
                (gain_hbm, gain_ref),
                (router_hbm, router_ref),
            )
        )
    ]
    for copy in inputs:
        copy.start()
    loads = [
        pltpu.make_async_copy(wg_hbm, wg, w_sem.at[0]),
        pltpu.make_async_copy(wu_hbm, wu, w_sem.at[1]),
    ]
    distances = ((1, 2), (3, 0))

    def receiver(f, k):
        return lax.rem(e // 2 + distances[f][k // 2], EXPERTS // 2) * 2 + lax.rem(e + k, 2)

    for f in range(2):
        for k in range(EXPERTS // 2):
            cols = pl.ds(pl.multiple_of(receiver(f, k) * CHUNK, CHUNK), CHUNK)
            loads.append(
                pltpu.make_async_copy(wd_hbm.at[:, cols], wd.at[f, :, pl.ds(k * CHUNK, CHUNK)], w_sem.at[2])
            )
    for load in loads:
        load.start()
    inputs[0].wait()
    inputs[1].wait()

    n = n_rows = att_ref.shape[0]
    onehot = (lax.broadcasted_iota(jnp.int32, (EXPERTS, n_rows), 0) == routes_ref[...]).astype(jnp.float32)
    before = (
        lax.broadcasted_iota(jnp.int32, (n_rows, n_rows), 0)
        < lax.broadcasted_iota(jnp.int32, (n_rows, n_rows), 1)
    ).astype(jnp.bfloat16)
    earlier = jnp.dot(onehot.astype(jnp.bfloat16), before, preferred_element_type=jnp.float32)
    code = jnp.sum(onehot * earlier, axis=0, keepdims=True).astype(jnp.int32) + routes_ref[...] * CAP
    placing = (lax.broadcasted_iota(jnp.int32, (EXPERTS * CAP, n_rows), 0) == code).astype(jnp.bfloat16)


    half_n = n // 2

    def positions(c, shape, dim):
        i = lax.broadcasted_iota(jnp.int32, shape, dim)
        return i + jnp.where(i < half_n, order_ref[2 * c] * half_n, (order_ref[2 * c + 1] - 1) * half_n)

    query_pos = positions(ctx, (1, n), 1)
    for w in range(PLANES):

        @pl.loop(0, SIDE * SIDE)
        def _(i):
            kept = positions(planes[w] * SIDE * SIDE + i, (n, 1), 0) <= query_pos
            hidden_keys[w, i] = jnp.where(kept, 0.0, -1e30).astype(jnp.bfloat16)

    for copy in inputs[2:]:
        copy.wait()
    pl.semaphore_wait(barrier, len(partners))

    for t in tori:
        piece = (t.h, t.line(0), t.along(0))
        send(kv.at[0, *piece], kv.at[1, *piece], kv_s.at[0], kv_r.at[8], column(other, 0))

    def kv_near(w):
        for d in (1, -1, 2):
            for t in tori:
                piece = kv.at[w, t.h, t.line(0), t.along(0)]
                send(piece, piece, kv_s.at[1], kv_r.at[4 * w + t.h], t.dev(d, 0))

    def kv_far(w):
        for t in tori:
            arrived(kv.at[w, t.h, 0, pl.ds(0, SIDE - 1)], kv_r.at[4 * w + t.h])
            line = kv.at[w, t.h, t.line(0)]
            for d in (1, -1):
                send(line, line, kv_s.at[2], kv_r.at[4 * w + 2 + t.h], t.dev(0, d))

    def kv_forward(w):
        for t in tori:
            arrived(kv.at[w, t.h, pl.ds(0, 2)], kv_r.at[4 * w + 2 + t.h])
            for s, d in ((0, 1), (1, -1)):
                half = kv.at[w, t.h, t.line(-d), pl.ds(2 * s, 2)]
                send(half, half, kv_s.at[3], kv_r.at[9 + 2 * w + t.h], t.dev(0, d))

    def kv_done(w):
        for t in tori:
            arrived(kv.at[w, t.h, 0], kv_r.at[9 + 2 * w + t.h])

    scale = math.log2(math.e) / math.sqrt(HEAD_DIM)
    heads = q_ref.shape[1] // HEAD_DIM
    each = (
        lax.broadcasted_iota(jnp.int32, (n, n), 0) == lax.broadcasted_iota(jnp.int32, (n, n), 1)
    ).astype(jnp.bfloat16)

    def attend(w, blocks, first=False, last=False):
        places = [(mod4(y + dy), mod4(x + dx)) for dy, dx in blocks]
        keys = jnp.concatenate([kv[w, 0, r, i] for r, i in places], axis=0)
        values = jnp.concatenate([kv[w, 1, i, r] for r, i in places], axis=0)
        hide = jnp.concatenate([hidden_keys[w, r * SIDE + i] for r, i in places], axis=0)
        keys = jnp.concatenate([keys, hide], axis=1)
        for head in range(heads):
            q = jnp.concatenate([q_ref[:, pl.ds(head * HEAD_DIM, HEAD_DIM)], each], axis=1)
            scores = lax.dot_general(q, keys, (((1,), (1,)), ((), ())), preferred_element_type=jnp.float32)
            new = jnp.max(scores, axis=1, keepdims=True)
            if not first:
                old = soft_max[head]
                new = jnp.maximum(old, new)
                fade = jnp.exp2((old - new) * scale)
            probs = jnp.exp2(scores * scale - new * scale)
            total = jnp.sum(probs, axis=1, keepdims=True)
            mixed = jnp.dot(probs.astype(jnp.bfloat16), values, preferred_element_type=jnp.float32)
            if not first:
                total = total + soft_sum[head] * fade
                mixed = mixed + soft_acc[head] * fade
            if last:
                att_ref[:, pl.ds(head * HEAD_DIM, HEAD_DIM)] = (mixed / total).astype(jnp.bfloat16)
            else:
                soft_max[head] = new
                soft_sum[head] = total
                soft_acc[head] = mixed

    everyone = [(dy, dx) for dy in range(SIDE) for dx in range(SIDE)]
    close = [(dy, dx) for dy, dx in everyone if dy != 2 and dx != 2]
    distant = [block for block in everyone if block not in close]

    kv_near(0)
    kv_far(0)
    arrived(kv.at[1, 0, 0, pl.ds(0, 2)], kv_r.at[8])
    kv_near(1)
    kv_forward(0)
    attend(0, close, first=True)
    kv_far(1)
    kv_done(0)
    attend(0, distant)
    kv_forward(1)
    attend(1, close)
    kv_done(1)
    attend(1, distant, last=True)

    attended = pltpu.make_async_copy(att_ref, both_hbm.at[0], in_sem.at[7])
    attended.start()

    packed = jnp.dot(placing, att_ref[...], preferred_element_type=jnp.float32).astype(jnp.bfloat16)
    pack[...] = packed.reshape(EXPERTS, CAP, CHUNK)

    def dispatch(w, first, count):
        rows = pl.ds(first, count)
        h = first // HALF
        for d in range(1 - w, EXPERTS):
            to = lax.rem(e + d, EXPERTS)
            send(
                pack.at[to, rows], xin.at[w, e, rows], a2a_s.at[w], a2a_r.at[2 * w + h], column(planes[w], d)
            )

    dispatch(0, 0, HALF)
    dispatch(0, HALF, HALF)
    own = pltpu.make_async_copy(pack.at[e], xin.at[0, e], in_sem.at[9])
    own.start()

    def norm(w, first, count):
        rows = pl.ds(first, count)
        arrived(xin.at[w, pl.ds(0, EXPERTS - 1 + w), rows], a2a_r.at[2 * w + first // HALF])
        if w == 0 and first == 0:
            own.wait()
        squares = jnp.zeros((count, 1), jnp.float32)
        for j in range(EXPERTS):
            v = xin[w, j, rows].astype(jnp.float32)
            squares += jnp.sum(v * v, axis=1, keepdims=True)
        inverse = lax.rsqrt(squares / WIDTH + 1e-05)
        mine = lax.broadcasted_iota(jnp.int32, (EXPERTS, CHUNK), 0) == e
        logit = jnp.zeros((count, 1), jnp.float32)
        for j in range(EXPERTS):
            cols = pl.ds(j * CHUNK, CHUNK)
            v = xin[w, j, rows].astype(jnp.float32) * inverse * gain_ref[:, cols]
            weight = jnp.sum(jnp.where(mine, router_ref[:, cols], 0.0), axis=0, keepdims=True)
            logit += jnp.sum(v * weight, axis=1, keepdims=True)
        gate = 1.0 / (1.0 + jnp.exp(-logit))
        for j in range(EXPERTS):
            cols = pl.ds(j * CHUNK, CHUNK)
            v = xin[w, j, rows].astype(jnp.float32) * inverse * gain_ref[:, cols]
            v = (v * gate).astype(jnp.bfloat16)
            for k in range(count // HALF):
                g[w, first // HALF + k, tori[0].rows(0, 0), cols] = v[k * HALF : (k + 1) * HALF]


    gather = [
        Gather(
            tori,
            lambda t, dp, dq, w=w: g.at[w, t.h, t.rows(dp, dq)],
            lambda t, dp, dq, s, w=w: g.at[w, t.h, t.rows(dp, dq), pl.ds(s * PIECE_COLS, PIECE_COLS)],
            lambda k, w=w: g.at[w, 0, pl.ds(0, k * HALF)],
            ag_s,
            ag_r.at[w],
            send,
            arrived,
        )
        for w in range(PLANES)
    ]

    def ffn(w, h):
        step = 1280
        acc[...] = jnp.zeros_like(acc)

        @pl.loop(0, WIDTH // step)
        def _(k):
            cols = pl.ds(pl.multiple_of(k * step, step), step)
            rows = g[w, h, :, cols]
            acc[0] += jnp.dot(rows, wg[cols, :], preferred_element_type=jnp.float32)
            acc[1] += jnp.dot(rows, wu[cols, :], preferred_element_type=jnp.float32)

        v = acc[0]
        hid[...] = (v / (1.0 + jnp.exp(-v)) * acc[1]).astype(jnp.bfloat16)
        wide = 512

        @pl.loop(0, UNIT_COLS // wide)
        def _(k):
            cols = pl.ds(pl.multiple_of(k * wide, wide), wide)
            for f in range(2):
                part[w, f, h, :, cols] = jnp.dot(
                    hid[...], wd[f, :, cols], preferred_element_type=jnp.float32
                ).astype(jnp.bfloat16)

    def add(ref, *more):
        total = ref[...].astype(jnp.float32)
        for m in more:
            total = total + m[...].astype(jnp.float32)
        ref[...] = total.astype(jnp.bfloat16)

    mine = pltpu.make_async_copy(fin.at[0, 0, e // 2], ret.at[0, e], in_sem.at[10])

    class Unit:
        def __init__(self, n, w, f, chunks):
            self.n, self.w, self.f, self.chunks = n, w, f, chunks
            self.first, self.count = chunks[0] * CHUNK, len(chunks) * CHUNK
            self.cols = pl.ds(self.first, self.count)

        def part(self, t, dp, dq):
            return part.at[self.w, self.f, t.h, t.rows(dp, dq), self.cols]

        def half_part(self, t, dp, s):
            half = self.count // 2
            return part.at[self.w, self.f, t.h, t.rows(dp, 0), pl.ds(self.first + s * half, half)]

        def via(self, i, h):
            return ru1.at[self.w, self.f, i, h, :, self.cols]

        def second(self, i, s, h):
            return ru2.at[self.w, self.f, i, s, h, :, self.cols]

        def half_via(self, h, s):
            return rv1.at[self.w, self.f, h, s, :, pl.ds(self.first // 2, self.count // 2)]

        def first_axis(self, h, s):
            return rv2.at[self.w, self.f, h, s, :, self.cols]

        def sem(self, k):
            return rs_r.at[self.n, k]

    both = slice(None)

    def rs_begin(u):
        for t in tori:
            for i, s in OPPOSITE:
                send(u.part(t, OFFS[i], 2), u.via(i, t.h), rs_s.at[0], u.sem(i), t.dev(0, 1 if s == 0 else -1))
        for t in tori:
            for i, s in OPPOSITE:
                rs_second(u, t, i, 1 - s)

    def rs_second(u, t, i, s):
        dq = 1 if s == 0 else -1
        send(u.part(t, OFFS[i], dq), u.second(i, s, t.h), rs_s.at[1], u.sem(4 + i), t.dev(0, dq))

    def rs_join(u):
        for i, s in OPPOSITE:
            arrived(u.via(i, both), u.sem(i))
            for t in tori:
                add(u.part(t, OFFS[i], 1 if s == 0 else -1), u.via(i, t.h))
                rs_second(u, t, i, s)

    def rs_sum(u, i):
        arrived(u.second(i, both, both), u.sem(4 + i))
        for t in tori:
            add(u.part(t, OFFS[i], 0), u.second(i, 0, t.h), u.second(i, 1, t.h))

    def rs_turn(u):
        rs_sum(u, 3)
        for t in tori:
            for s, dp in ((0, 1), (1, -1)):
                send(u.half_part(t, 2, s), u.half_via(t.h, s), rs_s.at[2], u.sem(8), t.dev(dp, 0))
        rs_sum(u, 1)
        rs_sum(u, 2)

    def rs_last(u):
        arrived(u.half_via(both, both), u.sem(8))
        for t in tori:
            for s, dp in ((0, 1), (1, -1)):
                add(u.half_part(t, dp, s), u.half_via(t.h, s))
                send(u.part(t, dp, 0), u.first_axis(t.h, s), rs_s.at[3], u.sem(9), t.dev(dp, 0))
        rs_sum(u, 0)

    mine = pltpu.make_async_copy(fin.at[0, 1, 2], ret.at[0, e], in_sem.at[10])

    def rs_finish(u):
        arrived(u.first_axis(both, both), u.sem(9))
        w, f = u.w, u.f
        for k in u.chunks:
            cols = pl.ds(k * CHUNK, CHUNK)
            for t in tori:
                total = part[w, f, t.h, t.rows(0, 0), cols].astype(jnp.float32)
                for s in range(2):
                    total = total + rv2[w, f, t.h, s, :, cols].astype(jnp.float32)
                fin[w, f, k, pl.ds(t.h * HALF, HALF)] = total.astype(jnp.bfloat16)
            if (w, f, k) == (0, 1, 2):
                mine.start()
            else:
                to = receiver(f, k)
                dev = (planes[w] * SIDE * SIDE + spot, to)
                send(fin.at[w, f, k], ret.at[w, e], back_s.at[w], back_r.at[w], dev)

    a, b, c = Unit(0, 0, 0, range(4)), Unit(1, 1, 0, range(4)), Unit(2, 1, 1, range(4))
    p, q = Unit(3, 0, 1, range(2)), Unit(4, 0, 1, range(2, 4))

    for t in tori:
        norm(0, t.h * HALF, HALF)
        gather[0].start(t)
    dispatch(1, 0, CAP)
    gather[0].near()
    gather[0].far()
    gather[0].forward(0)
    gather[0].forward(1)
    norm(1, 0, CAP)
    for t in tori:
        gather[1].start(t)
    gather[0].forward(2)
    gather[0].forward(3)
    gather[1].near()
    gather[1].far()
    loads[0].wait()
    loads[1].wait()
    pltpu.make_async_copy(wd, wd, w_sem.at[2]).wait()
    gather[0].done()
    gather[1].forward(0)
    gather[1].forward(1)
    ffn(0, 0)
    gather[1].forward(2)
    gather[1].forward(3)
    ffn(0, 1)
    rs_begin(a)
    rs_begin(p)
    gather[1].done()
    rs_join(a)
    ffn(1, 0)
    ffn(1, 1)
    rs_begin(b)
    rs_turn(a)
    rs_join(b)
    rs_begin(c)
    rs_last(a)
    rs_turn(b)
    rs_finish(a)
    rs_join(c)
    rs_join(p)
    rs_begin(q)
    rs_last(b)
    rs_turn(c)
    rs_finish(b)
    rs_turn(p)
    rs_last(c)
    rs_join(q)
    rs_last(p)
    rs_finish(c)
    rs_turn(q)
    rs_finish(p)
    rs_last(q)
    rs_finish(q)

    routed = None
    for w in range(PLANES):
        arrived(ret.at[w, pl.ds(0, EXPERTS - 1 + w)], back_r.at[w])
        if w == 0:
            mine.wait()
        rows = ret[w].reshape(EXPERTS * CAP, CHUNK)
        term = lax.dot_general(
            placing, rows, (((0,), (0,)), ((), ())), preferred_element_type=jnp.float32
        )
        routed = term if routed is None else routed + term
    out_ref[...] = routed.astype(jnp.bfloat16)
    result = pltpu.make_async_copy(out_ref, both_hbm.at[1], in_sem.at[8])
    result.start()
    attended.wait()
    result.wait()
    all_sent(kv.at[0, 0, 0, pl.ds(0, 2)], kv_s.at[0])
    all_sent(kv.at[0, 0, pl.ds(0, SIDE - 1)], kv_s.at[1])
    all_sent(kv.at[:, :, pl.ds(0, 2)], kv_s.at[2])
    all_sent(kv.at[:, :, 0], kv_s.at[3])
    all_sent(xin.at[0, pl.ds(0, EXPERTS - 1)], a2a_s.at[0])
    all_sent(xin.at[1], a2a_s.at[1])
    all_sent(g.at[0, 0, pl.ds(0, 8 * HALF)], ag_s.at[0])
    all_sent(g.at[0, 0, pl.ds(0, 4 * HALF)], ag_s.at[1])
    all_sent(g.at[0], ag_s.at[2])
    all_sent(g.at[0, 0], ag_s.at[3])
    for i, ref in enumerate((ru1, ru2, rv1, rv2)):
        all_sent(ref, rs_s.at[i])
    all_sent(ret.at[0, pl.ds(0, EXPERTS - 1)], back_s.at[0])
    all_sent(ret.at[1], back_s.at[1])


def per_device(queries, keys, values, block_order, routes, norm_gain, router, w_gate, w_up, w_down):
    anywhere = pl.BlockSpec(memory_space=pl.ANY)
    bf16, f32 = jnp.bfloat16, jnp.float32
    dma = pltpu.SemaphoreType.DMA
    here, features = queries.shape
    heads = features // HEAD_DIM
    both = pl.pallas_call(
        kernel,
        out_shape=jax.ShapeDtypeStruct((2, *queries.shape), bf16),
        in_specs=[anywhere] * 10,
        out_specs=anywhere,
        scratch_shapes=[
            pltpu.VMEM((here, features), bf16),
            pltpu.SMEM(block_order.shape, jnp.int32),
            pltpu.VMEM((1, here), jnp.int32),
            pltpu.VMEM((1, WIDTH), f32),
            pltpu.VMEM((EXPERTS, WIDTH), f32),
            pltpu.VMEM((here, features), bf16),
            pltpu.VMEM((here, features), bf16),
            pltpu.VMEM((PLANES, SIDE * SIDE, here, here), bf16),
            pltpu.VMEM((PLANES, 2, SIDE, SIDE, here, HEAD_DIM), bf16),
            pltpu.VMEM((heads, here, 1), f32),
            pltpu.VMEM((heads, here, 1), f32),
            pltpu.VMEM((heads, here, HEAD_DIM), f32),
            pltpu.VMEM((WIDTH, HID), bf16),
            pltpu.VMEM((WIDTH, HID), bf16),
            pltpu.VMEM((2, HID, UNIT_COLS), bf16),
            pltpu.VMEM((EXPERTS, CAP, CHUNK), bf16),
            pltpu.VMEM((PLANES, EXPERTS, CAP, CHUNK), bf16),
            pltpu.VMEM((PLANES, 2, GROUP, WIDTH), bf16),
            pltpu.VMEM((PLANES, 2, 2, GROUP, UNIT_COLS), bf16),
            pltpu.VMEM((PLANES, 2, 4, 2, HALF, UNIT_COLS), bf16),
            pltpu.VMEM((PLANES, 2, 4, 2, 2, HALF, UNIT_COLS), bf16),
            pltpu.VMEM((PLANES, 2, 2, 2, HALF, UNIT_COLS // 2), bf16),
            pltpu.VMEM((PLANES, 2, 2, 2, HALF, UNIT_COLS), bf16),
            pltpu.VMEM((PLANES, 2, EXPERTS // 2, CAP, CHUNK), bf16),
            pltpu.VMEM((PLANES, EXPERTS, CAP, CHUNK), bf16),
            pltpu.VMEM((2, GROUP, HID), f32),
            pltpu.VMEM((GROUP, HID), bf16),
            dma((11,)),
            dma((3,)),
            dma((4,)),
            dma((13,)),
            dma((2,)),
            dma((3,)),
            dma((4,)),
            dma((PLANES, 9)),
            dma((4,)),
            dma((5, 10)),
            dma((2,)),
            dma((2,)),
        ],
        compiler_params=pltpu.CompilerParams(
            collective_id=1, has_side_effects=True, vmem_limit_bytes=62 << 20
        ),
        name="layer",
    )(
        queries,
        keys,
        values,
        block_order,
        routes.reshape(1, -1),
        norm_gain.reshape(1, -1),
        router.T,
        w_gate[0],
        w_up[0],
        w_down[0],
    )
    return both[0], both[1]


def solution(mesh):
    in_specs = (
        P("ctx", "exp"),
        P("ctx", "exp"),
        P("ctx", "exp"),
        P(),
        P("ctx", None),
        P(),
        P(),
        P("exp", None, "ctx"),
        P("exp", None, "ctx"),
        P("exp", "ctx", None),
    )
    out_specs = (P("ctx", "exp"), P("ctx", "exp"))
    return jax.shard_map(
        per_device, mesh=mesh, in_specs=in_specs, out_specs=out_specs, check_vma=False
    )
```

```python
import functools
import math

import jax
import jax.numpy as jnp
from jax import lax
from jax.experimental import pallas as pl
from jax.experimental.pallas import tpu as pltpu
from jax.sharding import PartitionSpec as P

HEAD_DIM = 128
CAP = 32
MESH = pl.DeviceIdType.MESH

PLANES = 2
SIDE = 4
EXPERTS = 8
WIDTH = 5120
CHUNK = WIDTH // EXPERTS
HALF = CAP // 2
PIECE_COLS = WIDTH // 2
UNIT_COLS = WIDTH // 2
GROUP = SIDE * SIDE * HALF
HID = 256


def mod4(v):
    return lax.rem(v + 2 * SIDE, SIDE)


OFFS = (0, -1, 1, 2)
OPPOSITE = ((0, 0), (1, 1), (2, 1), (3, 0))

HANDED = (0, 1)


class Gather:
    def __init__(self, whole, tori, piece, half, rows, ssem, rsem, send, arrived):
        self.whole = whole
        self.tori, self.piece, self.half, self.rows = tori, piece, half, rows
        self.ssem, self.rsem, self.send, self.arrived = ssem, rsem, send, arrived

    def second(self, t, i):
        piece = self.piece(t, OFFS[i], 0)
        for s, dq in ((0, 1), (1, -1)):
            r = 4 + i if s == OPPOSITE[i][1] and (self.whole or i not in HANDED) else 8
            self.send(piece, piece, self.ssem.at[2], self.rsem.at[r], t.dev(0, dq))

    def start(self, t):
        piece = self.piece(t, 0, 0)
        for dp in (1, -1):
            self.send(piece, piece, self.ssem.at[0], self.rsem.at[t.h], t.dev(dp, 0))
        self.second(t, 0)

    def near(self):
        for t in self.tori:
            self.arrived(self.rows(2), self.rsem.at[t.h])
            for s, dp in ((0, -1), (1, 1)):
                half = self.half(t, dp, 0, s)
                self.send(half, half, self.ssem.at[1], self.rsem.at[2 + t.h], t.dev(-dp, 0))
        for t in self.tori:
            self.second(t, 1)
            self.second(t, 2)

    def far(self):
        for t in self.tori:
            self.arrived(self.rows(1), self.rsem.at[2 + t.h])
            self.second(t, 3)

    def forward(self, i):
        dq = 1 if OPPOSITE[i][1] == 0 else -1
        if i in HANDED and not self.whole:
            return
        self.arrived(self.rows(2), self.rsem.at[4 + i])
        for t in self.tori:
            piece = self.piece(t, OFFS[i], -dq)
            self.send(piece, piece, self.ssem.at[3], self.rsem.at[9 if i in HANDED else 8], t.dev(0, dq))

    def handed(self):
        self.arrived(self.rows(2 * len(HANDED)), self.rsem.at[9])

    def done(self):
        self.arrived(self.rows(16 - 2 * len(HANDED) if self.whole else 16), self.rsem.at[8])


class Torus:
    def __init__(self, h, plane, y, x, e):
        self.h, self.plane, self.y, self.x, self.e = h, plane, y, x, e

    def at(self, dp, dq):
        if self.h == 0:
            return mod4(self.y + dq), mod4(self.x + dp)
        return mod4(self.y + dp), mod4(self.x + dq)

    def rows(self, dp, dq):
        y, x = self.at(dp, dq)
        return pl.ds(pl.multiple_of((y * SIDE + x) * HALF, HALF), HALF)

    def line(self, dq):
        return mod4((self.y if self.h == 0 else self.x) + dq)

    def along(self, dp):
        return mod4((self.x if self.h == 0 else self.y) + dp)

    def dev(self, dp, dq):
        y, x = self.at(dp, dq)
        return (self.plane * SIDE * SIDE + y * SIDE + x, self.e)


def kernel(
    q_hbm,
    k_hbm,
    v_hbm,
    order_hbm,
    routes_hbm,
    gain_hbm,
    router_hbm,
    wg_hbm,
    wu_hbm,
    wd_hbm,
    both_hbm,
    q_ref,
    order_ref,
    routes_ref,
    gain_ref,
    router_ref,
    att_ref,
    out_ref,
    hidden_keys,
    kv,
    soft_max,
    soft_sum,
    soft_acc,
    wg,
    wu,
    wd,
    pack,
    xin,
    g,
    part,
    ru1,
    ru2,
    rv1,
    rv2,
    fin,
    ret,
    acc,
    hid,
    in_sem,
    w_sem,
    kv_s,
    kv_r,
    a2a_s,
    a2a_r,
    ag_s,
    ag_r,
    rs_s,
    rs_r,
    back_s,
    back_r,
):
    ctx = lax.axis_index("ctx")
    e = lax.axis_index("exp")
    plane = ctx // (SIDE * SIDE)
    other = 1 - plane
    spot = lax.rem(ctx, SIDE * SIDE)
    y, x = spot // SIDE, lax.rem(spot, SIDE)
    tori = [Torus(h, plane, y, x, e) for h in range(2)]
    planes = (plane, other)

    def send(src, dst, ssem, rsem, dev):
        copy = pltpu.make_async_remote_copy(
            src_ref=src, dst_ref=dst, send_sem=ssem, recv_sem=rsem, device_id=dev, device_id_type=MESH
        )
        copy.start()

    def arrived(ref, rsem):
        pltpu.make_async_remote_copy(
            src_ref=ref, dst_ref=ref, send_sem=rsem, recv_sem=rsem, device_id=tori[0].dev(1, 0), device_id_type=MESH
        ).wait_recv()

    def all_sent(ref, ssem):
        pltpu.make_async_remote_copy(
            src_ref=ref, dst_ref=ref, send_sem=ssem, recv_sem=ssem, device_id=tori[0].dev(1, 0), device_id_type=MESH
        ).wait_send()

    def column(pl_index, d):
        return (pl_index * SIDE * SIDE + spot, lax.rem(e + d, EXPERTS))

    barrier = pltpu.get_barrier_semaphore()
    partners = [column(plane, d) for d in range(1, EXPERTS)]
    partners += [column(other, d) for d in range(EXPERTS)]
    partners += [tori[0].dev(k, 0) for k in (1, -1, 2)] + [tori[0].dev(0, k) for k in (1, -1, 2)]
    for dev in partners:
        pl.semaphore_signal(barrier, inc=1, device_id=dev, device_id_type=MESH)

    inputs = [
        pltpu.make_async_copy(src, dst, in_sem.at[i])
        for i, (src, dst) in enumerate(
            (
                (order_hbm, order_ref),
                (routes_hbm, routes_ref),
                (k_hbm, kv.at[0, 0, tori[0].line(0), tori[0].along(0)]),
                (v_hbm, kv.at[0, 1, tori[1].line(0), tori[1].along(0)]),
                (q_hbm, q_ref),
                (gain_hbm, gain_ref),
                (router_hbm, router_ref),
            )
        )
    ]
    for copy in inputs:
        copy.start()
    loads = [
        pltpu.make_async_copy(wg_hbm, wg, w_sem.at[0]),
        pltpu.make_async_copy(wu_hbm, wu, w_sem.at[1]),
    ]
    distances = ((1, 2), (3, 0))

    def receiver(f, k):
        return lax.rem(e // 2 + distances[f][k // 2], EXPERTS // 2) * 2 + lax.rem(e + k, 2)

    for f in range(2):
        for k in range(EXPERTS // 2):
            cols = pl.ds(pl.multiple_of(receiver(f, k) * CHUNK, CHUNK), CHUNK)
            loads.append(
                pltpu.make_async_copy(wd_hbm.at[:, cols], wd.at[f, :, pl.ds(k * CHUNK, CHUNK)], w_sem.at[2])
            )
    for load in loads:
        load.start()
    inputs[0].wait()
    inputs[1].wait()

    n = n_rows = att_ref.shape[0]
    onehot = (lax.broadcasted_iota(jnp.int32, (EXPERTS, n_rows), 0) == routes_ref[...]).astype(jnp.float32)
    before = (
        lax.broadcasted_iota(jnp.int32, (n_rows, n_rows), 0)
        < lax.broadcasted_iota(jnp.int32, (n_rows, n_rows), 1)
    ).astype(jnp.bfloat16)
    earlier = jnp.dot(onehot.astype(jnp.bfloat16), before, preferred_element_type=jnp.float32)
    code = jnp.sum(onehot * earlier, axis=0, keepdims=True).astype(jnp.int32) + routes_ref[...] * CAP
    placing = (lax.broadcasted_iota(jnp.int32, (EXPERTS * CAP, n_rows), 0) == code).astype(jnp.bfloat16)


    half_n = n // 2

    def positions(c, shape, dim):
        i = lax.broadcasted_iota(jnp.int32, shape, dim)
        return i + jnp.where(i < half_n, order_ref[2 * c] * half_n, (order_ref[2 * c + 1] - 1) * half_n)

    query_pos = positions(ctx, (1, n), 1)
    for w in range(PLANES):

        @pl.loop(0, SIDE * SIDE)
        def _(i):
            kept = positions(planes[w] * SIDE * SIDE + i, (n, 1), 0) <= query_pos
            hidden_keys[w, i] = jnp.where(kept, 0.0, -1e30).astype(jnp.bfloat16)

    for copy in inputs[2:]:
        copy.wait()
    pl.semaphore_wait(barrier, len(partners))

    for t in tori:
        piece = (t.h, t.line(0), t.along(0))
        send(kv.at[0, *piece], kv.at[1, *piece], kv_s.at[0], kv_r.at[8], column(other, 0))

    def kv_near(w):
        for d in (1, -1, 2):
            for t in tori:
                piece = kv.at[w, t.h, t.line(0), t.along(0)]
                send(piece, piece, kv_s.at[1], kv_r.at[4 * w + t.h], t.dev(d, 0))

    def kv_far(w):
        for t in tori:
            arrived(kv.at[w, t.h, 0, pl.ds(0, SIDE - 1)], kv_r.at[4 * w + t.h])
            line = kv.at[w, t.h, t.line(0)]
            for d in (1, -1):
                send(line, line, kv_s.at[2], kv_r.at[4 * w + 2 + t.h], t.dev(0, d))

    def kv_forward(w):
        for t in tori:
            arrived(kv.at[w, t.h, pl.ds(0, 2)], kv_r.at[4 * w + 2 + t.h])
            for s, d in ((0, 1), (1, -1)):
                half = kv.at[w, t.h, t.line(-d), pl.ds(2 * s, 2)]
                send(half, half, kv_s.at[3], kv_r.at[9 + 2 * w + t.h], t.dev(0, d))

    def kv_done(w):
        for t in tori:
            arrived(kv.at[w, t.h, 0], kv_r.at[9 + 2 * w + t.h])

    scale = math.log2(math.e) / math.sqrt(HEAD_DIM)
    heads = q_ref.shape[1] // HEAD_DIM
    each = (
        lax.broadcasted_iota(jnp.int32, (n, n), 0) == lax.broadcasted_iota(jnp.int32, (n, n), 1)
    ).astype(jnp.bfloat16)

    def attend(w, blocks, first=False, last=False):
        places = [(mod4(y + dy), mod4(x + dx)) for dy, dx in blocks]
        keys = jnp.concatenate([kv[w, 0, r, i] for r, i in places], axis=0)
        values = jnp.concatenate([kv[w, 1, i, r] for r, i in places], axis=0)
        hide = jnp.concatenate([hidden_keys[w, r * SIDE + i] for r, i in places], axis=0)
        keys = jnp.concatenate([keys, hide], axis=1)
        for head in range(heads):
            q = jnp.concatenate([q_ref[:, pl.ds(head * HEAD_DIM, HEAD_DIM)], each], axis=1)
            scores = lax.dot_general(q, keys, (((1,), (1,)), ((), ())), preferred_element_type=jnp.float32)
            new = jnp.max(scores, axis=1, keepdims=True)
            if not first:
                old = soft_max[head]
                new = jnp.maximum(old, new)
                fade = jnp.exp2((old - new) * scale)
            probs = jnp.exp2(scores * scale - new * scale)
            total = jnp.sum(probs, axis=1, keepdims=True)
            mixed = jnp.dot(probs.astype(jnp.bfloat16), values, preferred_element_type=jnp.float32)
            if not first:
                total = total + soft_sum[head] * fade
                mixed = mixed + soft_acc[head] * fade
            if last:
                att_ref[:, pl.ds(head * HEAD_DIM, HEAD_DIM)] = (mixed / total).astype(jnp.bfloat16)
            else:
                soft_max[head] = new
                soft_sum[head] = total
                soft_acc[head] = mixed

    everyone = [(dy, dx) for dy in range(SIDE) for dx in range(SIDE)]
    close = [(dy, dx) for dy, dx in everyone if dy != 2 and dx != 2]
    distant = [block for block in everyone if block not in close]

    kv_near(0)
    kv_far(0)
    arrived(kv.at[1, 0, 0, pl.ds(0, 2)], kv_r.at[8])
    kv_near(1)
    kv_forward(0)
    attend(0, close, first=True)
    kv_far(1)
    kv_done(0)
    attend(0, distant)
    kv_forward(1)
    attend(1, close)
    kv_done(1)
    attend(1, distant, last=True)

    attended = pltpu.make_async_copy(att_ref, both_hbm.at[0], in_sem.at[7])
    attended.start()

    packed = jnp.dot(placing, att_ref[...], preferred_element_type=jnp.float32).astype(jnp.bfloat16)
    pack[...] = packed.reshape(EXPERTS, CAP, CHUNK)

    def dispatch(w, first, count):
        rows = pl.ds(first, count)
        h = first // HALF
        for d in range(1 - w, EXPERTS):
            to = lax.rem(e + d, EXPERTS)
            send(
                pack.at[to, rows], xin.at[w, e, rows], a2a_s.at[w], a2a_r.at[2 * w + h], column(planes[w], d)
            )

    dispatch(0, 0, HALF)
    dispatch(0, HALF, HALF)
    own = pltpu.make_async_copy(pack.at[e], xin.at[0, e], in_sem.at[9])
    own.start()

    def norm(w, first, count):
        rows = pl.ds(first, count)
        arrived(xin.at[w, pl.ds(0, EXPERTS - 1 + w), rows], a2a_r.at[2 * w + first // HALF])
        if w == 0 and first == 0:
            own.wait()
        squares = jnp.zeros((count, 1), jnp.float32)
        for j in range(EXPERTS):
            v = xin[w, j, rows].astype(jnp.float32)
            squares += jnp.sum(v * v, axis=1, keepdims=True)
        inverse = lax.rsqrt(squares / WIDTH + 1e-05)
        mine = lax.broadcasted_iota(jnp.int32, (EXPERTS, CHUNK), 0) == e
        logit = jnp.zeros((count, 1), jnp.float32)
        for j in range(EXPERTS):
            cols = pl.ds(j * CHUNK, CHUNK)
            v = xin[w, j, rows].astype(jnp.float32) * inverse * gain_ref[:, cols]
            weight = jnp.sum(jnp.where(mine, router_ref[:, cols], 0.0), axis=0, keepdims=True)
            logit += jnp.sum(v * weight, axis=1, keepdims=True)
        gate = 1.0 / (1.0 + jnp.exp(-logit))
        for j in range(EXPERTS):
            cols = pl.ds(j * CHUNK, CHUNK)
            v = xin[w, j, rows].astype(jnp.float32) * inverse * gain_ref[:, cols]
            v = (v * gate).astype(jnp.bfloat16)
            for k in range(count // HALF):
                g[w, first // HALF + k, tori[0].rows(0, 0), cols] = v[k * HALF : (k + 1) * HALF]


    gather = [
        Gather(
            w == 0,
            tori,
            lambda t, dp, dq, w=w: g.at[w, t.h, t.rows(dp, dq)],
            lambda t, dp, dq, s, w=w: g.at[w, t.h, t.rows(dp, dq), pl.ds(s * PIECE_COLS, PIECE_COLS)],
            lambda k, w=w: g.at[w, 0, pl.ds(0, k * HALF)],
            ag_s,
            ag_r.at[w],
            send,
            arrived,
        )
        for w in range(PLANES)
    ]

    def hand_over():
        gather[0].handed()
        for i in HANDED:
            for t in tori:
                rows = t.rows(OFFS[i], 2)
                send(g.at[0, t.h, rows], g.at[1, t.h, rows], ag_s.at[4], ag_r.at[1, 9], column(other, 0))

    def ffn(w, h):
        step = 1280
        acc[...] = jnp.zeros_like(acc)

        @pl.loop(0, WIDTH // step)
        def _(k):
            cols = pl.ds(pl.multiple_of(k * step, step), step)
            rows = g[w, h, :, cols]
            acc[0] += jnp.dot(rows, wg[cols, :], preferred_element_type=jnp.float32)
            acc[1] += jnp.dot(rows, wu[cols, :], preferred_element_type=jnp.float32)

        v = acc[0]
        hid[...] = (v / (1.0 + jnp.exp(-v)) * acc[1]).astype(jnp.bfloat16)
        wide = 512

        @pl.loop(0, UNIT_COLS // wide)
        def _(k):
            cols = pl.ds(pl.multiple_of(k * wide, wide), wide)
            for f in range(2):
                part[w, f, h, :, cols] = jnp.dot(
                    hid[...], wd[f, :, cols], preferred_element_type=jnp.float32
                ).astype(jnp.bfloat16)

    def add(ref, *more):
        total = ref[...].astype(jnp.float32)
        for m in more:
            total = total + m[...].astype(jnp.float32)
        ref[...] = total.astype(jnp.bfloat16)

    mine = pltpu.make_async_copy(fin.at[0, 0, e // 2], ret.at[0, e], in_sem.at[10])

    class Unit:
        def __init__(self, n, w, f, chunks):
            self.n, self.w, self.f, self.chunks = n, w, f, chunks
            self.first, self.count = chunks[0] * CHUNK, len(chunks) * CHUNK
            self.cols = pl.ds(self.first, self.count)

        def part(self, t, dp, dq):
            return part.at[self.w, self.f, t.h, t.rows(dp, dq), self.cols]

        def half_part(self, t, dp, s):
            half = self.count // 2
            return part.at[self.w, self.f, t.h, t.rows(dp, 0), pl.ds(self.first + s * half, half)]

        def via(self, i, h):
            return ru1.at[self.w, self.f, i, h, :, self.cols]

        def second(self, i, s, h):
            return ru2.at[self.w, self.f, i, s, h, :, self.cols]

        def half_via(self, h, s):
            return rv1.at[self.w, self.f, h, s, :, pl.ds(self.first // 2, self.count // 2)]

        def first_axis(self, h, s):
            return rv2.at[self.w, self.f, h, s, :, self.cols]

        def sem(self, k):
            return rs_r.at[self.n, k]

    both = slice(None)

    def rs_begin(u):
        for t in tori:
            for i, s in OPPOSITE:
                send(u.part(t, OFFS[i], 2), u.via(i, t.h), rs_s.at[0], u.sem(i), t.dev(0, 1 if s == 0 else -1))
        for t in tori:
            for i, s in OPPOSITE:
                rs_second(u, t, i, 1 - s)

    def rs_second(u, t, i, s):
        dq = 1 if s == 0 else -1
        send(u.part(t, OFFS[i], dq), u.second(i, s, t.h), rs_s.at[1], u.sem(4 + i), t.dev(0, dq))

    def rs_join(u):
        for i, s in OPPOSITE:
            arrived(u.via(i, both), u.sem(i))
            for t in tori:
                add(u.part(t, OFFS[i], 1 if s == 0 else -1), u.via(i, t.h))
                rs_second(u, t, i, s)

    def rs_sum(u, i):
        arrived(u.second(i, both, both), u.sem(4 + i))
        for t in tori:
            add(u.part(t, OFFS[i], 0), u.second(i, 0, t.h), u.second(i, 1, t.h))

    def rs_turn(u):
        rs_sum(u, 3)
        for t in tori:
            for s, dp in ((0, 1), (1, -1)):
                send(u.half_part(t, 2, s), u.half_via(t.h, s), rs_s.at[2], u.sem(8), t.dev(dp, 0))
        rs_sum(u, 1)
        rs_sum(u, 2)

    def rs_last(u):
        arrived(u.half_via(both, both), u.sem(8))
        for t in tori:
            for s, dp in ((0, 1), (1, -1)):
                add(u.half_part(t, dp, s), u.half_via(t.h, s))
                send(u.part(t, dp, 0), u.first_axis(t.h, s), rs_s.at[3], u.sem(9), t.dev(dp, 0))
        rs_sum(u, 0)

    mine = pltpu.make_async_copy(fin.at[0, 1, 2], ret.at[0, e], in_sem.at[10])

    def rs_finish(u):
        arrived(u.first_axis(both, both), u.sem(9))
        w, f = u.w, u.f
        for k in u.chunks:
            cols = pl.ds(k * CHUNK, CHUNK)
            for t in tori:
                total = part[w, f, t.h, t.rows(0, 0), cols].astype(jnp.float32)
                for s in range(2):
                    total = total + rv2[w, f, t.h, s, :, cols].astype(jnp.float32)
                fin[w, f, k, pl.ds(t.h * HALF, HALF)] = total.astype(jnp.bfloat16)
            if (w, f, k) == (0, 1, 2):
                mine.start()
            else:
                to = receiver(f, k)
                dev = (planes[w] * SIDE * SIDE + spot, to)
                send(fin.at[w, f, k], ret.at[w, e], back_s.at[w], back_r.at[w], dev)

    a, b, c = Unit(0, 0, 0, range(4)), Unit(1, 1, 0, range(4)), Unit(2, 1, 1, range(4))
    p, q = Unit(3, 0, 1, range(2)), Unit(4, 0, 1, range(2, 4))

    for t in tori:
        norm(0, t.h * HALF, HALF)
        gather[0].start(t)
    dispatch(1, 0, CAP)
    gather[0].near()
    gather[0].far()
    gather[0].forward(0)
    gather[0].forward(1)
    norm(1, 0, CAP)
    for t in tori:
        gather[1].start(t)
    gather[0].forward(2)
    gather[0].forward(3)
    hand_over()
    gather[1].near()
    gather[1].far()
    loads[0].wait()
    loads[1].wait()
    pltpu.make_async_copy(wd, wd, w_sem.at[2]).wait()
    gather[0].done()
    gather[1].forward(0)
    gather[1].forward(1)
    ffn(0, 0)
    gather[1].forward(2)
    gather[1].forward(3)
    ffn(0, 1)
    rs_begin(a)
    rs_begin(p)
    gather[1].done()
    gather[1].handed()
    rs_join(a)
    ffn(1, 0)
    ffn(1, 1)
    rs_begin(b)
    rs_turn(a)
    rs_join(b)
    rs_begin(c)
    rs_last(a)
    rs_turn(b)
    rs_finish(a)
    rs_join(c)
    rs_join(p)
    rs_begin(q)
    rs_last(b)
    rs_turn(c)
    rs_finish(b)
    rs_turn(p)
    rs_last(c)
    rs_join(q)
    rs_last(p)
    rs_finish(c)
    rs_turn(q)
    rs_finish(p)
    rs_last(q)
    rs_finish(q)

    routed = None
    for w in range(PLANES):
        arrived(ret.at[w, pl.ds(0, EXPERTS - 1 + w)], back_r.at[w])
        if w == 0:
            mine.wait()
        rows = ret[w].reshape(EXPERTS * CAP, CHUNK)
        term = lax.dot_general(
            placing, rows, (((0,), (0,)), ((), ())), preferred_element_type=jnp.float32
        )
        routed = term if routed is None else routed + term
    out_ref[...] = routed.astype(jnp.bfloat16)
    result = pltpu.make_async_copy(out_ref, both_hbm.at[1], in_sem.at[8])
    result.start()
    attended.wait()
    result.wait()
    all_sent(kv.at[0, 0, 0, pl.ds(0, 2)], kv_s.at[0])
    all_sent(kv.at[0, 0, pl.ds(0, SIDE - 1)], kv_s.at[1])
    all_sent(kv.at[:, :, pl.ds(0, 2)], kv_s.at[2])
    all_sent(kv.at[:, :, 0], kv_s.at[3])
    all_sent(xin.at[0, pl.ds(0, EXPERTS - 1)], a2a_s.at[0])
    all_sent(xin.at[1], a2a_s.at[1])
    all_sent(g.at[0, 0, pl.ds(0, 8 * HALF)], ag_s.at[0])
    all_sent(g.at[0, 0, pl.ds(0, 4 * HALF)], ag_s.at[1])
    all_sent(g.at[0], ag_s.at[2])
    all_sent(g.at[0, 0, pl.ds(0, (16 - 2 * len(HANDED)) * HALF)], ag_s.at[3])
    all_sent(g.at[0, 0, pl.ds(0, 2 * len(HANDED) * HALF)], ag_s.at[4])
    for i, ref in enumerate((ru1, ru2, rv1, rv2)):
        all_sent(ref, rs_s.at[i])
    all_sent(ret.at[0, pl.ds(0, EXPERTS - 1)], back_s.at[0])
    all_sent(ret.at[1], back_s.at[1])


def per_device(queries, keys, values, block_order, routes, norm_gain, router, w_gate, w_up, w_down):
    anywhere = pl.BlockSpec(memory_space=pl.ANY)
    bf16, f32 = jnp.bfloat16, jnp.float32
    dma = pltpu.SemaphoreType.DMA
    here, features = queries.shape
    heads = features // HEAD_DIM
    both = pl.pallas_call(
        kernel,
        out_shape=jax.ShapeDtypeStruct((2, *queries.shape), bf16),
        in_specs=[anywhere] * 10,
        out_specs=anywhere,
        scratch_shapes=[
            pltpu.VMEM((here, features), bf16),
            pltpu.SMEM(block_order.shape, jnp.int32),
            pltpu.VMEM((1, here), jnp.int32),
            pltpu.VMEM((1, WIDTH), f32),
            pltpu.VMEM((EXPERTS, WIDTH), f32),
            pltpu.VMEM((here, features), bf16),
            pltpu.VMEM((here, features), bf16),
            pltpu.VMEM((PLANES, SIDE * SIDE, here, here), bf16),
            pltpu.VMEM((PLANES, 2, SIDE, SIDE, here, HEAD_DIM), bf16),
            pltpu.VMEM((heads, here, 1), f32),
            pltpu.VMEM((heads, here, 1), f32),
            pltpu.VMEM((heads, here, HEAD_DIM), f32),
            pltpu.VMEM((WIDTH, HID), bf16),
            pltpu.VMEM((WIDTH, HID), bf16),
            pltpu.VMEM((2, HID, UNIT_COLS), bf16),
            pltpu.VMEM((EXPERTS, CAP, CHUNK), bf16),
            pltpu.VMEM((PLANES, EXPERTS, CAP, CHUNK), bf16),
            pltpu.VMEM((PLANES, 2, GROUP, WIDTH), bf16),
            pltpu.VMEM((PLANES, 2, 2, GROUP, UNIT_COLS), bf16),
            pltpu.VMEM((PLANES, 2, 4, 2, HALF, UNIT_COLS), bf16),
            pltpu.VMEM((PLANES, 2, 4, 2, 2, HALF, UNIT_COLS), bf16),
            pltpu.VMEM((PLANES, 2, 2, 2, HALF, UNIT_COLS // 2), bf16),
            pltpu.VMEM((PLANES, 2, 2, 2, HALF, UNIT_COLS), bf16),
            pltpu.VMEM((PLANES, 2, EXPERTS // 2, CAP, CHUNK), bf16),
            pltpu.VMEM((PLANES, EXPERTS, CAP, CHUNK), bf16),
            pltpu.VMEM((2, GROUP, HID), f32),
            pltpu.VMEM((GROUP, HID), bf16),
            dma((11,)),
            dma((3,)),
            dma((4,)),
            dma((13,)),
            dma((2,)),
            dma((3,)),
            dma((5,)),
            dma((PLANES, 10)),
            dma((4,)),
            dma((5, 10)),
            dma((2,)),
            dma((2,)),
        ],
        compiler_params=pltpu.CompilerParams(
            collective_id=1, has_side_effects=True, vmem_limit_bytes=62 << 20
        ),
        name="layer",
    )(
        queries,
        keys,
        values,
        block_order,
        routes.reshape(1, -1),
        norm_gain.reshape(1, -1),
        router.T,
        w_gate[0],
        w_up[0],
        w_down[0],
    )
    return both[0], both[1]


def solution(mesh):
    in_specs = (
        P("ctx", "exp"),
        P("ctx", "exp"),
        P("ctx", "exp"),
        P(),
        P("ctx", None),
        P(),
        P(),
        P("exp", None, "ctx"),
        P("exp", None, "ctx"),
        P("exp", "ctx", None),
    )
    out_specs = (P("ctx", "exp"), P("ctx", "exp"))
    return jax.shard_map(
        per_device, mesh=mesh, in_specs=in_specs, out_specs=out_specs, check_vma=False
    )
```

```python
import functools
import math

import jax
import jax.numpy as jnp
from jax import lax
from jax.experimental import pallas as pl
from jax.experimental.pallas import tpu as pltpu
from jax.sharding import PartitionSpec as P

HEAD_DIM = 128
CAP = 32
MESH = pl.DeviceIdType.MESH

PLANES = 2
SIDE = 4
EXPERTS = 8
WIDTH = 5120
CHUNK = WIDTH // EXPERTS
HALF = CAP // 2
PIECE_COLS = WIDTH // 2
UNIT_COLS = WIDTH // 2
GROUP = SIDE * SIDE * HALF
HID = 256


def mod4(v):
    return lax.rem(v + 2 * SIDE, SIDE)


OFFS = (0, -1, 1, 2)
OPPOSITE = ((0, 0), (1, 1), (2, 1), (3, 0))

HANDED = (0, 1)


class Gather:
    def __init__(self, whole, tori, piece, half, rows, ssem, rsem, send, arrived):
        self.whole = whole
        self.tori, self.piece, self.half, self.rows = tori, piece, half, rows
        self.ssem, self.rsem, self.send, self.arrived = ssem, rsem, send, arrived

    def second(self, t, i):
        piece = self.piece(t, OFFS[i], 0)
        for s, dq in ((0, 1), (1, -1)):
            r = 4 + i if s == OPPOSITE[i][1] and (self.whole or i not in HANDED) else 8
            self.send(piece, piece, self.ssem.at[2], self.rsem.at[r], t.dev(0, dq))

    def start(self, t):
        piece = self.piece(t, 0, 0)
        for dp in (1, -1):
            self.send(piece, piece, self.ssem.at[0], self.rsem.at[t.h], t.dev(dp, 0))
        self.second(t, 0)

    def near(self):
        for t in self.tori:
            self.arrived(self.rows(2), self.rsem.at[t.h])
            for s, dp in ((0, -1), (1, 1)):
                half = self.half(t, dp, 0, s)
                self.send(half, half, self.ssem.at[1], self.rsem.at[2 + t.h], t.dev(-dp, 0))
        for t in self.tori:
            self.second(t, 1)
            self.second(t, 2)

    def far(self):
        for t in self.tori:
            self.arrived(self.rows(1), self.rsem.at[2 + t.h])
            self.second(t, 3)

    def forward(self, i):
        dq = 1 if OPPOSITE[i][1] == 0 else -1
        if i in HANDED and not self.whole:
            return
        self.arrived(self.rows(2), self.rsem.at[4 + i])
        for t in self.tori:
            piece = self.piece(t, OFFS[i], -dq)
            self.send(piece, piece, self.ssem.at[3], self.rsem.at[9 if i in HANDED else 8], t.dev(0, dq))

    def handed(self):
        self.arrived(self.rows(2 * len(HANDED)), self.rsem.at[9])

    def done(self):
        self.arrived(self.rows(16 - 2 * len(HANDED) if self.whole else 16), self.rsem.at[8])


class Torus:
    def __init__(self, h, plane, y, x, e):
        self.h, self.plane, self.y, self.x, self.e = h, plane, y, x, e

    def at(self, dp, dq):
        if self.h == 0:
            return mod4(self.y + dq), mod4(self.x + dp)
        return mod4(self.y + dp), mod4(self.x + dq)

    def rows(self, dp, dq):
        y, x = self.at(dp, dq)
        return pl.ds(pl.multiple_of((y * SIDE + x) * HALF, HALF), HALF)

    def line(self, dq):
        return mod4((self.y if self.h == 0 else self.x) + dq)

    def along(self, dp):
        return mod4((self.x if self.h == 0 else self.y) + dp)

    def dev(self, dp, dq):
        y, x = self.at(dp, dq)
        return (self.plane * SIDE * SIDE + y * SIDE + x, self.e)


def kernel(
    q_hbm,
    k_hbm,
    v_hbm,
    order_hbm,
    routes_hbm,
    gain_hbm,
    router_hbm,
    wg_hbm,
    wu_hbm,
    wd_hbm,
    both_hbm,
    q_ref,
    order_ref,
    routes_ref,
    gain_ref,
    router_ref,
    att_ref,
    out_ref,
    hidden_keys,
    kv,
    soft_max,
    soft_sum,
    soft_acc,
    wg,
    wu,
    wd,
    pack,
    xin,
    g,
    part,
    ru1,
    ru2,
    rv1,
    rv2,
    fin,
    ret,
    acc,
    hid,
    in_sem,
    w_sem,
    kv_s,
    kv_r,
    a2a_s,
    a2a_r,
    ag_s,
    ag_r,
    rs_s,
    rs_r,
    back_s,
    back_r,
):
    ctx = lax.axis_index("ctx")
    e = lax.axis_index("exp")
    plane = ctx // (SIDE * SIDE)
    other = 1 - plane
    spot = lax.rem(ctx, SIDE * SIDE)
    y, x = spot // SIDE, lax.rem(spot, SIDE)
    tori = [Torus(h, plane, y, x, e) for h in range(2)]
    planes = (plane, other)

    def send(src, dst, ssem, rsem, dev):
        copy = pltpu.make_async_remote_copy(
            src_ref=src, dst_ref=dst, send_sem=ssem, recv_sem=rsem, device_id=dev, device_id_type=MESH
        )
        copy.start()

    def arrived(ref, rsem):
        pltpu.make_async_remote_copy(
            src_ref=ref, dst_ref=ref, send_sem=rsem, recv_sem=rsem, device_id=tori[0].dev(1, 0), device_id_type=MESH
        ).wait_recv()

    def all_sent(ref, ssem):
        pltpu.make_async_remote_copy(
            src_ref=ref, dst_ref=ref, send_sem=ssem, recv_sem=ssem, device_id=tori[0].dev(1, 0), device_id_type=MESH
        ).wait_send()

    def column(pl_index, d):
        return (pl_index * SIDE * SIDE + spot, lax.rem(e + d, EXPERTS))

    barrier = pltpu.get_barrier_semaphore()
    partners = [column(plane, d) for d in range(1, EXPERTS)]
    partners += [column(other, d) for d in range(EXPERTS)]
    partners += [tori[0].dev(k, 0) for k in (1, -1, 2)] + [tori[0].dev(0, k) for k in (1, -1, 2)]
    for dev in partners:
        pl.semaphore_signal(barrier, inc=1, device_id=dev, device_id_type=MESH)

    inputs = [
        pltpu.make_async_copy(src, dst, in_sem.at[i])
        for i, (src, dst) in enumerate(
            (
                (order_hbm, order_ref),
                (routes_hbm, routes_ref),
                (k_hbm, kv.at[0, 0, tori[0].line(0), tori[0].along(0)]),
                (v_hbm, kv.at[0, 1, tori[1].line(0), tori[1].along(0)]),
                (q_hbm, q_ref),
                (gain_hbm, gain_ref),
                (router_hbm, router_ref),
            )
        )
    ]
    for copy in inputs:
        copy.start()
    loads = [
        pltpu.make_async_copy(wg_hbm, wg, w_sem.at[0]),
        pltpu.make_async_copy(wu_hbm, wu, w_sem.at[1]),
    ]
    distances = ((1, 2), (3, 0))

    def receiver(f, k):
        return lax.rem(e // 2 + distances[f][k // 2], EXPERTS // 2) * 2 + lax.rem(e + k, 2)

    for f in range(2):
        for k in range(EXPERTS // 2):
            cols = pl.ds(pl.multiple_of(receiver(f, k) * CHUNK, CHUNK), CHUNK)
            loads.append(
                pltpu.make_async_copy(wd_hbm.at[:, cols], wd.at[f, :, pl.ds(k * CHUNK, CHUNK)], w_sem.at[2])
            )
    for load in loads:
        load.start()
    inputs[0].wait()
    inputs[1].wait()

    n = n_rows = att_ref.shape[0]
    onehot = (lax.broadcasted_iota(jnp.int32, (EXPERTS, n_rows), 0) == routes_ref[...]).astype(jnp.float32)
    before = (
        lax.broadcasted_iota(jnp.int32, (n_rows, n_rows), 0)
        < lax.broadcasted_iota(jnp.int32, (n_rows, n_rows), 1)
    ).astype(jnp.bfloat16)
    earlier = jnp.dot(onehot.astype(jnp.bfloat16), before, preferred_element_type=jnp.float32)
    code = jnp.sum(onehot * earlier, axis=0, keepdims=True).astype(jnp.int32) + routes_ref[...] * CAP
    placing = (lax.broadcasted_iota(jnp.int32, (EXPERTS * CAP, n_rows), 0) == code).astype(jnp.bfloat16)


    half_n = n // 2

    def positions(c, shape, dim):
        i = lax.broadcasted_iota(jnp.int32, shape, dim)
        return i + jnp.where(i < half_n, order_ref[2 * c] * half_n, (order_ref[2 * c + 1] - 1) * half_n)

    query_pos = positions(ctx, (1, n), 1)
    for w in range(PLANES):

        @pl.loop(0, SIDE * SIDE)
        def _(i):
            kept = positions(planes[w] * SIDE * SIDE + i, (n, 1), 0) <= query_pos
            hidden_keys[w, i] = jnp.where(kept, 0.0, -1e30).astype(jnp.bfloat16)

    for copy in inputs[2:]:
        copy.wait()
    pl.semaphore_wait(barrier, len(partners))

    for t in tori:
        piece = (t.h, t.line(0), t.along(0))
        send(kv.at[0, *piece], kv.at[1, *piece], kv_s.at[0], kv_r.at[8], column(other, 0))

    def kv_near(w):
        for d in (1, -1, 2):
            for t in tori:
                piece = kv.at[w, t.h, t.line(0), t.along(0)]
                send(piece, piece, kv_s.at[1], kv_r.at[4 * w + t.h], t.dev(d, 0))

    def kv_far(w):
        for t in tori:
            arrived(kv.at[w, t.h, 0, pl.ds(0, SIDE - 1)], kv_r.at[4 * w + t.h])
            line = kv.at[w, t.h, t.line(0)]
            for d in (1, -1):
                send(line, line, kv_s.at[2], kv_r.at[4 * w + 2 + t.h], t.dev(0, d))

    def kv_forward(w):
        for t in tori:
            arrived(kv.at[w, t.h, pl.ds(0, 2)], kv_r.at[4 * w + 2 + t.h])
            for s, d in ((0, 1), (1, -1)):
                half = kv.at[w, t.h, t.line(-d), pl.ds(2 * s, 2)]
                send(half, half, kv_s.at[3], kv_r.at[9 + 2 * w + t.h], t.dev(0, d))

    def kv_done(w):
        for t in tori:
            arrived(kv.at[w, t.h, 0], kv_r.at[9 + 2 * w + t.h])

    scale = math.log2(math.e) / math.sqrt(HEAD_DIM)
    heads = q_ref.shape[1] // HEAD_DIM
    each = (
        lax.broadcasted_iota(jnp.int32, (n, n), 0) == lax.broadcasted_iota(jnp.int32, (n, n), 1)
    ).astype(jnp.bfloat16)

    def attend(w, blocks, first=False, last=False):
        places = [(mod4(y + dy), mod4(x + dx)) for dy, dx in blocks]
        keys = jnp.concatenate([kv[w, 0, r, i] for r, i in places], axis=0)
        values = jnp.concatenate([kv[w, 1, i, r] for r, i in places], axis=0)
        hide = jnp.concatenate([hidden_keys[w, r * SIDE + i] for r, i in places], axis=0)
        keys = jnp.concatenate([keys, hide], axis=1)
        for head in range(heads):
            q = jnp.concatenate([q_ref[:, pl.ds(head * HEAD_DIM, HEAD_DIM)], each], axis=1)
            scores = lax.dot_general(q, keys, (((1,), (1,)), ((), ())), preferred_element_type=jnp.float32)
            new = jnp.max(scores, axis=1, keepdims=True)
            if not first:
                old = soft_max[head]
                new = jnp.maximum(old, new)
                fade = jnp.exp2((old - new) * scale)
            probs = jnp.exp2(scores * scale - new * scale)
            total = jnp.sum(probs, axis=1, keepdims=True)
            mixed = jnp.dot(probs.astype(jnp.bfloat16), values, preferred_element_type=jnp.float32)
            if not first:
                total = total + soft_sum[head] * fade
                mixed = mixed + soft_acc[head] * fade
            if last:
                att_ref[:, pl.ds(head * HEAD_DIM, HEAD_DIM)] = (mixed / total).astype(jnp.bfloat16)
            else:
                soft_max[head] = new
                soft_sum[head] = total
                soft_acc[head] = mixed

    everyone = [(dy, dx) for dy in range(SIDE) for dx in range(SIDE)]
    close = [(dy, dx) for dy, dx in everyone if dy != 2 and dx != 2]
    distant = [block for block in everyone if block not in close]

    kv_near(0)
    kv_far(0)
    arrived(kv.at[1, 0, 0, pl.ds(0, 2)], kv_r.at[8])
    kv_near(1)
    kv_forward(0)
    attend(0, close, first=True)
    kv_far(1)
    kv_done(0)
    attend(0, distant)
    kv_forward(1)
    attend(1, close)
    kv_done(1)
    attend(1, distant, last=True)

    attended = pltpu.make_async_copy(att_ref, both_hbm.at[0], in_sem.at[7])
    attended.start()

    packed = jnp.dot(placing, att_ref[...], preferred_element_type=jnp.float32).astype(jnp.bfloat16)
    pack[...] = packed.reshape(EXPERTS, CAP, CHUNK)

    def dispatch(w, first, count):
        rows = pl.ds(first, count)
        h = first // HALF
        for d in range(1 - w, EXPERTS):
            to = lax.rem(e + d, EXPERTS)
            send(
                pack.at[to, rows], xin.at[w, e, rows], a2a_s.at[w], a2a_r.at[2 * w + h], column(planes[w], d)
            )

    dispatch(0, 0, HALF)
    dispatch(0, HALF, HALF)
    own = pltpu.make_async_copy(pack.at[e], xin.at[0, e], in_sem.at[9])
    own.start()

    def norm(w, first, count):
        rows = pl.ds(first, count)
        arrived(xin.at[w, pl.ds(0, EXPERTS - 1 + w), rows], a2a_r.at[2 * w + first // HALF])
        if w == 0 and first == 0:
            own.wait()
        squares = jnp.zeros((count, 1), jnp.float32)
        for j in range(EXPERTS):
            v = xin[w, j, rows].astype(jnp.float32)
            squares += jnp.sum(v * v, axis=1, keepdims=True)
        inverse = lax.rsqrt(squares / WIDTH + 1e-05)
        mine = lax.broadcasted_iota(jnp.int32, (EXPERTS, CHUNK), 0) == e
        logit = jnp.zeros((count, 1), jnp.float32)
        for j in range(EXPERTS):
            cols = pl.ds(j * CHUNK, CHUNK)
            v = xin[w, j, rows].astype(jnp.float32) * inverse * gain_ref[:, cols]
            weight = jnp.sum(jnp.where(mine, router_ref[:, cols], 0.0), axis=0, keepdims=True)
            logit += jnp.sum(v * weight, axis=1, keepdims=True)
        gate = 1.0 / (1.0 + jnp.exp(-logit))
        for j in range(EXPERTS):
            cols = pl.ds(j * CHUNK, CHUNK)
            v = xin[w, j, rows].astype(jnp.float32) * inverse * gain_ref[:, cols]
            v = (v * gate).astype(jnp.bfloat16)
            for k in range(count // HALF):
                g[w, first // HALF + k, tori[0].rows(0, 0), cols] = v[k * HALF : (k + 1) * HALF]


    gather = [
        Gather(
            w == 0,
            tori,
            lambda t, dp, dq, w=w: g.at[w, t.h, t.rows(dp, dq)],
            lambda t, dp, dq, s, w=w: g.at[w, t.h, t.rows(dp, dq), pl.ds(s * PIECE_COLS, PIECE_COLS)],
            lambda k, w=w: g.at[w, 0, pl.ds(0, k * HALF)],
            ag_s,
            ag_r.at[w],
            send,
            arrived,
        )
        for w in range(PLANES)
    ]

    def hand_over():
        gather[0].handed()
        for i in HANDED:
            for t in tori:
                rows = t.rows(OFFS[i], 2)
                send(g.at[0, t.h, rows], g.at[1, t.h, rows], ag_s.at[4], ag_r.at[1, 9], column(other, 0))

    def ffn(w, h):
        step = 1280
        acc[...] = jnp.zeros_like(acc)

        @pl.loop(0, WIDTH // step)
        def _(k):
            cols = pl.ds(pl.multiple_of(k * step, step), step)
            rows = g[w, h, :, cols]
            acc[0] += jnp.dot(rows, wg[cols, :], preferred_element_type=jnp.float32)
            acc[1] += jnp.dot(rows, wu[cols, :], preferred_element_type=jnp.float32)

        v = acc[0]
        hid[...] = (v / (1.0 + jnp.exp(-v)) * acc[1]).astype(jnp.bfloat16)
        wide = 512

        @pl.loop(0, UNIT_COLS // wide)
        def _(k):
            cols = pl.ds(pl.multiple_of(k * wide, wide), wide)
            for f in range(2):
                part[w, f, h, :, cols] = jnp.dot(
                    hid[...], wd[f, :, cols], preferred_element_type=jnp.float32
                ).astype(jnp.bfloat16)

    def add(ref, *more):
        total = ref[...].astype(jnp.float32)
        for m in more:
            total = total + m[...].astype(jnp.float32)
        ref[...] = total.astype(jnp.bfloat16)

    mine = pltpu.make_async_copy(fin.at[0, 0, e // 2], ret.at[0, e], in_sem.at[10])

    class Unit:
        def __init__(self, n, w, f, chunks):
            self.n, self.w, self.f, self.chunks = n, w, f, chunks
            self.first, self.count = chunks[0] * CHUNK, len(chunks) * CHUNK
            self.cols = pl.ds(self.first, self.count)

        def part(self, t, dp, dq):
            return part.at[self.w, self.f, t.h, t.rows(dp, dq), self.cols]

        def half_part(self, t, dp, s):
            half = self.count // 2
            return part.at[self.w, self.f, t.h, t.rows(dp, 0), pl.ds(self.first + s * half, half)]

        def via(self, i, h):
            return ru1.at[self.w, self.f, i, h, :, self.cols]

        def second(self, i, s, h):
            return ru2.at[self.w, self.f, i, s, h, :, self.cols]

        def half_via(self, h, s):
            return rv1.at[self.w, self.f, h, s, :, pl.ds(self.first // 2, self.count // 2)]

        def first_axis(self, h, s):
            return rv2.at[self.w, self.f, h, s, :, self.cols]

        def sem(self, k):
            return rs_r.at[self.n, k]

    both = slice(None)

    def rs_begin(u):
        for t in tori:
            for i, s in OPPOSITE:
                send(u.part(t, OFFS[i], 2), u.via(i, t.h), rs_s.at[0], u.sem(i), t.dev(0, 1 if s == 0 else -1))
        for t in tori:
            for i, s in OPPOSITE:
                rs_second(u, t, i, 1 - s)

    def rs_second(u, t, i, s):
        dq = 1 if s == 0 else -1
        send(u.part(t, OFFS[i], dq), u.second(i, s, t.h), rs_s.at[1], u.sem(4 + i), t.dev(0, dq))

    def rs_join(u):
        for i, s in OPPOSITE:
            arrived(u.via(i, both), u.sem(i))
            for t in tori:
                add(u.part(t, OFFS[i], 1 if s == 0 else -1), u.via(i, t.h))
                rs_second(u, t, i, s)

    def rs_sum(u, i):
        arrived(u.second(i, both, both), u.sem(4 + i))
        for t in tori:
            add(u.part(t, OFFS[i], 0), u.second(i, 0, t.h), u.second(i, 1, t.h))

    def rs_turn(u):
        rs_sum(u, 3)
        for t in tori:
            for s, dp in ((0, 1), (1, -1)):
                send(u.half_part(t, 2, s), u.half_via(t.h, s), rs_s.at[2], u.sem(8), t.dev(dp, 0))
        rs_sum(u, 1)
        rs_sum(u, 2)

    def rs_last(u):
        arrived(u.half_via(both, both), u.sem(8))
        for t in tori:
            for s, dp in ((0, 1), (1, -1)):
                add(u.half_part(t, dp, s), u.half_via(t.h, s))
                send(u.part(t, dp, 0), u.first_axis(t.h, s), rs_s.at[3], u.sem(9), t.dev(dp, 0))
        rs_sum(u, 0)

    mine = pltpu.make_async_copy(fin.at[0, 1, 2], ret.at[0, e], in_sem.at[10])

    def rs_finish(u):
        arrived(u.first_axis(both, both), u.sem(9))
        w, f = u.w, u.f
        for k in u.chunks:
            cols = pl.ds(k * CHUNK, CHUNK)
            for t in tori:
                total = part[w, f, t.h, t.rows(0, 0), cols].astype(jnp.float32)
                for s in range(2):
                    total = total + rv2[w, f, t.h, s, :, cols].astype(jnp.float32)
                fin[w, f, k, pl.ds(t.h * HALF, HALF)] = total.astype(jnp.bfloat16)
            if (w, f, k) == (0, 1, 2):
                mine.start()
            else:
                to = receiver(f, k)
                dev = (planes[w] * SIDE * SIDE + spot, to)
                send(fin.at[w, f, k], ret.at[w, e], back_s.at[w], back_r.at[w], dev)

    a, b, c = Unit(0, 0, 0, range(4)), Unit(1, 1, 0, range(4)), Unit(2, 1, 1, range(4))
    p, q = Unit(3, 0, 1, range(2)), Unit(4, 0, 1, range(2, 4))

    for t in tori:
        norm(0, t.h * HALF, HALF)
        gather[0].start(t)
    dispatch(1, 0, CAP)
    gather[0].near()
    gather[0].far()
    gather[0].forward(0)
    gather[0].forward(1)
    norm(1, 0, CAP)
    for t in tori:
        gather[1].start(t)
    gather[0].forward(2)
    gather[0].forward(3)
    hand_over()
    gather[1].near()
    gather[1].far()
    loads[0].wait()
    loads[1].wait()
    pltpu.make_async_copy(wd, wd, w_sem.at[2]).wait()
    gather[0].done()
    gather[1].forward(0)
    gather[1].forward(1)
    ffn(0, 0)
    gather[1].forward(2)
    gather[1].forward(3)
    ffn(0, 1)
    rs_begin(a)
    rs_begin(p)
    gather[1].done()
    gather[1].handed()
    rs_join(a)
    ffn(1, 0)
    ffn(1, 1)
    rs_begin(b)
    rs_turn(a)
    rs_join(b)
    rs_begin(c)
    rs_last(a)
    rs_turn(b)
    rs_finish(a)
    rs_join(c)
    rs_join(p)
    rs_begin(q)
    rs_last(b)
    rs_turn(c)
    rs_finish(b)
    rs_turn(p)
    rs_last(c)
    rs_join(q)
    rs_last(p)
    rs_finish(c)
    rs_turn(q)
    rs_finish(p)
    rs_last(q)
    rs_finish(q)

    all_sent(kv.at[0, 0, 0, pl.ds(0, 2)], kv_s.at[0])
    all_sent(kv.at[0, 0, pl.ds(0, SIDE - 1)], kv_s.at[1])
    all_sent(kv.at[:, :, pl.ds(0, 2)], kv_s.at[2])
    all_sent(kv.at[:, :, 0], kv_s.at[3])
    all_sent(xin.at[0, pl.ds(0, EXPERTS - 1)], a2a_s.at[0])
    all_sent(xin.at[1], a2a_s.at[1])
    all_sent(g.at[0, 0, pl.ds(0, 8 * HALF)], ag_s.at[0])
    all_sent(g.at[0, 0, pl.ds(0, 4 * HALF)], ag_s.at[1])
    all_sent(g.at[0], ag_s.at[2])
    all_sent(g.at[0, 0, pl.ds(0, (16 - 2 * len(HANDED)) * HALF)], ag_s.at[3])
    all_sent(g.at[0, 0, pl.ds(0, 2 * len(HANDED) * HALF)], ag_s.at[4])
    for i, ref in enumerate((ru1, ru2, rv1, rv2)):
        all_sent(ref, rs_s.at[i])

    routed = None
    for w in (1, 0):
        arrived(ret.at[w, pl.ds(0, EXPERTS - 1 + w)], back_r.at[w])
        if w == 0:
            mine.wait()
        rows = ret[w].reshape(EXPERTS * CAP, CHUNK)
        term = lax.dot_general(
            placing, rows, (((0,), (0,)), ((), ())), preferred_element_type=jnp.float32
        )
        routed = term if routed is None else routed + term
    out_ref[...] = routed.astype(jnp.bfloat16)
    result = pltpu.make_async_copy(out_ref, both_hbm.at[1], in_sem.at[8])
    result.start()
    attended.wait()
    result.wait()
    all_sent(ret.at[0, pl.ds(0, EXPERTS - 1)], back_s.at[0])
    all_sent(ret.at[1], back_s.at[1])


def per_device(queries, keys, values, block_order, routes, norm_gain, router, w_gate, w_up, w_down):
    anywhere = pl.BlockSpec(memory_space=pl.ANY)
    bf16, f32 = jnp.bfloat16, jnp.float32
    dma = pltpu.SemaphoreType.DMA
    here, features = queries.shape
    heads = features // HEAD_DIM
    both = pl.pallas_call(
        kernel,
        out_shape=jax.ShapeDtypeStruct((2, *queries.shape), bf16),
        in_specs=[anywhere] * 10,
        out_specs=anywhere,
        scratch_shapes=[
            pltpu.VMEM((here, features), bf16),
            pltpu.SMEM(block_order.shape, jnp.int32),
            pltpu.VMEM((1, here), jnp.int32),
            pltpu.VMEM((1, WIDTH), f32),
            pltpu.VMEM((EXPERTS, WIDTH), f32),
            pltpu.VMEM((here, features), bf16),
            pltpu.VMEM((here, features), bf16),
            pltpu.VMEM((PLANES, SIDE * SIDE, here, here), bf16),
            pltpu.VMEM((PLANES, 2, SIDE, SIDE, here, HEAD_DIM), bf16),
            pltpu.VMEM((heads, here, 1), f32),
            pltpu.VMEM((heads, here, 1), f32),
            pltpu.VMEM((heads, here, HEAD_DIM), f32),
            pltpu.VMEM((WIDTH, HID), bf16),
            pltpu.VMEM((WIDTH, HID), bf16),
            pltpu.VMEM((2, HID, UNIT_COLS), bf16),
            pltpu.VMEM((EXPERTS, CAP, CHUNK), bf16),
            pltpu.VMEM((PLANES, EXPERTS, CAP, CHUNK), bf16),
            pltpu.VMEM((PLANES, 2, GROUP, WIDTH), bf16),
            pltpu.VMEM((PLANES, 2, 2, GROUP, UNIT_COLS), bf16),
            pltpu.VMEM((PLANES, 2, 4, 2, HALF, UNIT_COLS), bf16),
            pltpu.VMEM((PLANES, 2, 4, 2, 2, HALF, UNIT_COLS), bf16),
            pltpu.VMEM((PLANES, 2, 2, 2, HALF, UNIT_COLS // 2), bf16),
            pltpu.VMEM((PLANES, 2, 2, 2, HALF, UNIT_COLS), bf16),
            pltpu.VMEM((PLANES, 2, EXPERTS // 2, CAP, CHUNK), bf16),
            pltpu.VMEM((PLANES, EXPERTS, CAP, CHUNK), bf16),
            pltpu.VMEM((2, GROUP, HID), f32),
            pltpu.VMEM((GROUP, HID), bf16),
            dma((11,)),
            dma((3,)),
            dma((4,)),
            dma((13,)),
            dma((2,)),
            dma((3,)),
            dma((5,)),
            dma((PLANES, 10)),
            dma((4,)),
            dma((5, 10)),
            dma((2,)),
            dma((2,)),
        ],
        compiler_params=pltpu.CompilerParams(
            collective_id=1, has_side_effects=True, vmem_limit_bytes=62 << 20
        ),
        name="layer",
    )(
        queries,
        keys,
        values,
        block_order,
        routes.reshape(1, -1),
        norm_gain.reshape(1, -1),
        router.T,
        w_gate[0],
        w_up[0],
        w_down[0],
    )
    return both[0], both[1]


def solution(mesh):
    in_specs = (
        P("ctx", "exp"),
        P("ctx", "exp"),
        P("ctx", "exp"),
        P(),
        P("ctx", None),
        P(),
        P(),
        P("exp", None, "ctx"),
        P("exp", None, "ctx"),
        P("exp", "ctx", None),
    )
    out_specs = (P("ctx", "exp"), P("ctx", "exp"))
    return jax.shard_map(
        per_device, mesh=mesh, in_specs=in_specs, out_specs=out_specs, check_vma=False
    )
```
